32 devices in a mesh: wide: 16 (over z, y, core), narrow: 2 (over x).
Axes of the slice: x: 2, y: 2, z: 4, core: 2. Of those that a mesh axis runs over, the one named last changes fastest.
Arguments:
- tokens: bfloat16 [16384, 768], P(('wide', 'narrow')), may hold values from -6 to 6
- memory: bfloat16 [16384, 768], P(('wide', 'narrow')), may hold values from -6 to 6
- target_segments: int32 [16384], P(('wide', 'narrow')), may hold values from 0 to 3, as said below
- memory_segments: int32 [16384], P(('wide', 'narrow')), may hold values from 0 to 3, as said below
- attention_weights: bfloat16 [8, 768, 768], P(None, ('wide', 'narrow')), may hold values from -1 to 1
- expand_weights: bfloat16 [2, 768, 2048], P(None, ('wide', 'narrow')), may hold values from -0.21875 to 0.21875
- contract_weights: bfloat16 [2048, 768], P(('wide', 'narrow')), may hold values from -0.125 to 0.125
- norm_gains: bfloat16 [3, 768], P(None, ('wide', 'narrow')), may hold values from 0.5 to 1.5
- bucket_table: bfloat16 [32, 12], replicated, may hold values from -4 to 4
- cotangent: bfloat16 [16384, 768], P(('wide', 'narrow')), may hold values from -6 to 6
Outputs:
- output: bfloat16 [16384, 768], P(('wide', 'narrow'))
- input_grad: bfloat16 [16384, 768], P(('wide', 'narrow'))
- memory_grad: bfloat16 [16384, 768], P(('wide', 'narrow'))
- attention_grad: float32 [8, 768, 768], P(None, ('wide', 'narrow'))
- expand_grad: float32 [2, 768, 2048], P(None, ('wide', 'narrow'))
- contract_grad: float32 [2048, 768], P(('wide', 'narrow'))
- gains_grad: float32 [3, 768], P(None, ('wide', 'narrow'))
- bucket_grad: float32 [32, 12], replicated
- attention_rows: float32 [6, 768], P(None, ('wide', 'narrow'))
- attention_columns: float32 [6, 768], replicated
- expand_rows: float32 [2, 768], P(None, ('wide', 'narrow'))
- expand_columns: float32 [2, 2048], replicated
- contract_rows: float32 [2048], P(('wide', 'narrow'))
- contract_columns: float32 [768], replicated
- attention_new: float32 [8, 768, 768], P(None, ('wide', 'narrow'))
- expand_new: float32 [2, 768, 2048], P(None, ('wide', 'narrow'))
- contract_new: float32 [2048, 768], P(('wide', 'narrow'))
- projection_statistics: float32 [2, 2, 768], P(None, None, ('wide', 'narrow'))
The draws below stay inside these ranges and needn't reach their ends.
Inputs may be any that keep to these rules, and one draw needn't show every extreme that they name: `target_segments`: within each packed row the ids never fall and run from 0 to 3, each on one position or more; the memory of the same row holds the same ids likewise. `memory_segments`: within each packed row the ids never fall and run from 0 to 3, each on one slot or more.
All inputs are finite; a program needn't handle non-finite values.
Results may differ from the reference program's by a relative error of at most 0.02.
The reference program's roundings to bfloat16 on the way count: a program that leaves them out, or rounds other values in their place, can miss the bound.
Values may be sent and summed in bfloat16 or wider, within the bound.
No kernel may reach another device: no remote copies, remote signals or barrier semaphores. Data moves between devices by JAX's collectives and lax.ppermute only.
A program may use at most 256 MiB of HBM per device.

```python
import math
import jax
import jax.numpy as jnp
import numpy as np
from jax import lax

D = 768
HEADS = 12
HEAD_DIM = 64
FF = 2048
BUCKETS = 32
MAX_DIST = 128
TGT_LEN = 512
MEM_LEN = 512
DOCS = 4
SEQS = 32
TOKENS = 16384
MEMS = 16384


def segment_ids(key, length, pieces, rows):
    row_keys = jax.random.split(key, rows)

    def one_row(row_key):
        shuffled = jax.random.permutation(row_key, length - 1) + 1
        cut_points = shuffled[:pieces - 1]
        positions = jnp.arange(length, dtype=jnp.int32)
        return jnp.sum((positions[:, None] >= cut_points[None, :]).astype(jnp.int32), axis=1)
    return jax.vmap(one_row)(row_keys).reshape(-1).astype(jnp.int32)


def draw_target_segments(key, part):
    key = jax.random.fold_in(key, 11)
    return segment_ids(key, TGT_LEN, DOCS, SEQS)


def draw_memory_segments(key, part):
    key = jax.random.fold_in(key, 12)
    return segment_ids(key, MEM_LEN, DOCS, SEQS)


def draw_attention_weights(key, part):
    key = jax.random.fold_in(key, 13)
    factors = jnp.array([0.45, 0.45, 1.0, 4.0, 0.45, 0.45, 1.0, 4.0], jnp.float32) * D ** (-0.5)
    base = jax.random.truncated_normal(key, -4.0, 4.0, (8, D, D), jnp.float32)
    return (base * factors[:, None, None]).astype(jnp.bfloat16)


def levels(own_key, dims, cuts, least, top_value):
    factor_of, own = 1.0, jax.random.fold_in(own_key, 6)
    for dim, parts in cuts:
        heights = jnp.exp(jax.random.uniform(jax.random.fold_in(own, dim), (parts,), jnp.float32, least / len(cuts), top_value / len(cuts)))
        factor_of = factor_of * jnp.repeat(heights, dims[dim] // parts).reshape([-1 if axis == dim else 1 for axis in range(len(dims))])
    return factor_of


def gaussian(own_key, dims, spread, limit, cuts=(), kind=jnp.bfloat16):
    entries = spread * jax.random.normal(own_key, dims, jnp.float32)
    if cuts:
        entries = entries * levels(own_key, dims, cuts, -0.22, 0.18)
    return jnp.clip(entries, -limit, limit).astype(kind)


def setup_inputs(seed: int = 0) -> dict:
    key_of = jax.random.split(jax.random.key(seed), 11)
    tokens = gaussian(key_of[0], (TOKENS, D), 1.0, 6.0, ((0, 32),))
    memory = gaussian(key_of[1], (MEMS, D), 1.0, 6.0, ((0, 32),))
    target_segments = draw_target_segments(jax.random.fold_in(key_of[10], 71), 0)
    memory_segments = draw_memory_segments(jax.random.fold_in(key_of[10], 71), 0)
    attention_weights = draw_attention_weights(jax.random.fold_in(key_of[10], 71), 0)
    expand_weights = gaussian(key_of[5], (2, D, FF), D ** -0.5, 0.21875, ((1, 32),))
    contract_weights = gaussian(key_of[6], (FF, D), FF ** -0.5, 0.125, ((0, 32),))
    norm_gains = jnp.clip(1.0 + 0.1 * jax.random.normal(key_of[7], (3, D), jnp.float32), 0.5, 1.5).astype(jnp.bfloat16)
    bucket_table = gaussian(key_of[8], (BUCKETS, HEADS), 1.0, 4.0)
    cotangent = gaussian(key_of[9], (TOKENS, D), 1.0, 6.0, ((0, 32),))
    return dict(tokens=tokens, memory=memory, target_segments=target_segments, memory_segments=memory_segments, attention_weights=attention_weights, expand_weights=expand_weights, contract_weights=contract_weights, norm_gains=norm_gains, bucket_table=bucket_table, cotangent=cotangent)


NEG_FILL = -1000000000.0
EPSILON = 1e-06
TINY = 1e-30
STEP_RATE = 0.01
top_precision = lax.Precision.HIGHEST

@jax.custom_vjp
def low(v):
    return lax.optimization_barrier(v.astype(jnp.bfloat16)).astype(jnp.float32)

@jax.custom_vjp
def low_back(v):
    return v

def low_keep(v):
    return (low(v), None)

def low_pass(kept, grad):
    return (grad,)

def back_keep(v):
    return (v, None)

def back_low(kept, grad):
    return (low(grad),)
low.defvjp(low_keep, low_pass)
low_back.defvjp(back_keep, back_low)

def bucket_onehot(length, bucket_count, far_limit):
    exact_span = bucket_count // 2
    onehot_rows = np.zeros((length, bucket_count), np.float32)
    for distance in range(length):
        if distance < exact_span:
            bucket_id = distance
        else:
            bucket_id = min(bucket_count - 1, exact_span + int(math.log(distance / exact_span) / math.log(far_limit / exact_span) * (bucket_count - exact_span)))
        onehot_rows[distance, bucket_id] = 1.0
    return onehot_rows

def distance_grid(length):
    places = np.arange(length)
    return np.maximum(places[:, None] - places[None, :], 0)

def norm_scale(values, gain_row):
    return values * lax.rsqrt(lax.optimization_barrier(jnp.mean(values * values, axis=-1, keepdims=True)) + EPSILON) * gain_row

def project(left, right):
    return jnp.dot(left, right, precision=top_precision)

def attend(query_rows, key_rows, value_rows, keep_mask, score_bias):
    scores = low_back(jnp.einsum('gqhd,gkhd->ghqk', query_rows, key_rows, precision=top_precision) + score_bias)
    scores = jnp.where(keep_mask[:, None], scores, NEG_FILL)
    probs = low(jax.nn.softmax(scores, axis=-1))
    return jnp.einsum('ghqk,gkhd->gqhd', probs, value_rows, precision=top_precision)

def grouped(operands, score_bias):

    def step(pack):
        return jax.checkpoint(attend)(pack[0], pack[1], pack[2], pack[3], score_bias)
    return lax.map(step, operands)

def factored(weight, gradient):
    squares = gradient * gradient + TINY
    row_stat = lax.optimization_barrier(jnp.mean(squares, axis=-1))
    column_stat = lax.optimization_barrier(jnp.mean(squares, axis=-2))
    scale = lax.optimization_barrier(jnp.mean(column_stat, axis=-1, keepdims=True))[..., None]
    second = row_stat[..., :, None] * column_stat[..., None, :] / scale
    return (row_stat, column_stat, weight - STEP_RATE * gradient * lax.rsqrt(second))

def without_outputs(stats):
    return jnp.concatenate([stats[0:3], stats[4:7]], axis=0)

def output_pair(stats):
    return jnp.stack([stats[3], stats[7]])

def reference(tokens, memory, target_segments, memory_segments, attention_weights, expand_weights, contract_weights, norm_gains, bucket_table, cotangent):
    count = TOKENS // TGT_LEN
    per_group = min(8, count)
    groups = count // per_group
    onehot_rows = jnp.asarray(bucket_onehot(TGT_LEN, BUCKETS, MAX_DIST))
    distance_index = distance_grid(TGT_LEN)
    causal = jnp.tril(jnp.ones((TGT_LEN, TGT_LEN), jnp.bool_))
    target_ids = target_segments.reshape(groups, per_group, TGT_LEN)
    memory_ids = memory_segments.reshape(groups, per_group, MEM_LEN)
    self_keep = (target_ids[..., :, None] == target_ids[..., None, :]) & causal
    cross_keep = target_ids[..., :, None] == memory_ids[..., None, :]

    def split_rows(rows, length):
        return rows.reshape(groups, per_group, length, HEADS, HEAD_DIM)

    def layer(token_rows, memory_rows, attention_full, expand_full, contract_full, gain_rows, table_rows):
        score_bias = jnp.transpose(project(onehot_rows, table_rows)[distance_index], (2, 0, 1))
        normed_one = low(norm_scale(token_rows, gain_rows[0]))
        query_self = low_back(low(project(normed_one, attention_full[0])))
        key_self = low_back(low(project(normed_one, attention_full[1])))
        value_self = low_back(low(project(normed_one, attention_full[2])))
        context_self = grouped((split_rows(query_self, TGT_LEN), split_rows(key_self, TGT_LEN), split_rows(value_self, TGT_LEN), self_keep), score_bias)
        context_self = low_back(low(context_self.reshape(TOKENS, D)))
        residual_one = token_rows + low_back(project(context_self, attention_full[3]))
        normed_two = low(norm_scale(residual_one, gain_rows[1]))
        query_cross = low_back(low(project(normed_two, attention_full[4])))
        key_cross = low_back(low(project(memory_rows, attention_full[5])))
        value_cross = low_back(low(project(memory_rows, attention_full[6])))
        context_cross = grouped((split_rows(query_cross, TGT_LEN), split_rows(key_cross, MEM_LEN), split_rows(value_cross, MEM_LEN), cross_keep), 0.0)
        context_cross = low_back(low(context_cross.reshape(TOKENS, D)))
        residual_two = residual_one + low_back(project(context_cross, attention_full[7]))
        normed_three = low(norm_scale(residual_two, gain_rows[2]))
        gate_input = low_back(project(normed_three, expand_full[0]))
        lift_input = low_back(project(normed_three, expand_full[1]))
        hidden = low(jax.nn.gelu(gate_input, approximate=True) * lift_input)
        return residual_two + low_back(project(hidden, contract_full))
    primals = (tokens.astype(jnp.float32), memory.astype(jnp.float32), attention_weights.astype(jnp.float32), expand_weights.astype(jnp.float32), contract_weights.astype(jnp.float32), norm_gains.astype(jnp.float32), bucket_table.astype(jnp.float32))
    output, pullback = jax.vjp(layer, *primals)
    grads = pullback(cotangent.astype(jnp.float32))
    attention_rows, attention_columns, attention_new = factored(primals[2], grads[2])
    expand_rows, expand_columns, expand_new = factored(primals[3], grads[3])
    contract_rows, contract_columns, contract_new = factored(primals[4], grads[4])
    projection_statistics = jnp.stack([output_pair(attention_rows), output_pair(attention_columns)])
    return (output.astype(jnp.bfloat16), grads[0].astype(jnp.bfloat16), grads[1].astype(jnp.bfloat16), grads[2], grads[3], grads[4], grads[5], grads[6], without_outputs(attention_rows), without_outputs(attention_columns), expand_rows, expand_columns, contract_rows, contract_columns, attention_new, expand_new, contract_new, projection_statistics)
```

```python
import functools
import math

import jax
import jax.numpy as jnp
import numpy as np
from jax import lax
from jax.experimental import pallas as pl
from jax.experimental.pallas import tpu as pltpu
from jax.sharding import PartitionSpec as P

D = 768
HEADS = 12
FF = 2048
BUCKETS = 32
MAX_DIST = 128
TGT_LEN = 512
MEM_LEN = 512
WIDE = 256
COLS = D // WIDE
BLOCKS = FF // WIDE
PAIRS = HEADS // 2
QROWS = 128

NEG_FILL = -1000000000.0
EPSILON = 1e-06
TINY = 1e-30
STEP_RATE = 0.01
AXES = ("wide", "narrow")
F32 = jnp.float32
BF16 = jnp.bfloat16
MIB = 1024 * 1024
VMEM = pltpu.VMEM


def bucket_onehot(length, bucket_count, far_limit):
    exact_span = bucket_count // 2
    onehot_rows = np.zeros((length, bucket_count), np.float32)
    for distance in range(length):
        if distance < exact_span:
            bucket_id = distance
        else:
            bucket_id = min(
                bucket_count - 1,
                exact_span
                + int(
                    math.log(distance / exact_span)
                    / math.log(far_limit / exact_span)
                    * (bucket_count - exact_span)
                ),
            )
        onehot_rows[distance, bucket_id] = 1.0
    return onehot_rows


def diagonal_onehot():
    t = np.arange(2 * QROWS)
    distance = np.where(t <= QROWS, QROWS - t, 3 * QROWS - t)
    return bucket_onehot(TGT_LEN, BUCKETS, MAX_DIST)[distance]


def mm(left, right):
    return jnp.dot(left, right, preferred_element_type=F32)


def mm_nt(left, right):
    return lax.dot_general(left, right, (((1,), (1,)), ((), ())), preferred_element_type=F32)


def mm_tn(left, right):
    return lax.dot_general(left, right, (((0,), (0,)), ((), ())), preferred_element_type=F32)


def low(values):
    return values.astype(BF16)


def cols(index):
    return slice(index * WIDE, (index + 1) * WIDE)


def inverse_rms(values):
    return lax.rsqrt(jnp.mean(values * values, axis=-1, keepdims=True) + EPSILON)


def norm_back(values, gain, grad):
    scale = inverse_rms(values)
    gain_grad = jnp.sum(values * scale * grad, axis=0, keepdims=True)
    scaled = gain * grad
    inner = jnp.mean(values * scaled, axis=-1, keepdims=True)
    return scale * scaled - values * (scale * scale * scale * inner), gain_grad


def my_index():
    return lax.axis_index("wide") * 2 + lax.axis_index("narrow")


def call(body, outs, in_specs, args, flops, moved, grid=None, scratch=(), limit=48, out_specs=None):
    kwargs = {} if grid is None else {"grid": grid}
    whole = pl.BlockSpec(memory_space=VMEM)
    return pl.pallas_call(
        body,
        out_shape=[jax.ShapeDtypeStruct(*o) for o in outs],
        in_specs=[whole if s is None else s for s in in_specs],
        out_specs=[whole] * len(outs) if out_specs is None else [whole if s is None else s for s in out_specs],
        scratch_shapes=list(scratch),
        compiler_params=pltpu.CompilerParams(vmem_limit_bytes=limit * MIB),
        cost_estimate=pl.CostEstimate(flops=int(flops), bytes_accessed=int(moved), transcendentals=0),
        **kwargs,
    )(*args)


def slot_mask(first, slot):
    high, mid, z = slot >> 3, (slot >> 2) & 1, slot & 3
    dy, dx = (high, mid) if first == 0 else (mid, high)
    return z * 8 + dy * 4 + dx


def put_matrix(ring, acc, own, sib, first, piece, value):
    if not ring:
        own[piece] = value
        return
    acc[...] = value
    me = my_index()
    for out, core in ((own, 0), (sib, 2)):
        for slot in range(16):
            owner = lax.bitwise_xor(me, slot_mask(first, slot) + core)
            rows = acc[pl.ds(pl.multiple_of(owner * 24, 8), 24), :]
            out[slot, piece] = low(rows.reshape(3, 8, WIDE))


def grad_shapes(ring, pieces):
    if ring:
        return [((16, pieces, 3, 8, WIDE), BF16)] * 2
    return [((pieces, D, WIDE), F32)]


def pre_kernel(tok, mem, gains, w, n1, q, k, v, kc, vc):
    x = tok[...].astype(F32)
    normed = low(x * inverse_rms(x) * gains[0:1, :])
    n1[...] = normed
    memory = mem[...]
    for c in range(COLS):
        q[:, cols(c)] = low(mm(normed, w[0, c]))
        k[:, cols(c)] = low(mm(normed, w[1, c]))
        v[:, cols(c)] = low(mm(normed, w[2, c]))
        kc[:, cols(c)] = low(mm(memory, w[5, c]))
        vc[:, cols(c)] = low(mm(memory, w[6, c]))


def halves(block):
    lane = lax.broadcasted_iota(jnp.int32, block.shape, 1)
    zero = jnp.zeros_like(block)
    return jnp.concatenate([jnp.where(lane < 64, block, zero), jnp.where(lane < 64, zero, block)], axis=0)


def side(pair):
    rows = pair.shape[0] // 2
    return jnp.concatenate([pair[:rows], pair[rows:]], axis=1)


def twice(block):
    return jnp.concatenate([block, block], axis=0)


def split_rows(pair, count):
    rows = pair.shape[0] // 2
    return jnp.concatenate([pair[:count], pair[rows : rows + count]], axis=0)


def softmax(scores):
    top = jnp.max(scores, axis=-1, keepdims=True)
    raised = jnp.exp(scores - top)
    return raised * (1.0 / jnp.sum(raised, axis=-1, keepdims=True))


def pair_bias(line):
    rows = [
        pltpu.roll(jnp.broadcast_to(line[h : h + 1, :], (QROWS, 2 * QROWS)), 0, 1, stride=1, stride_axis=0)
        for h in range(2)
    ]
    far = jnp.concatenate([jnp.broadcast_to(line[h : h + 1, 0:1], (QROWS, 1)) for h in range(2)], axis=0)
    return jnp.concatenate(rows, axis=0), far


def self_probs(block, q2, k, bias, far, seg_col, seg_row):
    end = (block + 1) * QROWS
    scores = mm_nt(q2, k[:end])
    if block == 0:
        scores = scores + bias[:, QROWS:]
    elif block == 1:
        scores = scores + bias
    else:
        scores = jnp.concatenate([scores[:, : end - 2 * QROWS] + far, scores[:, end - 2 * QROWS :] + bias], axis=1)
    keep = seg_col == seg_row[:, :end]
    row = lax.broadcasted_iota(jnp.int32, (QROWS, end), 0) + block * QROWS
    keep = keep & (lax.broadcasted_iota(jnp.int32, (QROWS, end), 1) <= row)
    return softmax(jnp.where(twice(keep), scores, NEG_FILL))


def cross_probs(q2, k, seg_col, seg_row):
    keep = seg_col == seg_row
    return softmax(jnp.where(twice(keep), mm_nt(q2, k), NEG_FILL))


def self_forward_kernel(q, k, v, line, seg_col, seg_row, out):
    bias, far = pair_bias(line[0])
    keys, values = k[...], halves(v[...])
    for block in range(TGT_LEN // QROWS):
        rows = slice(block * QROWS, (block + 1) * QROWS)
        probs = self_probs(block, halves(q[rows, :]), keys, bias, far, seg_col[rows, :], seg_row[...])
        out[rows, :] = low(mm(side(low(probs)), split_rows(values, (block + 1) * QROWS)))


def cross_forward_kernel(q, k, v, seg_col, seg_row, out):
    keys, values = k[...], halves(v[...])
    for block in range(TGT_LEN // QROWS):
        rows = slice(block * QROWS, (block + 1) * QROWS)
        probs = cross_probs(halves(q[rows, :]), keys, seg_col[rows, :], seg_row[...])
        out[rows, :] = low(mm(side(low(probs)), values))


def pair_spec(length):
    return pl.BlockSpec((length, 128), lambda p: (0, p))


LINE_SPEC = pl.BlockSpec((1, 2, 2 * QROWS), lambda p: (p, 0, 0))


def mid_kernel(ctx, tok, gains, w, res, n2, qc):
    context = ctx[...]
    for c in range(COLS):
        res[:, cols(c)] = tok[:, cols(c)].astype(F32) + mm(context, w[3, c])
    x = res[...]
    normed = low(x * inverse_rms(x) * gains[1:2, :])
    n2[...] = normed
    for c in range(COLS):
        qc[:, cols(c)] = low(mm(normed, w[4, c]))


def late_kernel(ctx, res1, gains, w, res2, n3):
    context = ctx[...]
    for c in range(COLS):
        res2[:, cols(c)] = res1[:, cols(c)] + mm(context, w[7, c])
    x = res2[...]
    n3[...] = low(x * inverse_rms(x) * gains[2:3, :])


def gelu_pair(gate):
    rate = math.sqrt(2.0 / math.pi)
    square = gate * gate
    bend = jnp.tanh(rate * gate * (1.0 + 0.044715 * square))
    half = 0.5 * (1.0 + bend)
    slope = half + 0.5 * gate * (1.0 - bend * bend) * rate * (1.0 + 3.0 * 0.044715 * square)
    return gate * half, slope


def ffn_kernel(ring, n3, res2, cot, gate_w, lift_w, con_w, out, dn3, *rest):
    grads, (n3t, total, acc, con_acc) = rest[:-4], rest[-4:]
    block = pl.program_id(0)

    @pl.when(block == 0)
    def _():
        n3t[...] = n3[...].T
        total[...] = res2[...]
        dn3[...] = jnp.zeros_like(dn3)

    normed = n3[...]
    gate_rows, lift_rows = gate_w[0, 0], lift_w[0, 0]
    lift = mm(normed, lift_rows)
    active, slope = gelu_pair(mm(normed, gate_rows))
    hidden = low(active * lift)
    back = jnp.zeros(lift.shape, F32)
    for c in range(COLS):
        total[:, cols(c)] += mm(hidden, con_w[c])
        back = back + mm_nt(cot[:, cols(c)], con_w[c])
    gate_grad = low(back * lift * slope)
    lift_grad = low(back * active)
    dn3[...] += mm_nt(gate_grad, gate_rows) + mm_nt(lift_grad, lift_rows)
    turned = hidden.T
    if ring:
        own_a, own_b, sib_a, sib_b = grads
        put_matrix(ring, acc, own_a, sib_a, 0, block, mm(n3t[...], gate_grad))
        put_matrix(ring, acc, own_b, sib_b, 1, block, mm(n3t[...], lift_grad))
        me = my_index()
        near = lax.bitwise_xor(block, lax.shift_right_logical(me, 2))
        dz, dy = lax.shift_right_logical(near, 1), lax.bitwise_and(near, 1)
        inner = lax.bitwise_and(me, 3)
        for c in range(COLS):
            con_acc[...] = mm(turned, cot[:, cols(c)])
            for core in range(2):
                for dx in range(2):
                    place = lax.bitwise_xor(inner, core * 2 + dx)
                    rows = low(con_acc[pl.ds(pl.multiple_of(place * 64, 8), 64), :].reshape(8, 8, WIDE))
                    (own_a, sib_a)[core][dy * 8 + dx * 4 + dz, 8:12, c] = rows[:4]
                    (own_b, sib_b)[core][dx * 8 + dy * 4 + dz, 8:12, c] = rows[4:]
    else:
        gate_out, lift_out, con_out = grads
        gate_out[block] = mm(n3t[...], gate_grad)
        lift_out[block] = mm(n3t[...], lift_grad)
        for c in range(COLS):
            con_out[c, pl.ds(pl.multiple_of(block * WIDE, 8), WIDE), :] = mm(turned, cot[:, cols(c)])

    @pl.when(block == BLOCKS - 1)
    def _():
        out[...] = low(total[...])


def third_back_kernel(dn3, res2, cot, gains, w, r2g, ccg, gg):
    back, gain_grad = norm_back(res2[...], gains[2:3, :], dn3[...])
    gg[...] = gain_grad
    grad = cot[...].astype(F32) + back
    r2g[...] = grad
    cross_low = low(grad)
    total = mm_nt(cross_low[:, cols(0)], w[7, 0])
    for c in range(1, COLS):
        total = total + mm_nt(cross_low[:, cols(c)], w[7, c])
    ccg[...] = low(total)


def backward_block(probs, q2, dc2, keys2, values, dq, dk, dv, rows, end):
    prob_grad = mm_nt(dc2, values[:end])
    moved = probs * prob_grad
    score_grad = low(moved - probs * jnp.sum(moved, axis=-1, keepdims=True))
    dq[rows, :] = low(mm(side(score_grad), split_rows(keys2, end)))
    dk[:end, :] += mm_tn(score_grad, q2)
    dv[:end, :] += mm_tn(low(probs), dc2)
    return score_grad


def cross_back_kernel(q, k, v, dc, seg_col, seg_row, dq, dk, dv, dk_acc, dv_acc):
    dk_acc[...] = jnp.zeros_like(dk_acc)
    dv_acc[...] = jnp.zeros_like(dv_acc)
    keys, values = k[...], v[...]
    keys2 = halves(keys)
    for block in range(TGT_LEN // QROWS):
        rows = slice(block * QROWS, (block + 1) * QROWS)
        q2 = halves(q[rows, :])
        probs = cross_probs(q2, keys, seg_col[rows, :], seg_row[...])
        backward_block(probs, q2, halves(dc[rows, :]), keys2, values, dq, dk_acc, dv_acc, rows, MEM_LEN)
    dk[...] = low(dk_acc[...])
    dv[...] = low(dv_acc[...])


def diagonal_sums(grid, start):
    width = 2 * QROWS
    group = grid[start : start + 8, :]
    for shift in range(8, QROWS, 8):
        group = group + pltpu.roll(grid[start + shift : start + shift + 8, :], width - shift, 1)
    row = lax.broadcasted_iota(jnp.int32, group.shape, 0)
    for bit in (1, 2, 4):
        group = jnp.where((row & bit) != 0, pltpu.roll(group, width - bit, 1), group)
    return jnp.sum(group, axis=0, keepdims=True)


def self_back_kernel(q, k, v, dc, line, seg_col, seg_row, dq, dk, dv, diag, dk_acc, dv_acc, near):
    dk_acc[...] = jnp.zeros_like(dk_acc)
    dv_acc[...] = jnp.zeros_like(dv_acc)
    bias, far = pair_bias(line[0])
    keys, values = k[...], v[...]
    keys2 = halves(keys)
    far_sum = jnp.zeros((2 * QROWS, QROWS), F32)
    for block in range(TGT_LEN // QROWS):
        rows = slice(block * QROWS, (block + 1) * QROWS)
        end = (block + 1) * QROWS
        q2 = halves(q[rows, :])
        probs = self_probs(block, q2, keys, bias, far, seg_col[rows, :], seg_row[...])
        score_grad = backward_block(
            probs, q2, halves(dc[rows, :]), keys2, values, dq, dk_acc, dv_acc, rows, end
        ).astype(F32)
        if block == 0:
            near[:, :QROWS] = jnp.zeros((2 * QROWS, QROWS), F32)
            near[:, QROWS:] = score_grad
        else:
            near[...] += score_grad[:, end - 2 * QROWS :]
        for other in range(block - 1):
            far_sum = far_sum + score_grad[:, other * QROWS : (other + 1) * QROWS]
    dk[...] = low(dk_acc[...])
    dv[...] = low(dv_acc[...])
    lane = lax.broadcasted_iota(jnp.int32, (1, 2 * QROWS), 1)
    for h in range(2):
        beyond = jnp.sum(far_sum[h * QROWS : (h + 1) * QROWS, :], keepdims=True)
        diag[0, h : h + 1, :] = diagonal_sums(near, h * QROWS) + jnp.where(lane == 0, beyond, 0.0)


def second_back_kernel(ring, dq, dk, dv, mem, res1, r2g, gains, w, ctxs, ctxc, n2, mg, r1g, csg, gg, *rest):
    grads, acc = rest[:-1], rest[-1]
    query_grad, key_grad, value_grad = dq[...], dk[...], dv[...]
    back = mm_nt(query_grad[:, cols(0)], w[4, 0])
    for c in range(1, COLS):
        back = back + mm_nt(query_grad[:, cols(c)], w[4, c])
    moved, gain_grad = norm_back(res1[...], gains[1:2, :], back)
    gg[...] = gain_grad
    grad = r2g[...] + moved
    r1g[...] = grad
    self_low, cross_low = low(grad), low(r2g[...])
    total = mm_nt(self_low[:, cols(0)], w[3, 0])
    for c in range(1, COLS):
        total = total + mm_nt(self_low[:, cols(c)], w[3, c])
    csg[...] = low(total)
    total = mm_nt(key_grad[:, cols(0)], w[5, 0]) + mm_nt(value_grad[:, cols(0)], w[6, 0])
    for c in range(1, COLS):
        total = total + mm_nt(key_grad[:, cols(c)], w[5, c]) + mm_nt(value_grad[:, cols(c)], w[6, c])
    mg[...] = low(total)
    memory_t = mem[...].T
    for matrix, left, right in (
        (3, ctxs[...].T, self_low),
        (4, n2[...].T, query_grad),
        (5, memory_t, key_grad),
        (6, memory_t, value_grad),
        (7, ctxc[...].T, cross_low),
    ):
        for c in range(COLS):
            put_piece(ring, grads, acc, (matrix - 3) * COLS + c, 8, mm(left, right[:, cols(c)]))


def put_piece(ring, grads, acc, index, split, value):
    if not ring:
        grads[0][index] = value
        return
    own_a, own_b, sib_a, sib_b = grads
    if index < split:
        put_matrix(ring, acc, own_a, sib_a, 0, index, value)
    else:
        put_matrix(ring, acc, own_b, sib_b, 1, index - split, value)


def first_grads_kernel(ring, dq, dk, dv, n1, *rest):
    grads, acc = rest[:-1], rest[-1]
    left = n1[...].T
    for matrix, right in enumerate((dq, dk, dv)):
        for c in range(COLS):
            put_piece(ring, grads, acc, matrix * COLS + c, 5, mm(left, right[:, cols(c)]))


def first_back_kernel(dq, dk, dv, tok, r1g, gains, w, ig, gg):
    back = None
    for matrix, right in enumerate((dq, dk, dv)):
        for c in range(COLS):
            term = mm_nt(right[:, cols(c)], w[matrix, c])
            back = term if back is None else back + term
    moved, gain_grad = norm_back(tok[...].astype(F32), gains[0:1, :], back)
    gg[...] = gain_grad
    ig[...] = low(r1g[...] + moved)


def hop(values, mask):
    return lax.ppermute(values, AXES, [(k, k ^ mask) for k in range(32)])


def after(values, *earlier):
    return lax.optimization_barrier((values,) + earlier)[0]


def place_kernel(plan, targets, count, *refs):
    ins, outs, sem = refs[:count], refs[count:-1], refs[-1]
    me = my_index()
    copies = []
    for ref, (masks, low_piece, high_piece) in zip(ins, plan):
        for index, mask in enumerate(masks):
            owner = lax.bitwise_xor(me, mask)
            for out, first, last, start, column in targets:
                begin, end = max(low_piece, first), min(high_piece, last)
                if begin >= end:
                    continue
                pieces = pl.ds(begin - low_piece, end - begin)
                into = pl.ds(start + begin - first, end - begin)
                if column is None:
                    pair = (ref.at[index, pieces], outs[out].at[into, owner])
                else:
                    pair = (ref.at[index, pieces, column], outs[out].at[column, owner, into])
                copies.append(pltpu.make_async_copy(*pair, sem.at[len(copies)]))
                copies[-1].start()
    for copy in copies:
        copy.wait()


def place(arrays, outs, targets):
    plan = [a[1:] for a in arrays]
    return call(
        functools.partial(place_kernel, plan, targets, len(arrays)),
        [(o, BF16) for o in outs],
        [pl.BlockSpec(memory_space=pl.ANY)] * len(arrays),
        [a[0] for a in arrays],
        0,
        2 * 2 * math.prod(outs[0]),
        scratch=[pltpu.SemaphoreType.DMA((320,))],
        limit=32,
    )


def spread_start(chunks, *earlier):
    own = jnp.stack(chunks) if len(chunks) > 1 else chunks[0][None]
    if earlier:
        own = after(own, *earlier)
    return own, hop(own, 1), hop(own, 4)


def spread_end(started, masks, half):
    own, by_x, by_y = started
    pieces = own.shape[1]
    first = hop(by_x[:, :half], 4)
    second = hop(by_y[:, half:], 1)
    shift = lambda d: [m + d for m in masks]
    return [
        (own, shift(0), 0, pieces),
        (by_x, shift(1), 0, pieces),
        (by_y, shift(4), 0, pieces),
        (first, shift(5), 0, half),
        (second, shift(5), half, pieces),
    ]


def with_core(arrays):
    return arrays + [(hop(a, 2), [m + 2 for m in masks], lo, hi) for a, masks, lo, hi in arrays]


def gather_ring(attention, expand, contract, gains):
    attention_pieces = attention.reshape(8, 24, COLS, WIDE).transpose(0, 2, 1, 3).reshape(24, 3, 8, WIDE)
    gain_piece = jnp.pad(gains.reshape(1, 3, 1, 24), ((0, 0), (0, 0), (0, 7), (0, WIDE - 24)))
    first = jnp.concatenate([attention_pieces, gain_piece])
    expand_pieces = expand.reshape(2, 24, BLOCKS, WIDE).transpose(0, 2, 1, 3).reshape(2, BLOCKS, 3, 8, WIDE)
    contract_pieces = contract.reshape(8, 8, COLS, WIDE).transpose(0, 2, 1, 3)
    second = jnp.concatenate([expand_pieces[0], contract_pieces[:4], expand_pieces[1], contract_pieces[4:]])
    half_first, half_second = 13, 12

    z1 = hop(first, 8)
    z3 = hop(after(first, z1), 24)
    s0 = spread_start([first, z1])
    z2 = hop(after(z3, s0[1], s0[2]), 8)
    a0 = spread_end(s0, [0, 8], half_first)
    s1 = spread_start([z2, z3], s0[1], s0[2])
    v1 = hop(after(second, z2), 8)
    v3 = hop(after(second, v1), 24)
    v2 = hop(v3, 8)
    a1 = spread_end(s1, [16, 24], half_first)
    t0 = spread_start([second, v1], s1[1], s1[2], a0[3][0], a0[4][0])
    b0 = spread_end(t0, [0, 8], half_second)
    t1 = spread_start([v2, v3], t0[1], t0[2], a1[3][0], a1[4][0])
    b1 = spread_end(t1, [16, 24], half_second)
    square, gains_out = place(
        with_core(a0) + with_core(a1),
        [(24, 32, 3, 8, WIDE), (1, 32, 3, 8, WIDE)],
        [(0, 0, 24, 0, None), (1, 24, 25, 0, None)],
    )
    wide, narrow = place(
        with_core(b0) + with_core(b1),
        [(16, 32, 3, 8, WIDE), (COLS, 32, 8, 8, WIDE)],
        [(0, 0, 8, 0, None), (0, 12, 20, 8, None)]
        + [(1, 8, 12, 0, c) for c in range(COLS)]
        + [(1, 20, 24, 4, c) for c in range(COLS)],
    )
    gain_rows = gains_out[0, :, :, 0, :24].transpose(1, 0, 2).reshape(3, D)
    return (
        square.reshape(8, COLS, D, WIDE),
        wide.reshape(2, BLOCKS, D, WIDE),
        narrow.reshape(COLS, FF, WIDE),
        gain_rows,
    )


def gather_plain(attention, expand, contract, gains):
    attention, expand, contract, gains = (
        lax.all_gather(attention, AXES, axis=1, tiled=True),
        lax.all_gather(expand, AXES, axis=1, tiled=True),
        lax.all_gather(contract, AXES, axis=0, tiled=True),
        lax.all_gather(gains, AXES, axis=1, tiled=True),
    )
    return (
        attention.reshape(8, D, COLS, WIDE).transpose(0, 2, 1, 3),
        expand.reshape(2, D, BLOCKS, WIDE).transpose(0, 2, 1, 3),
        contract.reshape(FF, COLS, WIDE).transpose(1, 0, 2),
        gains,
    )


def total(*terms):
    result = terms[0].astype(F32)
    for term in terms[1:]:
        result = result + term.astype(F32)
    return result


def scatter_ring(grads, *earlier):
    own_a, own_b, sib_a, sib_b = grads
    from_a, from_b = hop(sib_a, 2), hop(sib_b, 2)
    send_a = low(total(own_a[8:], from_a[8:]))
    send_b = low(total(own_b[8:], from_b[8:]))
    a1, b1 = hop(send_a, 4), hop(send_b, 1)
    next_a = low(total(own_a[4:8], from_a[4:8], a1[4:]))
    next_b = low(total(own_b[4:8], from_b[4:8], b1[4:]))
    a2, b2 = hop(next_a, 1), hop(next_b, 4)
    mine_a = total(own_a[:4], from_a[:4], a1[:4], a2)
    mine_b = total(own_b[:4], from_b[:4], b1[:4], b2)
    mine = jnp.concatenate([mine_a, mine_b], axis=1)
    near = hop(low(mine[1:3]), 8)
    far = hop(low(mine[3] + near[1].astype(F32)), 24)
    return total(mine[0], near[0], far)


def scatter_plain(pieces, shape, axis):
    count = pieces.shape[0]
    if axis == 0:
        whole = pieces.transpose(1, 0, 2).reshape(shape)
    else:
        per = shape[2] // WIDE
        whole = pieces.reshape(shape[0], per, shape[1], WIDE).transpose(0, 2, 1, 3).reshape(shape)
    return lax.psum_scatter(whole, AXES, scatter_dimension=axis, tiled=True)


def sum_ring(values):
    values = values + hop(values, 2)
    values = (values + hop(values, 1)) + (hop(values, 4) + hop(values, 5))
    return (values + hop(values, 8)) + (hop(values, 16) + hop(values, 24))


def factored_stats(grad_shard, total_rows):
    squares = grad_shard * grad_shard + TINY
    return (jnp.mean(squares, axis=-1), jnp.sum(squares, axis=-2) / total_rows)


def factored_update(weight_shard, grad_shard, row_stat, column_stat):
    scale = jnp.mean(column_stat, axis=-1, keepdims=True)[..., None]
    second = row_stat[..., :, None] * column_stat[..., None, :] / scale
    return weight_shard.astype(F32) - STEP_RATE * grad_shard * lax.rsqrt(second)


def without_outputs(stats):
    return jnp.concatenate([stats[0:3], stats[4:7]], axis=0)


def output_pair(stats):
    return jnp.stack([stats[3], stats[7]])


def on_device(
    ring,
    tokens,
    memory,
    target_segments,
    memory_segments,
    attention_weights,
    expand_weights,
    contract_weights,
    norm_gains,
    bucket_table,
    cotangent,
):
    rows = tokens.shape[0]
    gather = gather_ring if ring else gather_plain
    square, wide, narrow, gains = gather(attention_weights, expand_weights, contract_weights, norm_gains)
    gains = gains.astype(F32)
    spread_buckets = jnp.asarray(diagonal_onehot())
    lines = jnp.dot(
        bucket_table.T.astype(F32), spread_buckets.T, precision=lax.Precision.HIGHEST, preferred_element_type=F32
    ).reshape(PAIRS, 2, 2 * QROWS)
    target_col, target_row = target_segments.reshape(rows, 1), target_segments.reshape(1, rows)
    memory_row = memory_segments.reshape(1, rows)
    act, act32 = ((rows, D), BF16), ((rows, D), F32)
    size = rows * D
    product = 2 * size * D
    none = [None]

    n1, q, k, v, kc, vc = call(
        pre_kernel, [act] * 6, none * 4, (tokens, memory, gains, square), 5 * product, 2 * (8 * size + 5 * D * D)
    )
    pair = pair_spec(rows)
    heads_work = 2 * HEADS * rows * rows * 256
    ctxs = call(
        self_forward_kernel,
        [act],
        [pair] * 3 + [LINE_SPEC, None, None],
        (q, k, v, lines, target_col, target_row),
        2 * heads_work,
        8 * size,
        grid=(PAIRS,),
        out_specs=[pair],
    )[0]
    res1, n2, qc = call(
        mid_kernel, [act32, act, act], none * 4, (ctxs, tokens, gains, square), 2 * product, 14 * size + 4 * D * D
    )
    ctxc = call(
        cross_forward_kernel,
        [act],
        [pair] * 3 + [None, None],
        (qc, kc, vc, target_col, memory_row),
        2 * heads_work,
        8 * size,
        grid=(PAIRS,),
        out_specs=[pair],
    )[0]
    res2, n3 = call(late_kernel, [act32, act], none * 4, (ctxc, res1, gains, square), product, 14 * size)

    expand_block = lambda m: pl.BlockSpec((1, 1, D, WIDE), lambda b: (m, b, 0, 0))
    if ring:
        grad_outs = [((16, 12, 3, 8, WIDE), BF16)] * 4
    else:
        grad_outs = [((BLOCKS, D, WIDE), F32)] * 2 + [((COLS, FF, WIDE), F32)]
    output, dn3, *ffn_grads = call(
        functools.partial(ffn_kernel, ring),
        [act, act32] + grad_outs,
        none * 3 + [expand_block(0), expand_block(1), pl.BlockSpec((COLS, WIDE, WIDE), lambda b: (0, b, 0))],
        (n3, res2, cotangent, wide, wide, narrow),
        9 * 2 * rows * D * FF,
        4 * 3 * D * FF,
        grid=(BLOCKS,),
        scratch=[
            VMEM((D, rows), BF16),
            VMEM((rows, D), F32),
            VMEM((D, WIDE), F32),
            VMEM((WIDE, WIDE), F32),
        ],
    )

    r2g, ccg, gain_three = call(
        third_back_kernel,
        [act32, act, ((1, D), F32)],
        none * 5,
        (dn3, res2, cotangent, gains, square),
        product,
        16 * size,
    )
    acc = VMEM((D, WIDE), F32)
    head_acc = VMEM((rows, 128), F32)
    dqc, dkc, dvc = call(
        cross_back_kernel,
        [act] * 3,
        [pair] * 4 + [None, None],
        (qc, kc, vc, ccg, target_col, memory_row),
        5 * heads_work,
        14 * size,
        grid=(PAIRS,),
        scratch=[head_acc, head_acc],
        out_specs=[pair] * 3,
    )
    second_grads = grad_shapes(ring, 8) + grad_shapes(ring, 7) if ring else grad_shapes(ring, 15)
    if ring:
        second_grads = [second_grads[0], second_grads[2], second_grads[1], second_grads[3]]
    memory_grad, r1g, csg, gain_two, *cross_grads = call(
        functools.partial(second_back_kernel, ring),
        [act, act32, act, ((1, D), F32)] + second_grads,
        none * 11,
        (dqc, dkc, dvc, memory, res1, r2g, gains, square, ctxs, ctxc, n2),
        9 * product,
        24 * size + 20 * D * D,
        scratch=[acc],
    )
    dqs, dks, dvs, diag = call(
        self_back_kernel,
        [act] * 3 + [((PAIRS, 2, 2 * QROWS), F32)],
        [pair] * 4 + [LINE_SPEC, None, None],
        (q, k, v, csg, lines, target_col, target_row),
        5 * heads_work,
        14 * size,
        grid=(PAIRS,),
        scratch=[head_acc, head_acc, VMEM((2 * QROWS, 2 * QROWS), F32)],
        out_specs=[pair] * 3 + [LINE_SPEC],
    )
    first_grads = grad_shapes(ring, 5) + grad_shapes(ring, 4) if ring else grad_shapes(ring, 9)
    if ring:
        first_grads = [first_grads[0], first_grads[2], first_grads[1], first_grads[3]]
    self_grads = call(
        functools.partial(first_grads_kernel, ring),
        first_grads,
        none * 4,
        (dqs, dks, dvs, n1),
        3 * product,
        8 * size + 6 * D * D,
        scratch=[acc],
    )
    input_grad, gain_one = call(
        first_back_kernel,
        [act, ((1, D), F32)],
        none * 7,
        (dqs, dks, dvs, tokens, r1g, gains, square),
        3 * product,
        16 * size + 6 * D * D,
    )
    bucket_part = jnp.dot(
        spread_buckets.T, diag.reshape(HEADS, 2 * QROWS).T, precision=lax.Precision.HIGHEST, preferred_element_type=F32
    )
    gains_part = jnp.concatenate([gain_one, gain_two, gain_three])

    if ring:
        ffn_share = scatter_ring(ffn_grads)
        cross_share = scatter_ring(cross_grads)
        self_share = scatter_ring(self_grads)
        squares = jnp.concatenate([self_share, cross_share]).reshape(8, COLS, 24, WIDE)
        attention_grad = squares.transpose(0, 2, 1, 3).reshape(8, 24, D)
        expand_grad = jnp.stack([ffn_share[0:8], ffn_share[12:20]])
        expand_grad = expand_grad.reshape(2, BLOCKS, 24, WIDE).transpose(0, 2, 1, 3).reshape(2, 24, FF)
        contract_grad = jnp.concatenate([ffn_share[8:12], ffn_share[20:24]])
        contract_grad = contract_grad.transpose(0, 2, 1, 3).reshape(64, D)
    else:
        pieces = jnp.concatenate([self_grads[0], cross_grads[0]])
        attention_grad = scatter_plain(pieces, (8, D, D), 1)
        expand_grad = scatter_plain(jnp.stack(ffn_grads[:2]), (2, D, FF), 1)
        contract_grad = scatter_plain(ffn_grads[2], (FF, D), 0)

    attention_rows, attention_part = factored_stats(attention_grad, D)
    expand_rows, expand_part = factored_stats(expand_grad, D)
    contract_rows, contract_part = factored_stats(contract_grad, FF)
    parts = (attention_part, expand_part, contract_part, bucket_part, gains_part)
    if ring:
        flat = jnp.concatenate([p.reshape(-1) for p in parts]).reshape(-1, 128)
        flat = sum_ring(flat).reshape(-1)
        sums, start = [], 0
        for p in parts:
            sums.append(flat[start : start + p.size].reshape(p.shape))
            start += p.size
    else:
        sums = lax.psum(parts, AXES)
    attention_columns, expand_columns, contract_columns, bucket_grad, gains_sum = sums
    attention_new = factored_update(attention_weights, attention_grad, attention_rows, attention_columns)
    expand_new = factored_update(expand_weights, expand_grad, expand_rows, expand_columns)
    contract_new = factored_update(contract_weights, contract_grad, contract_rows, contract_columns)
    share_width = attention_rows.shape[1]
    share_start = lax.axis_index(AXES) * share_width
    column_share = lax.dynamic_slice_in_dim(attention_columns, share_start, share_width, 1)
    gains_grad = lax.dynamic_slice_in_dim(gains_sum, share_start, share_width, 1)
    projection_statistics = jnp.stack([output_pair(attention_rows), output_pair(column_share)])
    return (
        output,
        input_grad,
        memory_grad,
        attention_grad,
        expand_grad,
        contract_grad,
        gains_grad,
        bucket_grad,
        without_outputs(attention_rows),
        without_outputs(attention_columns),
        expand_rows,
        expand_columns,
        contract_rows,
        contract_columns,
        attention_new,
        expand_new,
        contract_new,
        projection_statistics,
    )


def solution(mesh):
    ring = dict(mesh.shape) == {"wide": 16, "narrow": 2}
    rows, both = P(AXES, None), P(None, AXES, None)
    placed = (rows, rows, P(AXES), P(AXES), both, both, rows, P(None, AXES), P(), rows)
    return jax.shard_map(
        functools.partial(on_device, ring),
        mesh=mesh,
        in_specs=placed,
        out_specs=(
            rows,
            rows,
            rows,
            both,
            both,
            rows,
            P(None, AXES),
            P(),
            P(None, AXES),
            P(),
            P(None, AXES),
            P(),
            P(AXES),
            P(),
            both,
            both,
            rows,
            P(None, None, AXES),
        ),
        check_vma=False,
    )
```

```python
import functools
import math

import jax
import jax.numpy as jnp
import numpy as np
from jax import lax
from jax.experimental import pallas as pl
from jax.experimental.pallas import tpu as pltpu
from jax.sharding import PartitionSpec as P

D = 768
HEADS = 12
FF = 2048
BUCKETS = 32
MAX_DIST = 128
TGT_LEN = 512
MEM_LEN = 512
WIDE = 256
COLS = D // WIDE
BLOCKS = FF // WIDE
PAIRS = HEADS // 2
QROWS = 128

NEG_FILL = -1000000000.0
EPSILON = 1e-06
TINY = 1e-30
STEP_RATE = 0.01
AXES = ("wide", "narrow")
F32 = jnp.float32
BF16 = jnp.bfloat16
MIB = 1024 * 1024
VMEM = pltpu.VMEM


def bucket_onehot(length, bucket_count, far_limit):
    exact_span = bucket_count // 2
    onehot_rows = np.zeros((length, bucket_count), np.float32)
    for distance in range(length):
        if distance < exact_span:
            bucket_id = distance
        else:
            bucket_id = min(
                bucket_count - 1,
                exact_span
                + int(
                    math.log(distance / exact_span)
                    / math.log(far_limit / exact_span)
                    * (bucket_count - exact_span)
                ),
            )
        onehot_rows[distance, bucket_id] = 1.0
    return onehot_rows


def diagonal_onehot():
    t = np.arange(2 * QROWS)
    distance = np.where(t <= QROWS, QROWS - t, 3 * QROWS - t)
    return bucket_onehot(TGT_LEN, BUCKETS, MAX_DIST)[distance]


def mm(left, right):
    return jnp.dot(left, right, preferred_element_type=F32)


def mm_nt(left, right):
    return lax.dot_general(left, right, (((1,), (1,)), ((), ())), preferred_element_type=F32)


def mm_tn(left, right):
    return lax.dot_general(left, right, (((0,), (0,)), ((), ())), preferred_element_type=F32)


def low(values):
    return values.astype(BF16)


def cols(index):
    return slice(index * WIDE, (index + 1) * WIDE)


def inverse_rms(values):
    return lax.rsqrt(jnp.mean(values * values, axis=-1, keepdims=True) + EPSILON)


def norm_back(values, gain, grad):
    scale = inverse_rms(values)
    gain_grad = jnp.sum(values * scale * grad, axis=0, keepdims=True)
    scaled = gain * grad
    inner = jnp.mean(values * scaled, axis=-1, keepdims=True)
    return scale * scaled - values * (scale * scale * scale * inner), gain_grad


def my_index():
    return lax.axis_index("wide") * 2 + lax.axis_index("narrow")


def in_vmem(values):
    return pltpu.with_memory_space_constraint(values, pltpu.VMEM)


def call(
    body, outs, in_specs, args, flops, moved, grid=None, scratch=(), limit=20, out_specs=None, out_space=None
):
    kwargs = {} if grid is None else {"grid": grid}
    whole = pl.BlockSpec(memory_space=VMEM)
    return pl.pallas_call(
        body,
        out_shape=[(out_space or jax.ShapeDtypeStruct)(*o) for o in outs],
        in_specs=[whole if s is None else s for s in in_specs],
        out_specs=[whole] * len(outs) if out_specs is None else [whole if s is None else s for s in out_specs],
        scratch_shapes=list(scratch),
        compiler_params=pltpu.CompilerParams(vmem_limit_bytes=limit * MIB),
        cost_estimate=pl.CostEstimate(flops=int(flops), bytes_accessed=int(moved), transcendentals=0),
        **kwargs,
    )(*args)


def slot_mask(first, slot):
    high, mid, z = slot >> 3, (slot >> 2) & 1, slot & 3
    dy, dx = (high, mid) if first == 0 else (mid, high)
    return z * 8 + dy * 4 + dx


def put_matrix(ring, acc, own, sib, first, piece, value):
    if not ring:
        own[piece] = value
        return
    acc[...] = value
    me = my_index()
    for out, core in ((own, 0), (sib, 2)):
        for slot in range(16):
            owner = lax.bitwise_xor(me, slot_mask(first, slot) + core)
            rows = acc[pl.ds(pl.multiple_of(owner * 24, 8), 24), :]
            out[slot, piece] = low(rows.reshape(3, 8, WIDE))


def grad_shapes(ring, pieces):
    if ring:
        return [((16, pieces, 3, 8, WIDE), BF16)] * 2
    return [((pieces, D, WIDE), F32)]


def pre_kernel(ring, tok, mem, gains_in, w, wm, n1, q, k, v, kc, vc, gains):
    if ring:
        for c in range(COLS):
            gains[:, cols(c)] = jnp.sum(gains_in[0, :, c].astype(F32), axis=0)
    else:
        gains[...] = jnp.concatenate([gains_in[...].astype(F32), jnp.zeros((5, D), F32)], axis=0)
    x = tok[...].astype(F32)
    normed = low(x * inverse_rms(x) * gains[0:1, :])
    n1[...] = normed
    memory = mem[...]
    for c in range(COLS):
        q[:, cols(c)] = low(mm(normed, w[0, c]))
        k[:, cols(c)] = low(mm(normed, w[1, c]))
        v[:, cols(c)] = low(mm(normed, w[2, c]))
        kc[:, cols(c)] = low(mm(memory, wm[0, c]))
        vc[:, cols(c)] = low(mm(memory, wm[1, c]))


def halves(block):
    lane = lax.broadcasted_iota(jnp.int32, block.shape, 1)
    zero = jnp.zeros_like(block)
    return jnp.concatenate([jnp.where(lane < 64, block, zero), jnp.where(lane < 64, zero, block)], axis=0)


def side(pair):
    rows = pair.shape[0] // 2
    return jnp.concatenate([pair[:rows], pair[rows:]], axis=1)


def twice(block):
    return jnp.concatenate([block, block], axis=0)


def split_rows(pair, count):
    rows = pair.shape[0] // 2
    return jnp.concatenate([pair[:count], pair[rows : rows + count]], axis=0)


def softmax(scores):
    top = jnp.max(scores, axis=-1, keepdims=True)
    raised = jnp.exp(scores - top)
    return raised * (1.0 / jnp.sum(raised, axis=-1, keepdims=True))


def pair_bias(line):
    rows = [
        pltpu.roll(jnp.broadcast_to(line[h : h + 1, :], (QROWS, 2 * QROWS)), 0, 1, stride=1, stride_axis=0)
        for h in range(2)
    ]
    far = jnp.concatenate([jnp.broadcast_to(line[h : h + 1, 0:1], (QROWS, 1)) for h in range(2)], axis=0)
    return jnp.concatenate(rows, axis=0), far


def self_probs(block, q2, k, bias, far, seg_col, seg_row):
    end = (block + 1) * QROWS
    scores = mm_nt(q2, k[:end])
    if block == 0:
        scores = scores + bias[:, QROWS:]
    elif block == 1:
        scores = scores + bias
    else:
        scores = jnp.concatenate([scores[:, : end - 2 * QROWS] + far, scores[:, end - 2 * QROWS :] + bias], axis=1)
    keep = seg_col == seg_row[:, :end]
    row = lax.broadcasted_iota(jnp.int32, (QROWS, end), 0) + block * QROWS
    keep = keep & (lax.broadcasted_iota(jnp.int32, (QROWS, end), 1) <= row)
    return softmax(jnp.where(twice(keep), scores, NEG_FILL))


def cross_probs(q2, k, seg_col, seg_row):
    keep = seg_col == seg_row
    return softmax(jnp.where(twice(keep), mm_nt(q2, k), NEG_FILL))


def self_forward_kernel(q, k, v, line, seg_col, seg_row, out):
    bias, far = pair_bias(line[0])
    keys, values = k[...], halves(v[...])
    for block in range(TGT_LEN // QROWS):
        rows = slice(block * QROWS, (block + 1) * QROWS)
        probs = self_probs(block, halves(q[rows, :]), keys, bias, far, seg_col[rows, :], seg_row[...])
        out[rows, :] = low(mm(side(low(probs)), split_rows(values, (block + 1) * QROWS)))


def cross_forward_kernel(q, k, v, seg_col, seg_row, out):
    keys, values = k[...], halves(v[...])
    for block in range(TGT_LEN // QROWS):
        rows = slice(block * QROWS, (block + 1) * QROWS)
        probs = cross_probs(halves(q[rows, :]), keys, seg_col[rows, :], seg_row[...])
        out[rows, :] = low(mm(side(low(probs)), values))


def pair_spec(length):
    return pl.BlockSpec((length, 128), lambda p: (0, p))


LINE_SPEC = pl.BlockSpec((1, 2, 2 * QROWS), lambda p: (p, 0, 0))


def mid_kernel(ctx, tok, gains, w, res, n2, qc):
    context = ctx[...]
    for c in range(COLS):
        res[:, cols(c)] = tok[:, cols(c)].astype(F32) + mm(context, w[0, c])
    x = res[...]
    normed = low(x * inverse_rms(x) * gains[1:2, :])
    n2[...] = normed
    for c in range(COLS):
        qc[:, cols(c)] = low(mm(normed, w[1, c]))


def late_kernel(ctx, res1, gains, w, res2, n3):
    context = ctx[...]
    for c in range(COLS):
        res2[:, cols(c)] = res1[:, cols(c)] + mm(context, w[0, c])
    x = res2[...]
    n3[...] = low(x * inverse_rms(x) * gains[2:3, :])


def gelu_pair(gate):
    rate = math.sqrt(2.0 / math.pi)
    square = gate * gate
    bend = jnp.tanh(rate * gate * (1.0 + 0.044715 * square))
    half = 0.5 * (1.0 + bend)
    slope = half + 0.5 * gate * (1.0 - bend * bend) * rate * (1.0 + 3.0 * 0.044715 * square)
    return gate * half, slope


def ffn_kernel(ring, n3, res2, cot, gate_w, lift_w, con_w, out, dn3, *rest):
    grads, (n3t, total, acc, con_acc) = rest[:-4], rest[-4:]
    block = pl.program_id(0)

    @pl.when(block == 0)
    def _():
        n3t[...] = n3[...].T
        total[...] = res2[...]
        dn3[...] = jnp.zeros_like(dn3)

    normed = n3[...]
    gate_rows, lift_rows = gate_w[0, 0], lift_w[0, 0]
    lift = mm(normed, lift_rows)
    active, slope = gelu_pair(mm(normed, gate_rows))
    hidden = low(active * lift)
    back = jnp.zeros(lift.shape, F32)
    for c in range(COLS):
        total[:, cols(c)] += mm(hidden, con_w[c])
        back = back + mm_nt(cot[:, cols(c)], con_w[c])
    gate_grad = low(back * lift * slope)
    lift_grad = low(back * active)
    dn3[...] += mm_nt(gate_grad, gate_rows) + mm_nt(lift_grad, lift_rows)
    turned = hidden.T
    if ring:
        own_a, own_b, sib_a, sib_b = grads
        put_matrix(ring, acc, own_a, sib_a, 0, block, mm(n3t[...], gate_grad))
        put_matrix(ring, acc, own_b, sib_b, 1, block, mm(n3t[...], lift_grad))
        me = my_index()
        near = lax.bitwise_xor(block, lax.shift_right_logical(me, 2))
        dz, dy = lax.shift_right_logical(near, 1), lax.bitwise_and(near, 1)
        inner = lax.bitwise_and(me, 3)
        for c in range(COLS):
            con_acc[...] = mm(turned, cot[:, cols(c)])
            for core in range(2):
                for dx in range(2):
                    place = lax.bitwise_xor(inner, core * 2 + dx)
                    rows = low(con_acc[pl.ds(pl.multiple_of(place * 64, 8), 64), :].reshape(8, 8, WIDE))
                    (own_a, sib_a)[core][dy * 8 + dx * 4 + dz, 8:12, c] = rows[:4]
                    (own_b, sib_b)[core][dx * 8 + dy * 4 + dz, 8:12, c] = rows[4:]
    else:
        gate_out, lift_out, con_out = grads
        gate_out[block] = mm(n3t[...], gate_grad)
        lift_out[block] = mm(n3t[...], lift_grad)
        for c in range(COLS):
            con_out[c, pl.ds(pl.multiple_of(block * WIDE, 8), WIDE), :] = mm(turned, cot[:, cols(c)])

    @pl.when(block == BLOCKS - 1)
    def _():
        out[...] = low(total[...])


def third_back_kernel(dn3, res2, cot, gains, w, r2g, ccg, gg):
    back, gain_grad = norm_back(res2[...], gains[2:3, :], dn3[...])
    gg[...] = gain_grad
    grad = cot[...].astype(F32) + back
    r2g[...] = grad
    cross_low = low(grad)
    total = mm_nt(cross_low[:, cols(0)], w[0, 0])
    for c in range(1, COLS):
        total = total + mm_nt(cross_low[:, cols(c)], w[0, c])
    ccg[...] = low(total)


def backward_block(probs, q2, dc2, keys2, values, dq, dk, dv, rows, end):
    prob_grad = mm_nt(dc2, values[:end])
    moved = probs * prob_grad
    score_grad = low(moved - probs * jnp.sum(moved, axis=-1, keepdims=True))
    dq[rows, :] = low(mm(side(score_grad), split_rows(keys2, end)))
    dk[:end, :] += mm_tn(score_grad, q2)
    dv[:end, :] += mm_tn(low(probs), dc2)
    return score_grad


def cross_back_kernel(q, k, v, dc, seg_col, seg_row, dq, dk, dv, dk_acc, dv_acc):
    dk_acc[...] = jnp.zeros_like(dk_acc)
    dv_acc[...] = jnp.zeros_like(dv_acc)
    keys, values = k[...], v[...]
    keys2 = halves(keys)
    for block in range(TGT_LEN // QROWS):
        rows = slice(block * QROWS, (block + 1) * QROWS)
        q2 = halves(q[rows, :])
        probs = cross_probs(q2, keys, seg_col[rows, :], seg_row[...])
        backward_block(probs, q2, halves(dc[rows, :]), keys2, values, dq, dk_acc, dv_acc, rows, MEM_LEN)
    dk[...] = low(dk_acc[...])
    dv[...] = low(dv_acc[...])


def diagonal_sums(grid, start):
    width = 2 * QROWS
    group = grid[start : start + 8, :]
    for shift in range(8, QROWS, 8):
        group = group + pltpu.roll(grid[start + shift : start + shift + 8, :], width - shift, 1)
    row = lax.broadcasted_iota(jnp.int32, group.shape, 0)
    for bit in (1, 2, 4):
        group = jnp.where((row & bit) != 0, pltpu.roll(group, width - bit, 1), group)
    return jnp.sum(group, axis=0, keepdims=True)


def self_back_kernel(q, k, v, dc, line, seg_col, seg_row, dq, dk, dv, diag, dk_acc, dv_acc, near):
    dk_acc[...] = jnp.zeros_like(dk_acc)
    dv_acc[...] = jnp.zeros_like(dv_acc)
    bias, far = pair_bias(line[0])
    keys, values = k[...], v[...]
    keys2 = halves(keys)
    far_sum = jnp.zeros((2 * QROWS, QROWS), F32)
    for block in range(TGT_LEN // QROWS):
        rows = slice(block * QROWS, (block + 1) * QROWS)
        end = (block + 1) * QROWS
        q2 = halves(q[rows, :])
        probs = self_probs(block, q2, keys, bias, far, seg_col[rows, :], seg_row[...])
        score_grad = backward_block(
            probs, q2, halves(dc[rows, :]), keys2, values, dq, dk_acc, dv_acc, rows, end
        ).astype(F32)
        if block == 0:
            near[:, :QROWS] = jnp.zeros((2 * QROWS, QROWS), F32)
            near[:, QROWS:] = score_grad
        else:
            near[...] += score_grad[:, end - 2 * QROWS :]
        for other in range(block - 1):
            far_sum = far_sum + score_grad[:, other * QROWS : (other + 1) * QROWS]
    dk[...] = low(dk_acc[...])
    dv[...] = low(dv_acc[...])
    lane = lax.broadcasted_iota(jnp.int32, (1, 2 * QROWS), 1)
    for h in range(2):
        beyond = jnp.sum(far_sum[h * QROWS : (h + 1) * QROWS, :], keepdims=True)
        diag[0, h : h + 1, :] = diagonal_sums(near, h * QROWS) + jnp.where(lane == 0, beyond, 0.0)


def second_back_kernel(dq, res1, r2g, gains, w, r1g, csg, gg):
    query_grad = dq[...]
    back = mm_nt(query_grad[:, cols(0)], w[1, 0])
    for c in range(1, COLS):
        back = back + mm_nt(query_grad[:, cols(c)], w[1, c])
    moved, gain_grad = norm_back(res1[...], gains[1:2, :], back)
    gg[...] = gain_grad
    grad = r2g[...] + moved
    r1g[...] = grad
    self_low = low(grad)
    total = mm_nt(self_low[:, cols(0)], w[0, 0])
    for c in range(1, COLS):
        total = total + mm_nt(self_low[:, cols(c)], w[0, c])
    csg[...] = low(total)


def memory_grads_kernel(ring, dk, dv, mem, w, mg, *rest):
    grads, acc = rest[:-1], rest[-1]
    left = mem[...].T
    for matrix, right in enumerate((dk, dv)):
        for c in range(COLS):
            put_matrix(ring, acc, grads[0], grads[-1], 0, matrix * COLS + c, mm(left, right[:, cols(c)]))
    total = mm_nt(dk[:, cols(0)], w[0, 0]) + mm_nt(dv[:, cols(0)], w[1, 0])
    for c in range(1, COLS):
        total = total + mm_nt(dk[:, cols(c)], w[0, c]) + mm_nt(dv[:, cols(c)], w[1, c])
    mg[...] = low(total)


def middle_grads_kernel(ring, dq, n2, r1g, ctxs, r2g, ctxc, *rest):
    grads, acc = rest[:-1], rest[-1]
    for index, (left, right) in enumerate(((ctxs, low(r1g[...])), (n2, dq[...]), (ctxc, low(r2g[...])))):
        left = left[...].T
        for c in range(COLS):
            put_matrix(ring, acc, grads[0], grads[-1], 1, index * COLS + c, mm(left, right[:, cols(c)]))


def put_piece(ring, grads, acc, index, split, value):
    if not ring:
        grads[0][index] = value
        return
    own_a, own_b, sib_a, sib_b = grads
    if index < split:
        put_matrix(ring, acc, own_a, sib_a, 0, index, value)
    else:
        put_matrix(ring, acc, own_b, sib_b, 1, index - split, value)


def first_grads_kernel(ring, dq, dk, dv, n1, *rest):
    grads, acc = rest[:-1], rest[-1]
    left = n1[...].T
    for matrix, right in enumerate((dq, dk, dv)):
        for c in range(COLS):
            put_piece(ring, grads, acc, matrix * COLS + c, 5, mm(left, right[:, cols(c)]))


def first_back_kernel(dq, dk, dv, tok, r1g, gains, w, ig, gg):
    back = None
    for matrix, right in enumerate((dq, dk, dv)):
        for c in range(COLS):
            term = mm_nt(right[:, cols(c)], w[matrix, c])
            back = term if back is None else back + term
    moved, gain_grad = norm_back(tok[...].astype(F32), gains[0:1, :], back)
    gg[...] = gain_grad
    ig[...] = low(r1g[...] + moved)


ROW_GAINS, ROW_CONTRACT, ROW_EXPAND, ROW_BUCKETS, SUM_ROWS = 8, 11, 12, 18, 24
RUNS = ((0, D), (D, D), (2 * D, FF - 2 * D))


def squares_of(values):
    return values * values + TINY


def row_line(values):
    squares = squares_of(values)
    width = squares.shape[1]
    part = squares[:, :128]
    for start in range(128, width, 128):
        part = part + squares[:, start : start + 128]
    return jnp.sum(part.T, axis=0, keepdims=True) * (1.0 / width)


def share_kernel(
    m1, n1, f1, m2, n2, f2, m3, a3, b3, c3, gain_one, gain_two, gain_three, diag, onehot, att, exp, con, sums
):
    ffn = m1[...] + n1[...].astype(F32) + f1[...].astype(F32)
    cross = m2[...] + n2[...].astype(F32) + f2[...].astype(F32)
    own = m3[...] + a3[...].astype(F32) + (b3[...].astype(F32) + c3[...].astype(F32))
    sums[...] = jnp.zeros_like(sums)

    def keep(out, matrix, row, column, piece):
        rows = piece.reshape(24, WIDE)
        out[matrix, :, cols(column)] = rows
        place = column * WIDE
        sums[row + place // D : row + place // D + 1, place % D : place % D + WIDE] = jnp.sum(
            squares_of(rows), axis=0, keepdims=True
        )

    for c in range(COLS):
        for matrix in range(3):
            keep(att, matrix, matrix, c, own[matrix * COLS + c])
        for index, matrix in enumerate((5, 6, 3, 4, 7)):
            keep(att, matrix, matrix, c, cross[index * COLS + c])
        total = jnp.zeros((1, WIDE), F32)
        for octet in range(8):
            rows = ffn[8 + octet if octet < 4 else 16 + octet, c]
            con[octet * 8 : octet * 8 + 8, cols(c)] = rows
            total = total + jnp.sum(squares_of(rows), axis=0, keepdims=True)
        sums[ROW_CONTRACT : ROW_CONTRACT + 1, cols(c)] = total
    for b in range(BLOCKS):
        keep(exp, 0, ROW_EXPAND, b, ffn[b])
        keep(exp, 1, ROW_EXPAND + 3, b, ffn[12 + b])
    for row, gain in enumerate((gain_one, gain_two, gain_three)):
        sums[ROW_GAINS + row : ROW_GAINS + row + 1, :] = gain[...]
    for h in range(2):
        sums[ROW_BUCKETS:SUM_ROWS, h * BUCKETS : (h + 1) * BUCKETS] = jnp.dot(
            diag[:, h, :], onehot[...], precision=lax.Precision.HIGHEST, preferred_element_type=F32
        )


def rows_kernel(att, exp, con, att_rows, exp_rows, con_rows, pair_rows):
    for row, matrix in enumerate((0, 1, 2, 4, 5, 6)):
        att_rows[row : row + 1, :] = row_line(att[matrix])
    for row, matrix in enumerate((3, 7)):
        pair_rows[row : row + 1, :] = row_line(att[matrix])
    for matrix in range(2):
        exp_rows[matrix : matrix + 1, :] = row_line(exp[matrix])
    con_rows[...] = row_line(con[...])


def new_rows(weight, grad, column_stat):
    squares = squares_of(grad)
    row_stat = jnp.mean(squares, axis=-1, keepdims=True)
    scale = jnp.mean(column_stat, axis=-1, keepdims=True)
    second = (row_stat / scale) * column_stat
    return weight.astype(F32) - STEP_RATE * grad * lax.rsqrt(second)


def update_kernel(
    sums, att, exp, con, att_w, exp_w, con_w, att_new, exp_new, con_new, att_cols, exp_cols, con_cols, gains, pair_cols, buckets
):
    me = my_index()
    square = sums[0:8, :] * (1.0 / D)
    for matrix in range(8):
        att_new[matrix] = new_rows(att_w[matrix], att[matrix], square[matrix : matrix + 1, :])
    for row, matrix in enumerate((0, 1, 2, 4, 5, 6)):
        att_cols[row : row + 1, :] = square[matrix : matrix + 1, :]
    for matrix in range(2):
        first = ROW_EXPAND + 3 * matrix
        line = jnp.concatenate([sums[first + i : first + i + 1, :size] for i, (_, size) in enumerate(RUNS)], axis=1)
        line = line * (1.0 / D)
        exp_cols[matrix : matrix + 1, :] = line
        exp_new[matrix] = new_rows(exp_w[matrix], exp[matrix], line)
    line = sums[ROW_CONTRACT : ROW_CONTRACT + 1, :] * (1.0 / FF)
    con_cols[...] = line
    con_new[...] = new_rows(con_w[...], con[...], line)
    shift = lax.rem(D - me * 24, D)
    gains[...] = pltpu.roll(sums[8:16, :], shift, 1)[0:3, :24]
    turned = pltpu.roll(square, shift, 1)
    pair_cols[0:1, :] = turned[3:4, :24]
    pair_cols[1:2, :] = turned[7:8, :24]
    lines = sums[16:24, :128].T
    row = lax.broadcasted_iota(jnp.int32, (8, HEADS), 0)
    column = lax.broadcasted_iota(jnp.int32, (8, HEADS), 1)
    total = jnp.zeros((BUCKETS, HEADS), F32)
    for h in range(2):
        pick = jnp.where(column == 2 * (row - (ROW_BUCKETS - 16)) + h, 1.0, 0.0)
        total = total + jnp.dot(
            lines[h * BUCKETS : (h + 1) * BUCKETS, :],
            pick,
            precision=lax.Precision.HIGHEST,
            preferred_element_type=F32,
        )
    buckets[...] = total


def hop(values, mask):
    return lax.ppermute(values, AXES, [(k, k ^ mask) for k in range(32)])


def after(values, *earlier):
    return lax.optimization_barrier((values,) + earlier)[0]


def place_kernel(plan, targets, count, *refs):
    ins, outs, sem = refs[:count], refs[count:-1], refs[-1]
    me = my_index()
    copies = []
    for ref, (masks, low_piece, high_piece) in zip(ins, plan):
        for index, mask in enumerate(masks):
            owner = lax.bitwise_xor(me, mask)
            for out, first, last, start, column in targets:
                begin, end = max(low_piece, first), min(high_piece, last)
                if begin >= end:
                    continue
                pieces = pl.ds(begin - low_piece, end - begin)
                into = pl.ds(start + begin - first, end - begin)
                if column is None:
                    pair = (ref.at[index, pieces], outs[out].at[into, owner])
                else:
                    pair = (ref.at[index, pieces, column], outs[out].at[column, owner, into])
                copies.append(pltpu.make_async_copy(*pair, sem.at[len(copies)]))
                copies[-1].start()
    for copy in copies:
        copy.wait()


def place(arrays, outs, targets):
    plan = [a[1:] for a in arrays]
    return call(
        functools.partial(place_kernel, plan, targets, len(arrays)),
        [(o, BF16) for o in outs],
        [pl.BlockSpec(memory_space=pltpu.HBM)] * len(arrays),
        [pltpu.with_memory_space_constraint(a[0], pltpu.HBM) for a in arrays],
        0,
        4 * sum(math.prod(o) for o in outs),
        scratch=[pltpu.SemaphoreType.DMA((320,))],
        limit=20,
        out_space=VMEM,
    )


def with_core(arrays):
    return arrays + [(hop(a, 2), [m + 2 for m in masks], lo, hi) for a, masks, lo, hi in arrays]


def make_pieces(attention, expand, contract, gains):
    attention_pieces = attention.reshape(8, 24, COLS, WIDE).transpose(0, 2, 1, 3).reshape(24, 3, 8, WIDE)
    line = lax.dynamic_update_slice_in_dim(jnp.zeros((8, D), BF16), jnp.pad(gains, ((0, 5), (0, 0))), my_index() * 24, 1)
    gain_piece = line.reshape(1, 8, COLS, WIDE).transpose(0, 2, 1, 3)
    first = jnp.concatenate([attention_pieces, gain_piece])
    expand_pieces = expand.reshape(2, 24, BLOCKS, WIDE).transpose(0, 2, 1, 3).reshape(2, BLOCKS, 3, 8, WIDE)
    contract_pieces = contract.reshape(8, 8, COLS, WIDE).transpose(0, 2, 1, 3)
    second = jnp.concatenate([expand_pieces[0], contract_pieces[:4], expand_pieces[1], contract_pieces[4:]])
    return first, second


HALF = 12


def hop_xy(values):
    return values, hop(values, 1), hop(values, 4)


def spread_end(parts, masks):
    pieces = parts[0][0].shape[1]
    by_x = [p[1][:, :HALF] for p in parts]
    by_y = [p[2][:, HALF:] for p in parts]
    first = hop(jnp.concatenate(by_x) if len(parts) > 1 else by_x[0], 4)
    second = hop(jnp.concatenate(by_y) if len(parts) > 1 else by_y[0], 1)
    arrays, start = [], 0
    for own, x, y in parts:
        own_masks = masks[start : start + own.shape[0]]
        start += own.shape[0]
        arrays += [(own, own_masks, 0, pieces), (x, [m + 1 for m in own_masks], 0, pieces)]
        arrays += [(y, [m + 4 for m in own_masks], 0, pieces)]
    return arrays + [(first, [m + 5 for m in masks], 0, HALF), (second, [m + 5 for m in masks], HALF, pieces)]


def place_first(arrays):
    *groups, gains = place(
        arrays,
        [(n, 32, 3, 8, WIDE) for n in (9, 6, 6, 3, 1)],
        [(0, 0, 9, 0, None), (1, 9, 15, 0, None), (2, 15, 21, 0, None), (3, 21, 24, 0, None), (4, 24, 25, 0, None)],
    )
    return [w.reshape(-1, COLS, D, WIDE) for w in groups], gains


def place_second(arrays):
    wide, narrow = place(
        arrays,
        [(16, 32, 3, 8, WIDE), (COLS, 32, 8, 8, WIDE)],
        [(0, 0, 8, 0, None), (0, 12, 20, 8, None)]
        + [(1, 8, 12, 0, c) for c in range(COLS)]
        + [(1, 20, 24, 4, c) for c in range(COLS)],
    )
    return wide.reshape(2, BLOCKS, D, WIDE), narrow.reshape(COLS, FF, WIDE)


def gather_plain(attention, expand, contract, gains):
    attention, expand, contract, gains = (
        lax.all_gather(attention, AXES, axis=1, tiled=True),
        lax.all_gather(expand, AXES, axis=1, tiled=True),
        lax.all_gather(contract, AXES, axis=0, tiled=True),
        lax.all_gather(gains, AXES, axis=1, tiled=True),
    )
    return (
        attention.reshape(8, D, COLS, WIDE).transpose(0, 2, 1, 3),
        expand.reshape(2, D, BLOCKS, WIDE).transpose(0, 2, 1, 3),
        contract.reshape(FF, COLS, WIDE).transpose(1, 0, 2),
        gains,
    )


def total(*terms):
    result = terms[0].astype(F32)
    for term in terms[1:]:
        result = result + term.astype(F32)
    return result


class Scatter:
    def __init__(self, grads):
        self.own_a, self.own_b, self.sib_a, self.sib_b = grads

    def core(self):
        self.from_a, self.from_b = hop(self.sib_a, 2), hop(self.sib_b, 2)

    def pin(self, earlier):
        if earlier:
            self.own_a, self.own_b = lax.optimization_barrier((self.own_a, self.own_b) + earlier)[:2]

    def first(self, *earlier):
        self.pin(earlier)
        send_a = low(total(self.own_a[8:], self.from_a[8:]))
        send_b = low(total(self.own_b[8:], self.from_b[8:]))
        self.a1, self.b1 = hop(send_a, 4), hop(send_b, 1)
        return send_a, send_b

    def second(self, *earlier):
        self.pin(earlier)
        next_a = low(total(self.own_a[4:8], self.from_a[4:8], self.a1[4:]))
        next_b = low(total(self.own_b[4:8], self.from_b[4:8], self.b1[4:]))
        self.a2, self.b2 = hop(next_a, 1), hop(next_b, 4)
        return next_a, next_b

    def third(self, *earlier):
        self.pin(earlier)
        mine_a = total(self.own_a[:4], self.from_a[:4], self.a1[:4], self.a2)
        mine_b = total(self.own_b[:4], self.from_b[:4], self.b1[:4], self.b2)
        self.mine = jnp.concatenate([mine_a, mine_b], axis=1)
        send = low(self.mine[1:3])
        self.near = hop(send, 8)
        return (send,)

    def fourth(self, *earlier):
        mine = after(self.mine, *earlier) if earlier else self.mine
        send = low(mine[3] + self.near[1].astype(F32))
        self.far = hop(send, 24)
        return (send,)

    def third_direct(self):
        mine_a = total(self.own_a[:4], self.from_a[:4], self.a1[:4], self.a2)
        mine_b = total(self.own_b[:4], self.from_b[:4], self.b1[:4], self.b2)
        self.mine = jnp.concatenate([mine_a, mine_b], axis=1)
        send = low(self.mine)
        self.parts = [hop(send[d], 8 * d) for d in (1, 3, 2)]

    def share(self):
        if hasattr(self, "parts"):
            return total(self.mine[0], *self.parts)
        return total(self.mine[0], self.near[0], self.far)


def scatter_plain(pieces, shape, axis):
    count = pieces.shape[0]
    if axis == 0:
        whole = pieces.transpose(1, 0, 2).reshape(shape)
    else:
        per = shape[2] // WIDE
        whole = pieces.reshape(shape[0], per, shape[1], WIDE).transpose(0, 2, 1, 3).reshape(shape)
    return lax.psum_scatter(whole, AXES, scatter_dimension=axis, tiled=True)


def sum_ring(values):
    values = values + hop(values, 2)
    values = (values + hop(values, 1)) + (hop(values, 4) + hop(values, 5))
    return (values + hop(values, 8)) + (hop(values, 16) + hop(values, 24))


def factored_stats(grad_shard, total_rows):
    squares = grad_shard * grad_shard + TINY
    return (jnp.mean(squares, axis=-1), jnp.sum(squares, axis=-2) / total_rows)


def factored_update(weight_shard, grad_shard, row_stat, column_stat):
    scale = jnp.mean(column_stat, axis=-1, keepdims=True)[..., None]
    second = row_stat[..., :, None] * column_stat[..., None, :] / scale
    return weight_shard.astype(F32) - STEP_RATE * grad_shard * lax.rsqrt(second)


def without_outputs(stats):
    return jnp.concatenate([stats[0:3], stats[4:7]], axis=0)


def output_pair(stats):
    return jnp.stack([stats[3], stats[7]])


def on_device(
    ring,
    tokens,
    memory,
    target_segments,
    memory_segments,
    attention_weights,
    expand_weights,
    contract_weights,
    norm_gains,
    bucket_table,
    cotangent,
):
    rows = tokens.shape[0]
    spread_buckets = jnp.asarray(diagonal_onehot())
    lines = jnp.dot(
        bucket_table.T.astype(F32), spread_buckets.T, precision=lax.Precision.HIGHEST, preferred_element_type=F32
    ).reshape(PAIRS, 2, 2 * QROWS)
    target_col, target_row = target_segments.reshape(rows, 1), target_segments.reshape(1, rows)
    memory_row = memory_segments.reshape(1, rows)
    act, act32 = ((rows, D), BF16), ((rows, D), F32)
    size = rows * D
    product = 2 * size * D
    none = [None]
    pair = pair_spec(rows)
    heads_work = 2 * HEADS * rows * rows * 256
    acc = VMEM((D, WIDE), F32)
    head_acc = VMEM((rows, 128), F32)

    if ring:
        first, second = make_pieces(attention_weights, expand_weights, contract_weights, norm_gains)
        first, second = first[None], second[None]
        z1 = hop(first, 8)
        own1 = hop_xy(first)
        near1 = hop_xy(z1)
        z3 = hop(after(first, z1, own1[1], own1[2], lines, target_col), 24)
        first_a = with_core(spread_end([own1, near1], [0, 8]))
        z2 = hop(after(z3, near1[1], near1[2]), 8)
        v1 = hop(after(second, z2), 8)
        own2 = hop_xy(after(second, near1[1], near1[2]))
        far1 = hop_xy(after(jnp.concatenate([z2, z3]), first_a[3][0], first_a[4][0]))
        v3 = hop(after(second, v1, own2[1], own2[2]), 24)
        first_b = with_core(spread_end([far1], [16, 24]))
        v2 = hop(v3, 8)
        near2 = hop_xy(after(v1, far1[1], far1[2]))
        squares, gains_in = place_first(first_a + first_b)
        far2 = hop_xy(after(jnp.concatenate([v2, v3]), squares[0]))
    else:
        square, wide, narrow, gains_in = gather_plain(
            attention_weights, expand_weights, contract_weights, norm_gains
        )
        squares = [square[0:3], square[3:5], square[5:7], square[7:8]]
    if ring:
        squares = [in_vmem(w) for w in squares]
    w_self, w_mid, w_memory, w_late = squares

    n1, q, k, v, kc, vc, gains = call(
        functools.partial(pre_kernel, ring),
        [act] * 6 + [((8, D), F32)],
        none * 5,
        (tokens, memory, gains_in, w_self, w_memory),
        5 * product,
        2 * (8 * size + 5 * D * D),
    )
    if ring:
        near2 = tuple(lax.optimization_barrier(near2 + (q,))[:3])
        second_a = spread_end([own2, near2], [0, 8])
    ctxs = call(
        self_forward_kernel,
        [act],
        [pair] * 3 + [LINE_SPEC, None, None],
        (q, k, v, lines, target_col, target_row),
        2 * heads_work,
        8 * size,
        grid=(PAIRS,),
        out_specs=[pair],
    )[0]
    if ring:
        second_a = with_core([(after(a[0], ctxs), *a[1:]) for a in second_a])
        far2 = tuple(lax.optimization_barrier(far2 + (ctxs,))[:3])
        second_b = spread_end([far2], [16, 24])
        ctxs = after(ctxs, far2[1], far2[2])
    res1, n2, qc = call(
        mid_kernel, [act32, act, act], none * 4, (ctxs, tokens, gains, w_mid), 2 * product, 14 * size + 4 * D * D
    )
    if ring:
        second_b = with_core(second_b)
    ctxc = call(
        cross_forward_kernel,
        [act],
        [pair] * 3 + [None, None],
        (qc, kc, vc, target_col, memory_row),
        2 * heads_work,
        8 * size,
        grid=(PAIRS,),
        out_specs=[pair],
    )[0]
    res2, n3 = call(late_kernel, [act32, act], none * 4, (ctxc, res1, gains, w_late), product, 14 * size)
    if ring:
        wide, narrow = (in_vmem(w) for w in place_second(second_a + second_b))

    expand_block = lambda m: pl.BlockSpec((1, 1, D, WIDE), lambda b: (m, b, 0, 0))
    if ring:
        grad_outs = [((16, 12, 3, 8, WIDE), BF16)] * 4
    else:
        grad_outs = [((BLOCKS, D, WIDE), F32)] * 2 + [((COLS, FF, WIDE), F32)]
    output, dn3, *ffn_grads = call(
        functools.partial(ffn_kernel, ring),
        [act, act32] + grad_outs,
        none * 3 + [expand_block(0), expand_block(1), pl.BlockSpec((COLS, WIDE, WIDE), lambda b: (0, b, 0))],
        (n3, res2, cotangent, wide, wide, narrow),
        9 * 2 * rows * D * FF,
        4 * 3 * D * FF,
        grid=(BLOCKS,),
        scratch=[
            VMEM((D, rows), BF16),
            VMEM((rows, D), F32),
            VMEM((D, WIDE), F32),
            VMEM((WIDE, WIDE), F32),
        ],
        limit=28,
    )
    if ring:
        ffn = Scatter(ffn_grads)
        ffn.core()

    r2g, ccg, gain_three = call(
        third_back_kernel,
        [act32, act, ((1, D), F32)],
        none * 5,
        (dn3, res2, cotangent, gains, w_late),
        product,
        16 * size,
    )
    if ring:
        ccg = after(ccg, *ffn.first(r2g))
    dqc, dkc, dvc = call(
        cross_back_kernel,
        [act] * 3,
        [pair] * 4 + [None, None],
        (qc, kc, vc, ccg, target_col, memory_row),
        5 * heads_work,
        14 * size,
        grid=(PAIRS,),
        scratch=[head_acc, head_acc],
        out_specs=[pair] * 3,
    )
    memory_grad, *cross_a = call(
        functools.partial(memory_grads_kernel, ring),
        [act] + grad_shapes(ring, 6),
        none * 4,
        (dkc, dvc, memory, w_memory),
        4 * product,
        8 * size + 10 * D * D,
        scratch=[acc],
    )
    if ring:
        dqc = after(dqc, *ffn.second(memory_grad))
    r1g, csg, gain_two = call(
        second_back_kernel,
        [act32, act, ((1, D), F32)],
        none * 5,
        (dqc, res1, r2g, gains, w_mid),
        2 * product,
        16 * size,
    )
    cross_b = call(
        functools.partial(middle_grads_kernel, ring),
        grad_shapes(ring, 9),
        none * 6,
        (dqc, n2, r1g, ctxs, r2g, ctxc),
        3 * product,
        16 * size + 12 * D * D,
        scratch=[acc],
    )
    if ring:
        cross = Scatter([cross_a[0], cross_b[0], cross_a[1], cross_b[1]])
        cross.core()
        csg = after(csg, *ffn.third(cross_b[0]), *cross.first())
    dqs, dks, dvs, diag = call(
        self_back_kernel,
        [act] * 3 + [((PAIRS, 2, 2 * QROWS), F32)],
        [pair] * 4 + [LINE_SPEC, None, None],
        (q, k, v, csg, lines, target_col, target_row),
        5 * heads_work,
        14 * size,
        grid=(PAIRS,),
        scratch=[head_acc, head_acc, VMEM((2 * QROWS, 2 * QROWS), F32)],
        out_specs=[pair] * 3 + [LINE_SPEC],
    )
    if ring:
        dqs = after(dqs, *ffn.fourth(dqs), *cross.second(dqs))
    first_grads = grad_shapes(ring, 5) + grad_shapes(ring, 4) if ring else grad_shapes(ring, 9)
    if ring:
        first_grads = [first_grads[0], first_grads[2], first_grads[1], first_grads[3]]
    self_grads = call(
        functools.partial(first_grads_kernel, ring),
        first_grads,
        none * 4,
        (dqs, dks, dvs, n1),
        3 * product,
        8 * size + 6 * D * D,
        scratch=[acc],
    )
    if ring:
        own = Scatter(self_grads)
        own.core()
        dks = after(dks, *own.first())
    input_grad, gain_one = call(
        first_back_kernel,
        [act, ((1, D), F32)],
        none * 7,
        (dqs, dks, dvs, tokens, r1g, gains, w_self),
        3 * product,
        16 * size + 6 * D * D,
    )
    if ring:
        cross.third(input_grad)
        own.second(input_grad)
        cross.fourth()
        own.third_direct()
    gain_parts = (gain_one, gain_two, gain_three)
    if ring:
        parts = []
        for group in (ffn, cross):
            parts += [group.mine[0], group.near[0], group.far]
        parts += [own.mine[0]] + own.parts
        attention_grad, expand_grad, contract_grad, sums = call(
            share_kernel,
            [((8, 24, D), F32), ((2, 24, FF), F32), ((64, D), F32), ((SUM_ROWS, D), F32)],
            none * (len(parts) + 5),
            (*parts, *gain_parts, diag, spread_buckets),
            0,
            16 * 24 * 24 * WIDE,
        )
        sums = sum_ring(sums)
        attention_rows, expand_rows, contract_rows, pair_rows = call(
            rows_kernel,
            [((6, 24), F32), ((2, 24), F32), ((1, 64), F32), ((2, 24), F32)],
            none * 3,
            (attention_grad, expand_grad, contract_grad),
            0,
            4 * 48 * 24 * WIDE,
        )
        (
            attention_new,
            expand_new,
            contract_new,
            attention_columns,
            expand_columns,
            contract_columns,
            gains_grad,
            pair_columns,
            bucket_grad,
        ) = call(
            update_kernel,
            [
                ((8, 24, D), F32),
                ((2, 24, FF), F32),
                ((64, D), F32),
                ((6, D), F32),
                ((2, FF), F32),
                ((1, D), F32),
                ((3, 24), F32),
                ((2, 24), F32),
                ((BUCKETS, HEADS), F32),
            ],
            none * 7,
            (sums, attention_grad, expand_grad, contract_grad, attention_weights, expand_weights, contract_weights),
            0,
            10 * 48 * 24 * WIDE,
        )
        contract_rows, contract_columns = contract_rows.reshape(64), contract_columns.reshape(D)
        projection_statistics = jnp.stack([pair_rows, pair_columns])
    else:
        bucket_part = jnp.dot(
            spread_buckets.T,
            diag.reshape(HEADS, 2 * QROWS).T,
            precision=lax.Precision.HIGHEST,
            preferred_element_type=F32,
        )
        pieces = jnp.concatenate([self_grads[0], cross_b[0][:6], cross_a[0], cross_b[0][6:]])
        attention_grad = scatter_plain(pieces, (8, D, D), 1)
        expand_grad = scatter_plain(jnp.stack(ffn_grads[:2]), (2, D, FF), 1)
        contract_grad = scatter_plain(ffn_grads[2], (FF, D), 0)
        attention_rows, attention_part = factored_stats(attention_grad, D)
        expand_rows, expand_part = factored_stats(expand_grad, D)
        contract_rows, contract_part = factored_stats(contract_grad, FF)
        attention_columns, expand_columns, contract_columns, bucket_grad, gains_sum = lax.psum(
            (attention_part, expand_part, contract_part, bucket_part, jnp.concatenate(gain_parts)), AXES
        )
        attention_new = factored_update(attention_weights, attention_grad, attention_rows, attention_columns)
        expand_new = factored_update(expand_weights, expand_grad, expand_rows, expand_columns)
        contract_new = factored_update(contract_weights, contract_grad, contract_rows, contract_columns)
        share_width = attention_rows.shape[1]
        share_start = lax.axis_index(AXES) * share_width
        column_share = lax.dynamic_slice_in_dim(attention_columns, share_start, share_width, 1)
        gains_grad = lax.dynamic_slice_in_dim(gains_sum, share_start, share_width, 1)
        projection_statistics = jnp.stack([output_pair(attention_rows), output_pair(column_share)])
        attention_rows, attention_columns = without_outputs(attention_rows), without_outputs(attention_columns)
    return (
        output,
        input_grad,
        memory_grad,
        attention_grad,
        expand_grad,
        contract_grad,
        gains_grad,
        bucket_grad,
        attention_rows,
        attention_columns,
        expand_rows,
        expand_columns,
        contract_rows,
        contract_columns,
        attention_new,
        expand_new,
        contract_new,
        projection_statistics,
    )


def solution(mesh):
    ring = dict(mesh.shape) == {"wide": 16, "narrow": 2}
    rows, both = P(AXES, None), P(None, AXES, None)
    placed = (rows, rows, P(AXES), P(AXES), both, both, rows, P(None, AXES), P(), rows)
    return jax.shard_map(
        functools.partial(on_device, ring),
        mesh=mesh,
        in_specs=placed,
        out_specs=(
            rows,
            rows,
            rows,
            both,
            both,
            rows,
            P(None, AXES),
            P(),
            P(None, AXES),
            P(),
            P(None, AXES),
            P(),
            P(AXES),
            P(),
            both,
            both,
            rows,
            P(None, None, AXES),
        ),
        check_vma=False,
    )
```

```python
import functools
import math

import jax
import jax.numpy as jnp
import numpy as np
from jax import lax
from jax.experimental import pallas as pl
from jax.experimental.pallas import tpu as pltpu
from jax.sharding import PartitionSpec as P

D = 768
HEADS = 12
FF = 2048
BUCKETS = 32
MAX_DIST = 128
TGT_LEN = 512
MEM_LEN = 512
WIDE = 256
COLS = D // WIDE
BLOCKS = FF // WIDE
PAIRS = HEADS // 2
QROWS = 128
STEP_PAIRS = 3

NEG_FILL = -(2.0**30)
DOCS = 4
FAR_LANE = 8
EPSILON = 1e-06
TINY = 1e-30
STEP_RATE = 0.01
AXES = ("wide", "narrow")
F32 = jnp.float32
BF16 = jnp.bfloat16
MIB = 1024 * 1024
VMEM = pltpu.VMEM


def bucket_onehot(length, bucket_count, far_limit):
    exact_span = bucket_count // 2
    onehot_rows = np.zeros((length, bucket_count), np.float32)
    for distance in range(length):
        if distance < exact_span:
            bucket_id = distance
        else:
            bucket_id = min(
                bucket_count - 1,
                exact_span
                + int(
                    math.log(distance / exact_span)
                    / math.log(far_limit / exact_span)
                    * (bucket_count - exact_span)
                ),
            )
        onehot_rows[distance, bucket_id] = 1.0
    return onehot_rows


def diagonal_onehot():
    t = np.arange(2 * QROWS)
    distance = np.where(t <= QROWS, QROWS - t, 3 * QROWS - t)
    return bucket_onehot(TGT_LEN, BUCKETS, MAX_DIST)[distance]


def tile_onehot():
    t = np.arange(3 * QROWS)
    distance = np.where(t < QROWS, QROWS + t, t - 2 * QROWS)
    rows = bucket_onehot(TGT_LEN, BUCKETS, MAX_DIST)[np.maximum(distance, 0)]
    rows[:, BUCKETS - 1] -= 1.0
    return np.where((distance >= 0)[:, None], rows, 0.0).astype(np.float32)


def mm(left, right):
    return jnp.dot(left, right, preferred_element_type=F32)


def mm_nt(left, right):
    return lax.dot_general(left, right, (((1,), (1,)), ((), ())), preferred_element_type=F32)


def mm_tn(left, right):
    return lax.dot_general(left, right, (((0,), (0,)), ((), ())), preferred_element_type=F32)


def low(values):
    return values.astype(BF16)


def cols(index):
    return slice(index * WIDE, (index + 1) * WIDE)


def inverse_rms(values):
    return lax.rsqrt(jnp.mean(values * values, axis=-1, keepdims=True) + EPSILON)


def norm_back(values, gain, grad):
    scale = inverse_rms(values)
    gain_grad = jnp.sum(values * scale * grad, axis=0, keepdims=True)
    scaled = gain * grad
    inner = jnp.mean(values * scaled, axis=-1, keepdims=True)
    return scale * scaled - values * (scale * scale * scale * inner), gain_grad


def my_index():
    return lax.axis_index("wide") * 2 + lax.axis_index("narrow")


def in_vmem(values):
    return pltpu.with_memory_space_constraint(values, pltpu.VMEM)


RATE = 1.15e9
SCALE = 1.0


def call(body, outs, in_specs, args, us, grid=None, scratch=(), limit=20, out_specs=None, spaces=None):
    kwargs = {} if grid is None else {"grid": grid}
    whole = pl.BlockSpec(memory_space=VMEM)
    spaces = spaces or [jax.ShapeDtypeStruct] * len(outs)
    return pl.pallas_call(
        body,
        out_shape=[space(*o) for space, o in zip(spaces, outs)],
        in_specs=[whole if s is None else s for s in in_specs],
        out_specs=[whole] * len(outs) if out_specs is None else [whole if s is None else s for s in out_specs],
        scratch_shapes=list(scratch),
        compiler_params=pltpu.CompilerParams(vmem_limit_bytes=limit * MIB),
        cost_estimate=pl.CostEstimate(flops=int(us * RATE * SCALE), bytes_accessed=1, transcendentals=0),
        **kwargs,
    )(*args)


def slot_mask(first, slot):
    high, mid, z = slot >> 3, (slot >> 2) & 1, slot & 3
    dy, dx = (high, mid) if first == 0 else (mid, high)
    return z * 8 + dy * 4 + dx


BUFFERS = 4


class Sender:
    def __init__(self, acc, stage=None, sem=None):
        self.acc, self.stage, self.sem = acc, stage, sem
        self.count, self.pending = 0, [[] for _ in range(BUFFERS)]

    def turn(self):
        buffer = self.count % BUFFERS
        self.count += 1
        for copy in self.pending[buffer]:
            copy.wait()
        self.pending[buffer] = []
        return buffer

    def start(self, buffer, source, target):
        index = len(self.pending[buffer])
        copy = pltpu.make_async_copy(source, target, self.sem.at[buffer, index])
        copy.start()
        self.pending[buffer].append(copy)

    def finish(self):
        for pending in self.pending:
            for copy in pending:
                copy.wait()

    def matrix(self, own, sib, first, piece, value):
        buffer = self.turn()
        held = self.acc.at[buffer % self.acc.shape[0]]
        held[...] = value
        me = my_index()
        for index, (out, core) in enumerate(((own, 0), (sib, 2))):
            for slot in range(16):
                owner = lax.bitwise_xor(me, slot_mask(first, slot) + core)
                rows = held[pl.ds(pl.multiple_of(owner * 24, 8), 24), :]
                rows = low(rows.reshape(3, 8, WIDE))
                if self.stage is None:
                    out[slot, piece] = rows
                else:
                    self.stage[buffer, index, slot] = rows
            if self.stage is not None:
                self.start(buffer, self.stage.at[buffer, index], out.at[:, piece])

    def contract(self, outs, column, start, value_of):
        buffer = self.turn()
        me = my_index()
        for index, out in enumerate(outs):
            first, core = index % 2, index // 2 * 2
            for slot in range(16):
                owner = lax.bitwise_xor(me, slot_mask(first, slot) + core)
                rows = value_of(pl.ds(pl.multiple_of(owner * 64 + first * 32, 8), 32))
                self.stage[buffer, index, slot] = low(rows.reshape(4, 8, WIDE))
            self.start(buffer, self.stage.at[buffer, index], out.at[:, pl.ds(start, 4), column])


def send_scratch(ring, staged):
    if not ring:
        return []
    acc = [VMEM((2, D, WIDE), F32)]
    if not staged:
        return acc
    return acc + [VMEM((BUFFERS, 2, 16, 3, 8, WIDE), BF16), pltpu.SemaphoreType.DMA((BUFFERS, 2))]


def grad_shapes(ring, staged, *pieces):
    if not ring:
        return [((sum(pieces), D, WIDE), F32)], [jax.ShapeDtypeStruct], [None]
    shapes = [((16, n, 3, 8, WIDE), BF16) for n in pieces] * 2
    space, spec = (pltpu.HBM, pl.BlockSpec(memory_space=pl.ANY)) if staged else (VMEM, None)
    return shapes, [space] * len(shapes), [spec] * len(shapes)


def pre_kernel(ring, tok, mem, gains_in, w, wm, n1, q, k, v, kc, vc, gains):
    if ring:
        for c in range(COLS):
            gains[:, cols(c)] = jnp.sum(gains_in[0, :, c].astype(F32), axis=0)
    else:
        gains[...] = jnp.concatenate([gains_in[...].astype(F32), jnp.zeros((5, D), F32)], axis=0)
    x = tok[...].astype(F32)
    normed = low(x * inverse_rms(x) * gains[0:1, :])
    n1[...] = normed
    memory = mem[...]
    for c in range(COLS):
        q[:, cols(c)] = low(mm(normed, w[0, c]))
        k[:, cols(c)] = low(mm(normed, w[1, c]))
        v[:, cols(c)] = low(mm(normed, w[2, c]))
        kc[:, cols(c)] = low(mm(memory, wm[5, c]))
        vc[:, cols(c)] = low(mm(memory, wm[6, c]))


def halves(block):
    lane = lax.broadcasted_iota(jnp.int32, block.shape, 1)
    zero = jnp.zeros_like(block)
    return jnp.concatenate([jnp.where(lane < 64, block, zero), jnp.where(lane < 64, zero, block)], axis=0)


def prepare_kernel(target, memory, line, query_mask, self_mask, cross_mask, near):
    document = lax.broadcasted_iota(jnp.int32, (128, target.shape[1]), 0)
    real = document < DOCS
    self_mask[...] = low(jnp.where(real & (document == target[...]), 1.0, 0.0).T)
    cross_mask[...] = low(jnp.where(real & (document == memory[...]), 1.0, 0.0).T)
    other = jnp.where(real & (document != target[...]), NEG_FILL, 0.0).T
    lane = lax.broadcasted_iota(jnp.int32, (QROWS, 128), 1)
    for block in range(TGT_LEN // QROWS):
        for h in range(2):
            rows = other[block * QROWS : (block + 1) * QROWS, :]
            query_mask[block, h * QROWS : (h + 1) * QROWS, :] = low(jnp.where(lane == FAR_LANE + h, 1.0, rows))
    for head in range(HEADS):
        tile = jnp.broadcast_to(line[head : head + 1, :], (2 * QROWS, 3 * QROWS))
        tile = pltpu.roll(tile, 0, 1, stride=1, stride_axis=0)[:, :QROWS]
        near[head // 2, :, (head % 2) * QROWS : (head % 2 + 1) * QROWS] = tile


def add_near(scores, near, pair, block):
    if block == 0:
        return scores + near[pair, QROWS:, :]
    start = scores.shape[0] - 2 * QROWS
    if start == 0:
        return scores + near[pair]
    return jnp.concatenate([scores[:start], scores[start:] + near[pair]], axis=0)


def pair_columns(turned):
    return jnp.concatenate([turned[:64, :QROWS], turned[64:128, QROWS:]], axis=0)


def lanes(pair):
    return slice(pair * 128, (pair + 1) * 128)


def rows_of(block):
    return slice(block * QROWS, (block + 1) * QROWS)


def masked_keys(k, key_mask, far, pair):
    mask = key_mask[...] if far is None else key_mask[...] + far[pair]
    return jnp.concatenate([k[:, lanes(pair)], mask], axis=1)


def ahead(make, items, depth):
    ready = [make(item) for item in items[:depth]]
    for index, item in enumerate(items):
        if index + depth < len(items):
            ready.append(make(items[index + depth]))
        yield item, ready.pop(0)


def with_ones(values):
    turned = values.T
    return jnp.concatenate([turned, jnp.ones((16, turned.shape[1]), turned.dtype)], axis=0)


def attend_forward(q, k, v, near, query_mask, key_mask, far, out, lse):
    keys = [masked_keys(k, key_mask, far, pair) for pair in range(STEP_PAIRS)]
    values_t = [with_ones(v[:, lanes(pair)]) for pair in range(STEP_PAIRS)]
    items = [(pair, block) for pair in range(STEP_PAIRS) for block in range(TGT_LEN // QROWS)]

    def make(item):
        pair, block = item
        end = MEM_LEN if near is None else (block + 1) * QROWS
        queries = jnp.concatenate([halves(q[rows_of(block), lanes(pair)]), query_mask[block]], axis=1)
        return mm_nt(keys[pair][:end], queries)

    for (pair, block), scores in ahead(make, items, 2):
        if near is not None:
            scores = add_near(scores, near, pair, block)
        top = jnp.max(scores, axis=0, keepdims=True)
        raised = low(jnp.exp(scores - top))
        context = mm(values_t[pair][:, : scores.shape[0]], raised)
        sums = context[128:129, :]
        lse[pair, block : block + 1, :] = top + jnp.log(sums)
        context = pair_columns(context * (1.0 / sums))
        out[rows_of(block), lanes(pair)] = low(context.T)


def self_forward_kernel(q, k, v, near, query_mask, key_mask, far, out, lse):
    attend_forward(q, k, v, near, query_mask, key_mask, far, out, lse)


def cross_forward_kernel(q, k, v, query_mask, key_mask, out, lse):
    attend_forward(q, k, v, None, query_mask, key_mask, None, out, lse)


def pair_spec(length):
    return pl.BlockSpec((length, 128 * STEP_PAIRS), lambda p: (0, p))


def step_spec(*dims):
    return pl.BlockSpec((STEP_PAIRS, *dims), lambda p: (p, 0, 0))


NEAR_SPEC = step_spec(2 * QROWS, 2 * QROWS)
LSE_SPEC = step_spec(TGT_LEN // QROWS, 2 * QROWS)
FAR_SPEC = step_spec(1, 128)
FAR_SUM_SPEC = step_spec(8, 2 * QROWS)


def mid_kernel(ctx, tok, gains, w, res, n2, qc):
    context = ctx[...]
    for c in range(COLS):
        res[:, cols(c)] = tok[:, cols(c)].astype(F32) + mm(context, w[3, c])
    x = res[...]
    normed = low(x * inverse_rms(x) * gains[1:2, :])
    n2[...] = normed
    for c in range(COLS):
        qc[:, cols(c)] = low(mm(normed, w[4, c]))


def late_kernel(ctx, res1, gains, w, res2, n3):
    context = ctx[...]
    for c in range(COLS):
        res2[:, cols(c)] = res1[:, cols(c)] + mm(context, w[7, c])
    x = res2[...]
    n3[...] = low(x * inverse_rms(x) * gains[2:3, :])


def gelu_pair(gate):
    rate = math.sqrt(2.0 / math.pi)
    square = gate * gate
    bend = jnp.tanh(rate * gate * (1.0 + 0.044715 * square))
    half = 0.5 * (1.0 + bend)
    slope = half + 0.5 * gate * (1.0 - bend * bend) * rate * (1.0 + 3.0 * 0.044715 * square)
    return gate * half, slope


def ffn_kernel(ring, last, n3, before, dn3_before, hidden_before, cot, wide, narrow, out, dn3, hidden, *rest):
    half = BLOCKS // 2
    if ring:
        grads, rest = rest[:4], rest[4:]
        own_a, own_b, sib_a, sib_b = grads
        sender = Sender(*rest[:3])
    else:
        grads = rest[:3] if last else rest[:2]
    blocks = list(range(half, BLOCKS)) if last else list(range(half))
    normed, turned = n3[...], n3[...].T
    span = slice(blocks[0] * WIDE, (blocks[-1] + 1) * WIDE)

    def make(block):
        rows = slice(block * WIDE, (block + 1) * WIDE)
        back = mm_nt(cot[:, cols(0)], narrow[0, rows, :])
        for c in range(1, COLS):
            back = back + mm_nt(cot[:, cols(c)], narrow[c, rows, :])
        return mm(normed, wide[0, block]), mm(normed, wide[1, block]), back

    for index, (block, (gate, lift, back)) in enumerate(ahead(make, blocks, 1)):
        active, slope = gelu_pair(gate)
        hidden[:, cols(index)] = low(active * lift)
        gate_grad = low(back * lift * slope)
        lift_grad = low(back * active)
        part = mm_nt(gate_grad, wide[0, block]) + mm_nt(lift_grad, wide[1, block])
        if index == 0:
            dn3[...] = dn3_before[...] + part if last else part
        else:
            dn3[...] += part
        if ring:
            sender.matrix(own_a, sib_a, 0, index, mm(turned, gate_grad))
            sender.matrix(own_b, sib_b, 1, index, mm(turned, lift_grad))
        else:
            grads[0][index] = mm(turned, gate_grad)
            grads[1][index] = mm(turned, lift_grad)
    for c in range(COLS):
        total = before[:, cols(c)] + mm(hidden[...], narrow[c, span, :])
        out[:, cols(c)] = low(total) if last else total
    if last:
        con_acc = rest[-2] if ring else rest[-1]
        if ring:
            sender.finish()
            sender = Sender(None, rest[-1], rest[3])
        first_t, last_t = hidden_before[...].T, hidden[...].T
        for c in range(COLS):
            for rows, left in ((slice(0, FF // 2), first_t), (slice(FF // 2, FF), last_t)):
                con_acc[c % 2, rows, :] = mm(left, cot[:, cols(c)])
            if ring:
                sender.contract((own_a, own_b, sib_a, sib_b), c, half, lambda rows, c=c: con_acc[c % 2, rows, :])
            else:
                grads[2][c] = con_acc[c % 2]
    if ring:
        sender.finish()


def third_back_kernel(dn3, res2, cot, gains, w, r2g, ccg, gg):
    back, gain_grad = norm_back(res2[...], gains[2:3, :], dn3[...])
    gg[...] = gain_grad
    grad = cot[...].astype(F32) + back
    r2g[...] = grad
    cross_low = low(grad)
    total = mm_nt(cross_low[:, cols(0)], w[7, 0])
    for c in range(1, COLS):
        total = total + mm_nt(cross_low[:, cols(c)], w[7, c])
    ccg[...] = low(total)


def attend_backward(q, k, v, dc, o, lse, near, query_mask, key_mask, far, dq, dk, dv, dk_acc, dv_acc, near_sum, far_sum):
    keys = [masked_keys(k, key_mask, far, pair) for pair in range(STEP_PAIRS)]
    keys_t = [k[:, lanes(pair)].T for pair in range(STEP_PAIRS)]
    items = [(pair, block) for pair in range(STEP_PAIRS) for block in range(TGT_LEN // QROWS)]

    def make(item):
        pair, block = item
        end = MEM_LEN if near is None else (block + 1) * QROWS
        queries, grads = halves(q[rows_of(block), lanes(pair)]), halves(dc[rows_of(block), lanes(pair)])
        scores = mm_nt(keys[pair][:end], jnp.concatenate([queries, query_mask[block]], axis=1))
        return end, queries, grads, scores, mm_nt(v[:end, lanes(pair)], grads)

    beyond = None
    for (pair, block), (end, queries, grads, scores, prob_grad) in ahead(make, items, 1):
        rows = rows_of(block)
        if near is not None:
            scores = add_near(scores, near, pair, block)
        probs = jnp.exp(scores - lse[pair, block : block + 1, :])
        inner = (dc[rows, lanes(pair)].astype(F32) * o[rows, lanes(pair)].astype(F32)).T
        inner = jnp.concatenate(
            [jnp.sum(inner[:64], axis=0, keepdims=True), jnp.sum(inner[64:], axis=0, keepdims=True)], axis=1
        )
        score_grad = low(probs * (prob_grad - inner))
        dk_part, dv_part = mm(score_grad, queries), mm(low(probs), grads)
        if block == 0:
            dk_acc[:end, :], dv_acc[:end, :] = dk_part, dv_part
        else:
            before = end if near is None else end - QROWS
            dk_acc[:before, :] += dk_part[:before]
            dv_acc[:before, :] += dv_part[:before]
            if before < end:
                dk_acc[before:end, :], dv_acc[before:end, :] = dk_part[before:], dv_part[before:]
        dq[rows, lanes(pair)] = low(pair_columns(mm(keys_t[pair][:, :end], score_grad)).T)
        if near is not None:
            wide = score_grad.astype(F32)
            if block == 0:
                near_sum[pair, :QROWS, :] = jnp.zeros((QROWS, 2 * QROWS), F32)
                near_sum[pair, QROWS:, :] = wide
                beyond = jnp.zeros((1, 2 * QROWS), F32)
            else:
                near_sum[pair] += wide[end - 2 * QROWS :, :]
            if block > 1:
                beyond = beyond + jnp.sum(wide[: end - 2 * QROWS, :], axis=0, keepdims=True)
            far_sum[pair] = jnp.broadcast_to(beyond, (8, 2 * QROWS))
        if block == TGT_LEN // QROWS - 1:
            dk[:, lanes(pair)] = low(dk_acc[...])
            dv[:, lanes(pair)] = low(dv_acc[...])


def cross_back_kernel(q, k, v, dc, o, lse, query_mask, key_mask, dq, dk, dv, dk_acc, dv_acc):
    attend_backward(
        q, k, v, dc, o, lse, None, query_mask, key_mask, None, dq, dk, dv, dk_acc, dv_acc, None, None
    )


def self_back_kernel(
    q, k, v, dc, o, lse, near, query_mask, key_mask, far, dq, dk, dv, near_sum, far_sum, dk_acc, dv_acc
):
    attend_backward(
        q, k, v, dc, o, lse, near, query_mask, key_mask, far, dq, dk, dv, dk_acc, dv_acc, near_sum, far_sum
    )


def diagonal_sums(grid):
    width = 2 * QROWS
    group = grid[:8, :]
    for shift in range(8, QROWS, 8):
        group = group + pltpu.roll(grid[shift : shift + 8, :], width - shift, 1)
    row = lax.broadcasted_iota(jnp.int32, group.shape, 0)
    for bit in (1, 2, 4):
        group = jnp.where((row & bit) != 0, pltpu.roll(group, width - bit, 1), group)
    return jnp.sum(group, axis=0, keepdims=True)


def diagonals_kernel(near_sum, far_sum, diag):
    lane = lax.broadcasted_iota(jnp.int32, (1, 2 * QROWS), 1)
    for pair in range(PAIRS):
        for h in range(2):
            part = slice(h * QROWS, (h + 1) * QROWS)
            beyond = jnp.sum(far_sum[pair, 0:1, part], keepdims=True)
            diag[pair, h : h + 1, :] = diagonal_sums(near_sum[pair, :, part].T) + jnp.where(lane == 0, beyond, 0.0)


def second_back_kernel(dq, res1, r2g, gains, w, r1g, csg, gg):
    query_grad = dq[...]
    back = mm_nt(query_grad[:, cols(0)], w[4, 0])
    for c in range(1, COLS):
        back = back + mm_nt(query_grad[:, cols(c)], w[4, c])
    moved, gain_grad = norm_back(res1[...], gains[1:2, :], back)
    gg[...] = gain_grad
    grad = r2g[...] + moved
    r1g[...] = grad
    self_low = low(grad)
    total = mm_nt(self_low[:, cols(0)], w[3, 0])
    for c in range(1, COLS):
        total = total + mm_nt(self_low[:, cols(c)], w[3, c])
    csg[...] = low(total)


def memory_grads_kernel(ring, dk, dv, mem, w, mg, *rest):
    left = mem[...].T
    pieces = [(matrix * COLS + c, (dk, dv)[matrix], c) for matrix in range(2) for c in range(COLS)]
    put_pieces(ring, rest, [(0, piece, left, right[:, cols(c)]) for piece, right, c in pieces])
    total = mm_nt(dk[:, cols(0)], w[5, 0]) + mm_nt(dv[:, cols(0)], w[6, 0])
    for c in range(1, COLS):
        total = total + mm_nt(dk[:, cols(c)], w[5, c]) + mm_nt(dv[:, cols(c)], w[6, c])
    mg[...] = low(total)


def middle_grads_kernel(ring, dq, n2, r1g, ctxs, r2g, ctxc, *rest):
    pieces = []
    for index, (left, right) in enumerate(((ctxs, low(r1g[...])), (n2, dq[...]), (ctxc, low(r2g[...])))):
        left = left[...].T
        pieces += [(1, index * COLS + c, left, right[:, cols(c)]) for c in range(COLS)]
    put_pieces(ring, rest, pieces)


def put_pieces(ring, rest, pieces):
    if not ring:
        for index, (_, _, left, right) in enumerate(pieces):
            rest[0][index] = mm(left, right)
        return
    refs, sender = rest[:-1], Sender(rest[-1])
    for part, piece, left, right in pieces:
        group = refs[: len(refs) // 2], refs[len(refs) // 2 :]
        out = part if len(refs) == 4 else 0
        sender.matrix(group[0][out], group[1][out], part, piece, mm(left, right))


def first_grads_kernel(ring, dq, dk, dv, n1, *rest):
    left = n1[...].T
    pieces = [(right, c) for right in (dq, dk, dv) for c in range(COLS)]
    put_pieces(
        ring,
        rest,
        [(int(i >= 5), i - 5 if i >= 5 else i, left, right[:, cols(c)]) for i, (right, c) in enumerate(pieces)],
    )


def first_back_kernel(dq, dk, dv, tok, r1g, gains, w, ig, gg):
    back = None
    for matrix, right in enumerate((dq, dk, dv)):
        for c in range(COLS):
            term = mm_nt(right[:, cols(c)], w[matrix, c])
            back = term if back is None else back + term
    moved, gain_grad = norm_back(tok[...].astype(F32), gains[0:1, :], back)
    gg[...] = gain_grad
    ig[...] = low(r1g[...] + moved)


ROW_GAINS, ROW_CONTRACT, ROW_EXPAND, ROW_BUCKETS, SUM_ROWS = 8, 11, 12, 18, 24
RUNS = ((0, D), (D, D), (2 * D, FF - 2 * D))


def squares_of(values):
    return values * values + TINY


def row_line(values):
    squares = squares_of(values)
    width = squares.shape[1]
    part = squares[:, :128]
    for start in range(128, width, 128):
        part = part + squares[:, start : start + 128]
    return jnp.sum(part.T, axis=0, keepdims=True) * (1.0 / width)


def share_kernel(counts, *refs):
    shares, start = [], 0
    for count in counts:
        parts = [ref[0].astype(F32) for ref in refs[start : start + count]]
        start += count
        shares.append((parts[0] + parts[1]) + (parts[2] + parts[3]) if count == 4 else parts[0] + parts[1] + parts[2])
    ffn, cross, own = shares
    gain_one, gain_two, gain_three, diag, onehot, att, exp, con, sums = refs[start:]
    sums[...] = jnp.zeros_like(sums)

    def keep(out, matrix, row, column, piece):
        rows = piece.reshape(24, WIDE)
        out[matrix, :, cols(column)] = rows
        place = column * WIDE
        sums[row + place // D : row + place // D + 1, place % D : place % D + WIDE] = jnp.sum(
            squares_of(rows), axis=0, keepdims=True
        )

    for c in range(COLS):
        for matrix in range(3):
            keep(att, matrix, matrix, c, own[matrix * COLS + c])
        for index, matrix in enumerate((5, 6, 3, 4, 7)):
            keep(att, matrix, matrix, c, cross[index * COLS + c])
        total = jnp.zeros((1, WIDE), F32)
        for octet in range(8):
            rows = ffn[8 + octet if octet < 4 else 16 + octet, c]
            con[octet * 8 : octet * 8 + 8, cols(c)] = rows
            total = total + jnp.sum(squares_of(rows), axis=0, keepdims=True)
        sums[ROW_CONTRACT : ROW_CONTRACT + 1, cols(c)] = total
    for b in range(BLOCKS):
        keep(exp, 0, ROW_EXPAND, b, ffn[b])
        keep(exp, 1, ROW_EXPAND + 3, b, ffn[12 + b])
    for row, gain in enumerate((gain_one, gain_two, gain_three)):
        sums[ROW_GAINS + row : ROW_GAINS + row + 1, :] = gain[...]
    for h in range(2):
        sums[ROW_BUCKETS:SUM_ROWS, h * BUCKETS : (h + 1) * BUCKETS] = jnp.dot(
            diag[:, h, :], onehot[...], precision=lax.Precision.HIGHEST, preferred_element_type=F32
        )


def rows_kernel(att, exp, con, att_rows, exp_rows, con_rows, pair_rows):
    for row, matrix in enumerate((0, 1, 2, 4, 5, 6)):
        att_rows[row : row + 1, :] = row_line(att[matrix])
    for row, matrix in enumerate((3, 7)):
        pair_rows[row : row + 1, :] = row_line(att[matrix])
    for matrix in range(2):
        exp_rows[matrix : matrix + 1, :] = row_line(exp[matrix])
    con_rows[...] = row_line(con[...])


def new_rows(weight, grad, column_stat):
    squares = squares_of(grad)
    row_stat = jnp.mean(squares, axis=-1, keepdims=True)
    scale = jnp.mean(column_stat, axis=-1, keepdims=True)
    second = (row_stat / scale) * column_stat
    return weight.astype(F32) - STEP_RATE * grad * lax.rsqrt(second)


def update_kernel(
    sums, att, exp, con, att_w, exp_w, con_w, att_new, exp_new, con_new, att_cols, exp_cols, con_cols, gains, pair_cols, buckets
):
    me = my_index()
    square = sums[0:8, :] * (1.0 / D)
    for matrix in range(8):
        att_new[matrix] = new_rows(att_w[matrix], att[matrix], square[matrix : matrix + 1, :])
    for row, matrix in enumerate((0, 1, 2, 4, 5, 6)):
        att_cols[row : row + 1, :] = square[matrix : matrix + 1, :]
    for matrix in range(2):
        first = ROW_EXPAND + 3 * matrix
        line = jnp.concatenate([sums[first + i : first + i + 1, :size] for i, (_, size) in enumerate(RUNS)], axis=1)
        line = line * (1.0 / D)
        exp_cols[matrix : matrix + 1, :] = line
        exp_new[matrix] = new_rows(exp_w[matrix], exp[matrix], line)
    line = sums[ROW_CONTRACT : ROW_CONTRACT + 1, :] * (1.0 / FF)
    con_cols[...] = line
    con_new[...] = new_rows(con_w[...], con[...], line)
    shift = lax.rem(D - me * 24, D)
    gains[...] = pltpu.roll(sums[8:16, :], shift, 1)[0:3, :24]
    turned = pltpu.roll(square, shift, 1)
    pair_cols[0:1, :] = turned[3:4, :24]
    pair_cols[1:2, :] = turned[7:8, :24]
    lines = sums[16:24, :128].T
    row = lax.broadcasted_iota(jnp.int32, (8, HEADS), 0)
    column = lax.broadcasted_iota(jnp.int32, (8, HEADS), 1)
    total = jnp.zeros((BUCKETS, HEADS), F32)
    for h in range(2):
        pick = jnp.where(column == 2 * (row - (ROW_BUCKETS - 16)) + h, 1.0, 0.0)
        total = total + jnp.dot(
            lines[h * BUCKETS : (h + 1) * BUCKETS, :],
            pick,
            precision=lax.Precision.HIGHEST,
            preferred_element_type=F32,
        )
    buckets[...] = total


def hop(values, mask):
    return lax.ppermute(values, AXES, [(k, k ^ mask) for k in range(32)])


def after(values, *earlier):
    return lax.optimization_barrier((values,) + earlier)[0]


NEXT_Z = (1, 3, 0, 2)


def ring_hop(values):
    return lax.ppermute(values, AXES, [(k, NEXT_Z[k >> 3] * 8 + (k & 7)) for k in range(32)])


def ring_owner(me, steps, mask):
    z = lax.shift_right_logical(me, 3)
    inner = lax.bitwise_and(lax.bitwise_xor(z, lax.shift_right_logical(z, 1)), 1)
    distance = (0, 2 - inner, 3, 1 + inner)[steps]
    return lax.bitwise_xor(me, distance * 8 + mask)


def place_kernel(plan, targets, count, *refs):
    ins, outs, sem = refs[:count], refs[count:-1], refs[-1]
    me = my_index()
    copies = []
    for ref, (slot, low_piece, high_piece) in zip(ins, plan):
        owner = ring_owner(me, *slot)
        for out, first, last, column in targets:
            begin, end = max(low_piece, first), min(high_piece, last)
            if begin >= end:
                continue
            pieces, into = pl.ds(begin - low_piece, end - begin), pl.ds(begin - first, end - begin)
            if column is None:
                pair = (ref.at[0, pieces], outs[out].at[into, owner])
            else:
                pair = (ref.at[0, pieces, column], outs[out].at[column, owner, into])
            copies.append(pltpu.make_async_copy(*pair, sem.at[len(copies)]))
            copies[-1].start()
    for copy in copies:
        copy.wait()


def place(arrays, outs, targets):
    return call(
        functools.partial(place_kernel, [a[1:] for a in arrays], targets, len(arrays)),
        [(o, BF16) for o in outs],
        [pl.BlockSpec(memory_space=pl.ANY)] * len(arrays),
        [pltpu.with_memory_space_constraint(a[0], pltpu.HBM) for a in arrays],
        4.5,
        scratch=[pltpu.SemaphoreType.DMA((40 * len(targets),))],
        limit=24,
        spaces=[VMEM] * len(outs),
    )


def make_pieces(attention, expand, contract, gains):
    attention_pieces = attention.reshape(8, 24, COLS, WIDE).transpose(0, 2, 1, 3).reshape(24, 3, 8, WIDE)
    line = lax.dynamic_update_slice_in_dim(jnp.zeros((8, D), BF16), jnp.pad(gains, ((0, 5), (0, 0))), my_index() * 24, 1)
    gain_piece = line.reshape(1, 8, COLS, WIDE).transpose(0, 2, 1, 3)
    first = jnp.concatenate([attention_pieces, gain_piece])
    expand_pieces = expand.reshape(2, 24, BLOCKS, WIDE).transpose(0, 2, 1, 3).reshape(2, BLOCKS, 3, 8, WIDE)
    contract_pieces = contract.reshape(8, 8, COLS, WIDE).transpose(0, 2, 1, 3)
    second = jnp.concatenate([expand_pieces.reshape(2 * BLOCKS, 3, 8, WIDE), contract_pieces])
    return jnp.concatenate([first, second])


HALF = 24


def hop_xy(values):
    return hop(values, 1), hop(values, 4)


def corner_hops(by_x, by_y, *earlier):
    half_x, half_y = by_x[:, :HALF], by_y[:, HALF:]
    if earlier:
        half_x, half_y = lax.optimization_barrier((half_x, half_y) + earlier)[:2]
    return hop(half_x, 4), hop(half_y, 1)


def with_core(values, *earlier):
    return values, hop(after(values, *earlier) if earlier else values, 2)


def parts_of(steps, chunk, by_x, by_y, corner_x, corner_y):
    pieces = chunk[0].shape[1]
    plan = []
    for arrays, mask, first, last in (
        (chunk, 0, 0, pieces),
        (by_x, 1, 0, pieces),
        (by_y, 4, 0, pieces),
        (corner_x, 5, 0, HALF),
        (corner_y, 5, HALF, pieces),
    ):
        plan += [(arrays[core], (steps, mask + 2 * core), first, last) for core in range(2)]
    return plan


def place_all(arrays):
    square, gains, wide, narrow = place(
        arrays,
        [(24, 32, 3, 8, WIDE), (1, 32, 3, 8, WIDE), (16, 32, 3, 8, WIDE), (COLS, 32, 8, 8, WIDE)],
        [(0, 0, 24, None), (1, 24, 25, None), (2, 25, 41, None)] + [(3, 41, 49, c) for c in range(COLS)],
    )
    return square.reshape(8, COLS, D, WIDE), gains, wide.reshape(2, BLOCKS, D, WIDE), narrow.reshape(COLS, FF, WIDE)


def gather_plain(attention, expand, contract, gains):
    attention, expand, contract, gains = (
        lax.all_gather(attention, AXES, axis=1, tiled=True),
        lax.all_gather(expand, AXES, axis=1, tiled=True),
        lax.all_gather(contract, AXES, axis=0, tiled=True),
        lax.all_gather(gains, AXES, axis=1, tiled=True),
    )
    return (
        attention.reshape(8, D, COLS, WIDE).transpose(0, 2, 1, 3),
        expand.reshape(2, D, BLOCKS, WIDE).transpose(0, 2, 1, 3),
        contract.reshape(FF, COLS, WIDE).transpose(1, 0, 2),
        gains,
    )


def total(*terms):
    result = terms[0].astype(F32)
    for term in terms[1:]:
        result = result + term.astype(F32)
    return result


class Scatter:
    def __init__(self, grads):
        self.own_a, self.own_b, self.sib_a, self.sib_b = grads

    def core(self, *earlier):
        if earlier:
            self.sib_a, self.sib_b = lax.optimization_barrier((self.sib_a, self.sib_b) + earlier)[:2]
        self.from_a, self.from_b = hop(self.sib_a, 2), hop(self.sib_b, 2)

    def pin(self, earlier):
        if earlier:
            self.own_a, self.own_b = lax.optimization_barrier((self.own_a, self.own_b) + earlier)[:2]

    def first(self, *earlier):
        self.pin(earlier)
        send_a = low(total(self.own_a[8:], self.from_a[8:]))
        send_b = low(total(self.own_b[8:], self.from_b[8:]))
        self.a1, self.b1 = hop(send_a, 4), hop(send_b, 1)
        return send_a, send_b

    def halves(self, part, slots):
        if part == 0:
            return total(self.own_a[slots], self.from_a[slots], self.a1[slots])
        return total(self.own_b[slots], self.from_b[slots], self.b1[slots])


class Finish:
    def __init__(self, groups):
        self.groups = groups

    def second(self, *earlier):
        for group in self.groups:
            group.pin(earlier)
        sends = [
            low(jnp.concatenate([group.halves(part, slice(4, 8)) for group in self.groups], axis=1))
            for part in range(2)
        ]
        self.a2, self.b2 = hop(sends[0], 1), hop(sends[1], 4)
        return tuple(sends)

    def sums(self, slots):
        arrays = []
        for part, last in enumerate((self.a2, self.b2)):
            mine = jnp.concatenate([group.halves(part, slots) for group in self.groups], axis=1)
            arrays.append(mine + last[slots].astype(F32))
        return jnp.concatenate(arrays, axis=1)

    def third(self, *earlier):
        for group in self.groups:
            group.pin(earlier)
        self.mine = self.sums(slice(0, 4))
        send = low(self.mine[1:3])
        self.near = hop(send, 8)
        return (send,)

    def fourth(self, *earlier):
        mine = after(self.mine, *earlier)
        send = low(mine[3:4] + self.near[1:2].astype(F32))
        self.parts = [self.mine, self.near, hop(send, 24)]
        return (send,)

    def third_direct(self, *earlier):
        for group in self.groups:
            group.pin(earlier)
        self.mine = self.sums(slice(0, 4))
        send = low(self.mine)
        self.parts = [self.mine] + [hop(send[d : d + 1], 8 * d) for d in (1, 3, 2)]
        return (send,)


def scatter_plain(pieces, shape, axis):
    count = pieces.shape[0]
    if axis == 0:
        whole = pieces.transpose(1, 0, 2).reshape(shape)
    else:
        per = shape[2] // WIDE
        whole = pieces.reshape(shape[0], per, shape[1], WIDE).transpose(0, 2, 1, 3).reshape(shape)
    return lax.psum_scatter(whole, AXES, scatter_dimension=axis, tiled=True)


def sum_ring(values):
    values = values + hop(values, 2)
    values = (values + hop(values, 1)) + (hop(values, 4) + hop(values, 5))
    return (values + hop(values, 8)) + (hop(values, 16) + hop(values, 24))


def factored_stats(grad_shard, total_rows):
    squares = grad_shard * grad_shard + TINY
    return (jnp.mean(squares, axis=-1), jnp.sum(squares, axis=-2) / total_rows)


def factored_update(weight_shard, grad_shard, row_stat, column_stat):
    scale = jnp.mean(column_stat, axis=-1, keepdims=True)[..., None]
    second = row_stat[..., :, None] * column_stat[..., None, :] / scale
    return weight_shard.astype(F32) - STEP_RATE * grad_shard * lax.rsqrt(second)


def without_outputs(stats):
    return jnp.concatenate([stats[0:3], stats[4:7]], axis=0)


def output_pair(stats):
    return jnp.stack([stats[3], stats[7]])


def on_device(
    ring,
    tokens,
    memory,
    target_segments,
    memory_segments,
    attention_weights,
    expand_weights,
    contract_weights,
    norm_gains,
    bucket_table,
    cotangent,
):
    rows = tokens.shape[0]
    spread_buckets = jnp.asarray(diagonal_onehot())
    lines = jnp.dot(
        bucket_table.T.astype(F32), jnp.asarray(tile_onehot()).T, precision=lax.Precision.HIGHEST
    ) + jnp.where(jnp.arange(3 * QROWS) // QROWS == 1, NEG_FILL, 0.0)
    far = jnp.pad(bucket_table[BUCKETS - 1].reshape(PAIRS, 1, 2), ((0, 0), (0, 0), (FAR_LANE, 126 - FAR_LANE)))
    act, act32 = ((rows, D), BF16), ((rows, D), F32)
    none = [None]
    query_mask, self_mask, cross_mask, near_bias = call(
        prepare_kernel,
        [((rows // QROWS, 2 * QROWS, 128), BF16), ((rows, 128), BF16), ((rows, 128), BF16)]
        + [((PAIRS, 2 * QROWS, 2 * QROWS), F32)],
        none * 3,
        (target_segments.reshape(1, rows), memory_segments.reshape(1, rows), lines),
        0.8,
    )
    pair = pair_spec(rows)
    head_acc = VMEM((rows, 128), F32)

    if ring:
        first = make_pieces(attention_weights, expand_weights, contract_weights, norm_gains)[None]
        r1 = ring_hop(first)
        x0, y0 = hop_xy(first)
        x1, y1 = hop_xy(r1)
        r2 = ring_hop(after(r1, near_bias, x0, y0))
        a0, b0 = corner_hops(x0, y0)
        r3 = ring_hop(r2)
        x2, y2 = hop_xy(after(r2, x1, y1))
        a1, b1 = corner_hops(x1, y1, a0, b0)
        x3, y3 = hop_xy(after(r3, x2, y2))
        a2, b2 = corner_hops(x2, y2, x3)
        a3, b3 = corner_hops(x3, y3)
        parts = []
        for steps, chunk, waits in (
            (0, (first, x0, y0, a0, b0), (x1, y1)),
            (1, (r1, x1, y1, a1, b1), (x2, y2)),
            (2, (r2, x2, y2, a2, b2), (x3, y3)),
            (3, (r3, x3, y3, a3, b3), ()),
        ):
            parts += parts_of(steps, *(with_core(values, *waits) for values in chunk))
        square, gains_in, wide, narrow = place_all(parts)
    else:
        square, wide, narrow, gains_in = gather_plain(
            attention_weights, expand_weights, contract_weights, norm_gains
        )
    if ring:
        square = in_vmem(square)

    n1, q, k, v, kc, vc, gains = call(
        functools.partial(pre_kernel, ring),
        [act] * 6 + [((8, D), F32)],
        none * 5,
        (tokens, memory, gains_in, square, square),
        3.4,
    )
    lse_shape = ((PAIRS, rows // QROWS, 2 * QROWS), F32)
    ctxs, lse_self = call(
        self_forward_kernel,
        [act, lse_shape],
        [pair] * 3 + [NEAR_SPEC, None, None, FAR_SPEC],
        (q, k, v, near_bias, query_mask, self_mask, far),
        5.0,
        grid=(PAIRS // STEP_PAIRS,),
        out_specs=[pair, LSE_SPEC],
    )
    res1, n2, qc = call(
        mid_kernel, [act32, act, act], none * 4, (ctxs, tokens, gains, square), 1.9
    )
    ctxc, lse_cross = call(
        cross_forward_kernel,
        [act, lse_shape],
        [pair] * 3 + [None, None],
        (qc, kc, vc, query_mask, cross_mask),
        5.8,
        grid=(PAIRS // STEP_PAIRS,),
        out_specs=[pair, LSE_SPEC],
    )
    res2, n3 = call(late_kernel, [act32, act], none * 4, (ctxc, res1, gains, square), 1.0)
    if ring:
        wide, narrow = in_vmem(wide), in_vmem(narrow)
    half = BLOCKS // 2
    hidden_shape = ((rows, FF // 2), BF16)
    if ring:
        grad_outs = grad_shapes(ring, True, half, half), grad_shapes(ring, True, half + 4, half + 4)
        more = [VMEM((2, FF, WIDE), F32), VMEM((BUFFERS, 4, 16, 4, 8, WIDE), BF16)], 24
    else:
        grad_outs = [((half, D, WIDE), F32)] * 2
        grad_outs = [
            (outs, [jax.ShapeDtypeStruct] * len(outs), none * len(outs))
            for outs in (grad_outs, grad_outs + [((COLS, FF, WIDE), F32)])
        ]
        more = [VMEM((2, FF, WIDE), F32)], 40
    plain = [jax.ShapeDtypeStruct] * 3
    middle, dn3, hidden, *first_grads = call(
        functools.partial(ffn_kernel, ring, False),
        [act32, act32, hidden_shape] + grad_outs[0][0],
        none * 7,
        (n3, res2, res2, n3, cotangent, wide, narrow),
        8.0,
        scratch=send_scratch(ring, True),
        limit=more[1],
        spaces=plain + grad_outs[0][1],
        out_specs=none * 3 + grad_outs[0][2],
    )
    if ring:
        ffn_one = Scatter(first_grads)
        ffn_one.core()
        middle = after(middle, *ffn_one.first())
    output, dn3, _, *last_grads = call(
        functools.partial(ffn_kernel, ring, True),
        [act, act32, hidden_shape] + grad_outs[1][0],
        none * 7,
        (n3, middle, dn3, hidden, cotangent, wide, narrow),
        13.0,
        scratch=send_scratch(ring, True) + ([pltpu.SemaphoreType.DMA((BUFFERS, 4))] if ring else []) + more[0],
        limit=more[1],
        spaces=plain + grad_outs[1][1],
        out_specs=none * 3 + grad_outs[1][2],
    )
    if ring:
        ffn_two = Scatter(last_grads)
    r2g, ccg, gain_three = call(
        third_back_kernel,
        [act32, act, ((1, D), F32)],
        none * 5,
        (dn3, res2, cotangent, gains, square),
        1.3,
    )
    if ring:
        ffn_two.core(r2g, ffn_one.a1, ffn_one.b1)
        ccg = after(ccg, *ffn_two.first(r2g))
    dqc, dkc, dvc = call(
        cross_back_kernel,
        [act] * 3,
        [pair] * 5 + [LSE_SPEC, None, None],
        (qc, kc, vc, ccg, ctxc, lse_cross, query_mask, cross_mask),
        8.8,
        grid=(PAIRS // STEP_PAIRS,),
        scratch=[head_acc, head_acc],
        out_specs=[pair] * 3,
    )
    shapes = grad_shapes(ring, False, 6)
    memory_grad, *cross_a = call(
        functools.partial(memory_grads_kernel, ring),
        [act] + shapes[0],
        none * 4,
        (dkc, dvc, memory, square),
        3.9,
        scratch=send_scratch(ring, False),
        spaces=plain[:1] + shapes[1],
        out_specs=none + shapes[2],
    )
    dqc = after(dqc, memory_grad)
    r1g, csg, gain_two = call(
        second_back_kernel,
        [act32, act, ((1, D), F32)],
        none * 5,
        (dqc, res1, r2g, gains, square),
        3.0,
    )
    shapes = grad_shapes(ring, False, 9)
    cross_b = call(
        functools.partial(middle_grads_kernel, ring),
        shapes[0],
        none * 6,
        (dqc, n2, r1g, ctxs, r2g, ctxc),
        2.5,
        scratch=send_scratch(ring, False),
        spaces=shapes[1],
        out_specs=shapes[2],
    )
    if ring:
        cross = Scatter([cross_a[0], cross_b[0], cross_a[1], cross_b[1]])
        cross.core(ffn_two.a1, ffn_two.b1)
        ffn, rest = Finish([ffn_one, ffn_two]), Finish([cross])
        csg = after(csg, *ffn.second(cross_b[0]))
    dqs, dks, dvs, near_sum, far_sum = call(
        self_back_kernel,
        [act] * 3 + [((PAIRS, 2 * QROWS, 2 * QROWS), F32), ((PAIRS, 8, 2 * QROWS), F32)],
        [pair] * 5 + [LSE_SPEC, NEAR_SPEC, None, None, FAR_SPEC],
        (q, k, v, csg, ctxs, lse_self, near_bias, query_mask, self_mask, far),
        8.1,
        grid=(PAIRS // STEP_PAIRS,),
        scratch=[head_acc, head_acc],
        out_specs=[pair] * 3 + [NEAR_SPEC, FAR_SUM_SPEC],
    )
    if ring:
        dqs = after(dqs, *cross.first(dqs))
    shapes = grad_shapes(ring, False, 5, 4)
    self_grads = call(
        functools.partial(first_grads_kernel, ring),
        shapes[0],
        none * 4,
        (dqs, dks, dvs, n1),
        2.5,
        scratch=send_scratch(ring, False),
        spaces=shapes[1],
        out_specs=shapes[2],
    )
    if ring:
        own = Scatter(self_grads)
        dks = after(dks, self_grads[0])
    input_grad, gain_one = call(
        first_back_kernel,
        [act, ((1, D), F32)],
        none * 7,
        (dqs, dks, dvs, tokens, r1g, gains, square),
        3.4,
    )
    if ring:
        last = Finish([own])
        own.core(ffn.a2, ffn.b2)
        sent = ffn.third(input_grad)
        sent = own.first(*sent)
        sent = rest.second(*sent)
        sent = ffn.fourth(*sent)
        sent = last.second(*sent)
        sent = rest.third_direct(*sent)
        last.third_direct(*sent)
    diag = call(
        diagonals_kernel,
        [((PAIRS, 2, 2 * QROWS), F32)],
        none * 2,
        (after(near_sum, input_grad), far_sum),
        3.0,
    )[0]
    gain_parts = (gain_one, gain_two, gain_three)
    if ring:
        parts = []
        for group in (ffn, rest, last):
            parts += group.parts
        attention_grad, expand_grad, contract_grad, sums = call(
            functools.partial(share_kernel, [len(group.parts) for group in (ffn, rest, last)]),
            [((8, 24, D), F32), ((2, 24, FF), F32), ((64, D), F32), ((SUM_ROWS, D), F32)],
            none * (len(parts) + 5),
            (*parts, *gain_parts, diag, spread_buckets),
            1.5,
        )
        sums = sum_ring(sums)
        attention_rows, expand_rows, contract_rows, pair_rows = call(
            rows_kernel,
            [((6, 24), F32), ((2, 24), F32), ((1, 64), F32), ((2, 24), F32)],
            none * 3,
            (attention_grad, expand_grad, contract_grad),
            0.8,
        )
        (
            attention_new,
            expand_new,
            contract_new,
            attention_columns,
            expand_columns,
            contract_columns,
            gains_grad,
            pair_columns,
            bucket_grad,
        ) = call(
            update_kernel,
            [
                ((8, 24, D), F32),
                ((2, 24, FF), F32),
                ((64, D), F32),
                ((6, D), F32),
                ((2, FF), F32),
                ((1, D), F32),
                ((3, 24), F32),
                ((2, 24), F32),
                ((BUCKETS, HEADS), F32),
            ],
            none * 7,
            (sums, attention_grad, expand_grad, contract_grad, attention_weights, expand_weights, contract_weights),
            1.4,
        )
        contract_rows, contract_columns = contract_rows.reshape(64), contract_columns.reshape(D)
        projection_statistics = jnp.stack([pair_rows, pair_columns])
    else:
        bucket_part = jnp.dot(
            spread_buckets.T,
            diag.reshape(HEADS, 2 * QROWS).T,
            precision=lax.Precision.HIGHEST,
            preferred_element_type=F32,
        )
        pieces = jnp.concatenate([self_grads[0], cross_b[0][:6], cross_a[0], cross_b[0][6:]])
        attention_grad = scatter_plain(pieces, (8, D, D), 1)
        expand_pieces = jnp.stack([jnp.concatenate([first_grads[i], last_grads[i]]) for i in range(2)])
        expand_grad = scatter_plain(expand_pieces, (2, D, FF), 1)
        contract_grad = scatter_plain(last_grads[2], (FF, D), 0)
        attention_rows, attention_part = factored_stats(attention_grad, D)
        expand_rows, expand_part = factored_stats(expand_grad, D)
        contract_rows, contract_part = factored_stats(contract_grad, FF)
        attention_columns, expand_columns, contract_columns, bucket_grad, gains_sum = lax.psum(
            (attention_part, expand_part, contract_part, bucket_part, jnp.concatenate(gain_parts)), AXES
        )
        attention_new = factored_update(attention_weights, attention_grad, attention_rows, attention_columns)
        expand_new = factored_update(expand_weights, expand_grad, expand_rows, expand_columns)
        contract_new = factored_update(contract_weights, contract_grad, contract_rows, contract_columns)
        share_width = attention_rows.shape[1]
        share_start = lax.axis_index(AXES) * share_width
        column_share = lax.dynamic_slice_in_dim(attention_columns, share_start, share_width, 1)
        gains_grad = lax.dynamic_slice_in_dim(gains_sum, share_start, share_width, 1)
        projection_statistics = jnp.stack([output_pair(attention_rows), output_pair(column_share)])
        attention_rows, attention_columns = without_outputs(attention_rows), without_outputs(attention_columns)
    return (
        output,
        input_grad,
        memory_grad,
        attention_grad,
        expand_grad,
        contract_grad,
        gains_grad,
        bucket_grad,
        attention_rows,
        attention_columns,
        expand_rows,
        expand_columns,
        contract_rows,
        contract_columns,
        attention_new,
        expand_new,
        contract_new,
        projection_statistics,
    )


def solution(mesh):
    ring = dict(mesh.shape) == {"wide": 16, "narrow": 2}
    rows, both = P(AXES, None), P(None, AXES, None)
    placed = (rows, rows, P(AXES), P(AXES), both, both, rows, P(None, AXES), P(), rows)
    return jax.shard_map(
        functools.partial(on_device, ring),
        mesh=mesh,
        in_specs=placed,
        out_specs=(
            rows,
            rows,
            rows,
            both,
            both,
            rows,
            P(None, AXES),
            P(),
            P(None, AXES),
            P(),
            P(None, AXES),
            P(),
            P(AXES),
            P(),
            both,
            both,
            rows,
            P(None, None, AXES),
        ),
        check_vma=False,
    )
```

```python
import functools
import math

import jax
import jax.numpy as jnp
import numpy as np
from jax import lax
from jax.experimental import pallas as pl
from jax.experimental.pallas import tpu as pltpu
from jax.sharding import PartitionSpec as P

D = 768
HEADS = 12
FF = 2048
BUCKETS = 32
MAX_DIST = 128
TGT_LEN = 512
MEM_LEN = 512
WIDE = 256
COLS = D // WIDE
BLOCKS = FF // WIDE
PAIRS = HEADS // 2
QROWS = 128
STEP_PAIRS = 3

NEG_FILL = -(2.0**30)
DOCS = 4
FAR_LANE = 8
EPSILON = 1e-06
TINY = 1e-30
STEP_RATE = 0.01
AXES = ("wide", "narrow")
F32 = jnp.float32
BF16 = jnp.bfloat16
MIB = 1024 * 1024
VMEM = pltpu.VMEM


def bucket_onehot(length, bucket_count, far_limit):
    exact_span = bucket_count // 2
    onehot_rows = np.zeros((length, bucket_count), np.float32)
    for distance in range(length):
        if distance < exact_span:
            bucket_id = distance
        else:
            bucket_id = min(
                bucket_count - 1,
                exact_span
                + int(
                    math.log(distance / exact_span)
                    / math.log(far_limit / exact_span)
                    * (bucket_count - exact_span)
                ),
            )
        onehot_rows[distance, bucket_id] = 1.0
    return onehot_rows


def diagonal_onehot():
    t = np.arange(2 * QROWS)
    distance = np.where(t <= QROWS, QROWS - t, 3 * QROWS - t)
    return bucket_onehot(TGT_LEN, BUCKETS, MAX_DIST)[distance]


def tile_onehot():
    t = np.arange(3 * QROWS)
    distance = np.where(t < QROWS, QROWS + t, t - 2 * QROWS)
    rows = bucket_onehot(TGT_LEN, BUCKETS, MAX_DIST)[np.maximum(distance, 0)]
    rows[:, BUCKETS - 1] -= 1.0
    return np.where((distance >= 0)[:, None], rows, 0.0).astype(np.float32)


def mm(left, right):
    return jnp.dot(left, right, preferred_element_type=F32)


def mm_nt(left, right):
    return lax.dot_general(left, right, (((1,), (1,)), ((), ())), preferred_element_type=F32)


def mm_tn(left, right):
    return lax.dot_general(left, right, (((0,), (0,)), ((), ())), preferred_element_type=F32)


def low(values):
    return values.astype(BF16)


def cols(index):
    return slice(index * WIDE, (index + 1) * WIDE)


def inverse_rms(values):
    return lax.rsqrt(jnp.mean(values * values, axis=-1, keepdims=True) + EPSILON)


def norm_back(values, gain, grad):
    scale = inverse_rms(values)
    gain_grad = jnp.sum(values * scale * grad, axis=0, keepdims=True)
    scaled = gain * grad
    inner = jnp.mean(values * scaled, axis=-1, keepdims=True)
    return scale * scaled - values * (scale * scale * scale * inner), gain_grad


def my_index():
    return lax.axis_index("wide") * 2 + lax.axis_index("narrow")


def in_vmem(values):
    return pltpu.with_memory_space_constraint(values, pltpu.VMEM)


RATE = 1.15e9
SCALE = 1.0


def call(body, outs, in_specs, args, us, grid=None, scratch=(), limit=20, out_specs=None, spaces=None, resident=()):
    kwargs = {} if grid is None else {"grid": grid}
    whole = pl.BlockSpec(memory_space=VMEM)
    count, inner = len(args), body
    if resident:
        args, in_specs = (*args, *resident), [*in_specs, *[None] * len(resident)]
        body = lambda *refs: inner(*refs[:count], *refs[count + len(resident) :])
    spaces = spaces or [jax.ShapeDtypeStruct] * len(outs)
    return pl.pallas_call(
        body,
        out_shape=[space(*o) for space, o in zip(spaces, outs)],
        in_specs=[whole if s is None else s for s in in_specs],
        out_specs=[whole] * len(outs) if out_specs is None else [whole if s is None else s for s in out_specs],
        scratch_shapes=list(scratch),
        compiler_params=pltpu.CompilerParams(vmem_limit_bytes=limit * MIB),
        cost_estimate=pl.CostEstimate(flops=int(us * RATE * SCALE), bytes_accessed=1, transcendentals=0),
        **kwargs,
    )(*args)


def slot_mask(first, slot):
    high, mid, z = slot >> 3, (slot >> 2) & 1, slot & 3
    dy, dx = (high, mid) if first == 0 else (mid, high)
    return z * 8 + dy * 4 + dx


BUFFERS = 4


class Sender:
    def __init__(self, acc, stage=None, sem=None):
        self.acc, self.stage, self.sem = acc, stage, sem
        self.count, self.pending = 0, [[] for _ in range(BUFFERS)]

    def turn(self):
        buffer = self.count % BUFFERS
        self.count += 1
        for copy in self.pending[buffer]:
            copy.wait()
        self.pending[buffer] = []
        return buffer

    def start(self, buffer, source, target):
        index = len(self.pending[buffer])
        copy = pltpu.make_async_copy(source, target, self.sem.at[buffer, index])
        copy.start()
        self.pending[buffer].append(copy)

    def finish(self):
        for pending in self.pending:
            for copy in pending:
                copy.wait()

    def matrix(self, own, sib, first, piece, value):
        buffer = self.turn()
        held = self.acc.at[buffer % self.acc.shape[0]]
        held[...] = value
        me = my_index()
        for index, (out, core) in enumerate(((own, 0), (sib, 2))):
            for slot in range(16):
                owner = lax.bitwise_xor(me, slot_mask(first, slot) + core)
                rows = held[pl.ds(pl.multiple_of(owner * 24, 8), 24), :]
                rows = low(rows.reshape(3, 8, WIDE))
                if self.stage is None:
                    out[slot, piece] = rows
                else:
                    self.stage[buffer, index, slot] = rows
            if self.stage is not None:
                self.start(buffer, self.stage.at[buffer, index], out.at[:, piece])

    def contract(self, outs, column, start, value_of):
        buffer = self.turn()
        me = my_index()
        for index, out in enumerate(outs):
            first, core = index % 2, index // 2 * 2
            for slot in range(16):
                owner = lax.bitwise_xor(me, slot_mask(first, slot) + core)
                rows = value_of(pl.ds(pl.multiple_of(owner * 64 + first * 32, 8), 32))
                out[slot, start : start + 4, column] = low(rows.reshape(4, 8, WIDE))


def send_scratch(ring, staged):
    if not ring:
        return []
    acc = [VMEM((2, D, WIDE), F32)]
    if not staged:
        return acc
    return acc + [VMEM((BUFFERS, 2, 16, 3, 8, WIDE), BF16), pltpu.SemaphoreType.DMA((BUFFERS, 2))]


def grad_shapes(ring, staged, *pieces):
    if not ring:
        return [((sum(pieces), D, WIDE), F32)], [jax.ShapeDtypeStruct], [None]
    shapes = [((16, n, 3, 8, WIDE), BF16) for n in pieces] * 2
    space, spec = (pltpu.HBM, pl.BlockSpec(memory_space=pl.ANY)) if staged else (VMEM, None)
    return shapes, [space] * len(shapes), [spec] * len(shapes)


def pre_kernel(ring, tok, mem, gains_in, w, wm, n1, q, k, v, kc, vc, gains):
    if ring:
        for c in range(COLS):
            gains[:, cols(c)] = jnp.sum(gains_in[0, :, c].astype(F32), axis=0)
    else:
        gains[...] = jnp.concatenate([gains_in[...].astype(F32), jnp.zeros((5, D), F32)], axis=0)
    x = tok[...].astype(F32)
    normed = low(x * inverse_rms(x) * gains[0:1, :])
    n1[...] = normed
    memory = mem[...]
    for c in range(COLS):
        q[:, cols(c)] = low(mm(normed, w[0, c]))
        k[:, cols(c)] = low(mm(normed, w[1, c]))
        v[:, cols(c)] = low(mm(normed, w[2, c]))
        kc[:, cols(c)] = low(mm(memory, wm[5, c]))
        vc[:, cols(c)] = low(mm(memory, wm[6, c]))


def halves(block):
    lane = lax.broadcasted_iota(jnp.int32, block.shape, 1)
    zero = jnp.zeros_like(block)
    return jnp.concatenate([jnp.where(lane < 64, block, zero), jnp.where(lane < 64, zero, block)], axis=0)


def prepare_kernel(target, memory, line, query_mask, self_mask, cross_mask, near):
    document = lax.broadcasted_iota(jnp.int32, (128, target.shape[1]), 0)
    real = document < DOCS
    self_mask[...] = low(jnp.where(real & (document == target[...]), 1.0, 0.0).T)
    cross_mask[...] = low(jnp.where(real & (document == memory[...]), 1.0, 0.0).T)
    other = jnp.where(real & (document != target[...]), NEG_FILL, 0.0).T
    lane = lax.broadcasted_iota(jnp.int32, (QROWS, 128), 1)
    for block in range(TGT_LEN // QROWS):
        for h in range(2):
            rows = other[block * QROWS : (block + 1) * QROWS, :]
            query_mask[block, h * QROWS : (h + 1) * QROWS, :] = low(jnp.where(lane == FAR_LANE + h, 1.0, rows))
    for head in range(HEADS):
        tile = jnp.broadcast_to(line[head : head + 1, :], (2 * QROWS, 3 * QROWS))
        tile = pltpu.roll(tile, 0, 1, stride=1, stride_axis=0)[:, :QROWS]
        near[head // 2, :, (head % 2) * QROWS : (head % 2 + 1) * QROWS] = tile


def add_near(scores, near, pair, block):
    if block == 0:
        return scores + near[pair, QROWS:, :]
    start = scores.shape[0] - 2 * QROWS
    if start == 0:
        return scores + near[pair]
    return jnp.concatenate([scores[:start], scores[start:] + near[pair]], axis=0)


def pair_columns(turned):
    return jnp.concatenate([turned[:64, :QROWS], turned[64:128, QROWS:]], axis=0)


def lanes(pair):
    return slice(pair * 128, (pair + 1) * 128)


def rows_of(block):
    return slice(block * QROWS, (block + 1) * QROWS)


def masked_keys(k, key_mask, far, pair):
    mask = key_mask[...] if far is None else key_mask[...] + far[pair]
    return jnp.concatenate([k[:, lanes(pair)], mask], axis=1)


def ahead(make, items, depth):
    ready = [make(item) for item in items[:depth]]
    for index, item in enumerate(items):
        if index + depth < len(items):
            ready.append(make(items[index + depth]))
        yield item, ready.pop(0)


def with_ones(values):
    turned = values.T
    return jnp.concatenate([turned, jnp.ones((16, turned.shape[1]), turned.dtype)], axis=0)


def attend_forward(q, k, v, near, query_mask, key_mask, far, out, lse):
    keys = [masked_keys(k, key_mask, far, pair) for pair in range(STEP_PAIRS)]
    values_t = [with_ones(v[:, lanes(pair)]) for pair in range(STEP_PAIRS)]
    items = [(pair, block) for pair in range(STEP_PAIRS) for block in range(TGT_LEN // QROWS)]

    def make(item):
        pair, block = item
        end = MEM_LEN if near is None else (block + 1) * QROWS
        queries = jnp.concatenate([halves(q[rows_of(block), lanes(pair)]), query_mask[block]], axis=1)
        return mm_nt(keys[pair][:end], queries)

    for (pair, block), scores in ahead(make, items, 2):
        if near is not None:
            scores = add_near(scores, near, pair, block)
        top = jnp.max(scores, axis=0, keepdims=True)
        raised = low(jnp.exp(scores - top))
        context = mm(values_t[pair][:, : scores.shape[0]], raised)
        sums = context[128:129, :]
        lse[pair, block : block + 1, :] = top + jnp.log(sums)
        context = pair_columns(context * (1.0 / sums))
        out[rows_of(block), lanes(pair)] = low(context.T)


def self_forward_kernel(copies, count, q, k, v, near, query_mask, key_mask, far, *rest):
    out, lse = rest[count : count + 2]
    if copies is not None:
        started = copies(rest[:count], rest[count + 2 : -1], rest[-1])

        @pl.when(pl.program_id(0) == 0)
        def _():
            for copy in started:
                copy.start()

    attend_forward(q, k, v, near, query_mask, key_mask, far, out, lse)
    if copies is not None:

        @pl.when(pl.program_id(0) == pl.num_programs(0) - 1)
        def _():
            for copy in started:
                copy.wait()


def cross_forward_kernel(q, k, v, query_mask, key_mask, out, lse):
    attend_forward(q, k, v, None, query_mask, key_mask, None, out, lse)


def pair_spec(length):
    return pl.BlockSpec((length, 128 * STEP_PAIRS), lambda p: (0, p))


def step_spec(*dims):
    return pl.BlockSpec((STEP_PAIRS, *dims), lambda p: (p, 0, 0))


NEAR_SPEC = step_spec(2 * QROWS, 2 * QROWS)
LSE_SPEC = step_spec(TGT_LEN // QROWS, 2 * QROWS)
FAR_SPEC = step_spec(1, 128)
FAR_SUM_SPEC = step_spec(8, 2 * QROWS)


def mid_kernel(ctx, tok, gains, w, res, n2, qc):
    context = ctx[...]
    for c in range(COLS):
        res[:, cols(c)] = tok[:, cols(c)].astype(F32) + mm(context, w[3, c])
    x = res[...]
    normed = low(x * inverse_rms(x) * gains[1:2, :])
    n2[...] = normed
    for c in range(COLS):
        qc[:, cols(c)] = low(mm(normed, w[4, c]))


def late_kernel(ctx, res1, gains, w, res2, n3):
    context = ctx[...]
    for c in range(COLS):
        res2[:, cols(c)] = res1[:, cols(c)] + mm(context, w[7, c])
    x = res2[...]
    n3[...] = low(x * inverse_rms(x) * gains[2:3, :])


def gelu_pair(gate):
    rate = math.sqrt(2.0 / math.pi)
    square = gate * gate
    bend = jnp.tanh(rate * gate * (1.0 + 0.044715 * square))
    half = 0.5 * (1.0 + bend)
    slope = half + 0.5 * gate * (1.0 - bend * bend) * rate * (1.0 + 3.0 * 0.044715 * square)
    return gate * half, slope


def ffn_kernel(ring, last, n3, before, dn3_before, hidden_before, cot, wide, narrow, out, dn3, hidden, *rest):
    half = BLOCKS // 2
    if ring:
        grads, rest = rest[:4], rest[4:]
        own_a, own_b, sib_a, sib_b = grads
        sender = Sender(rest[0])
    else:
        grads = rest[:3] if last else rest[:2]
    blocks = list(range(half, BLOCKS)) if last else list(range(half))
    normed, turned = n3[...], n3[...].T
    span = slice(blocks[0] * WIDE, (blocks[-1] + 1) * WIDE)

    def make(block):
        rows = slice(block * WIDE, (block + 1) * WIDE)
        back = mm_nt(cot[:, cols(0)], narrow[0, rows, :])
        for c in range(1, COLS):
            back = back + mm_nt(cot[:, cols(c)], narrow[c, rows, :])
        return mm(normed, wide[0, block]), mm(normed, wide[1, block]), back

    for index, (block, (gate, lift, back)) in enumerate(ahead(make, blocks, 1)):
        active, slope = gelu_pair(gate)
        hidden[:, cols(index)] = low(active * lift)
        gate_grad = low(back * lift * slope)
        lift_grad = low(back * active)
        part = mm_nt(gate_grad, wide[0, block]) + mm_nt(lift_grad, wide[1, block])
        if index == 0:
            dn3[...] = dn3_before[...] + part if last else part
        else:
            dn3[...] += part
        if ring:
            sender.matrix(own_a, sib_a, 0, index, mm(turned, gate_grad))
            sender.matrix(own_b, sib_b, 1, index, mm(turned, lift_grad))
        else:
            grads[0][index] = mm(turned, gate_grad)
            grads[1][index] = mm(turned, lift_grad)
    for c in range(COLS):
        total = before[:, cols(c)] + mm(hidden[...], narrow[c, span, :])
        out[:, cols(c)] = low(total) if last else total
    if last:
        con_acc = rest[-1]
        first_t, last_t = hidden_before[...].T, hidden[...].T
        for c in range(COLS):
            for rows, left in ((slice(0, FF // 2), first_t), (slice(FF // 2, FF), last_t)):
                con_acc[c % 2, rows, :] = mm(left, cot[:, cols(c)])
            if ring:
                sender.contract((own_a, own_b, sib_a, sib_b), c, half, lambda rows, c=c: con_acc[c % 2, rows, :])
            else:
                grads[2][c] = con_acc[c % 2]
    if ring:
        sender.finish()


def third_back_kernel(dn3, res2, cot, gains, w, r2g, ccg, gg):
    back, gain_grad = norm_back(res2[...], gains[2:3, :], dn3[...])
    gg[...] = gain_grad
    grad = cot[...].astype(F32) + back
    r2g[...] = grad
    cross_low = low(grad)
    total = mm_nt(cross_low[:, cols(0)], w[7, 0])
    for c in range(1, COLS):
        total = total + mm_nt(cross_low[:, cols(c)], w[7, c])
    ccg[...] = low(total)


def attend_backward(q, k, v, dc, o, lse, near, query_mask, key_mask, far, dq, dk, dv, dk_acc, dv_acc, near_sum, far_sum):
    keys = [masked_keys(k, key_mask, far, pair) for pair in range(STEP_PAIRS)]
    keys_t = [k[:, lanes(pair)].T for pair in range(STEP_PAIRS)]
    items = [(pair, block) for pair in range(STEP_PAIRS) for block in range(TGT_LEN // QROWS)]

    def make(item):
        pair, block = item
        end = MEM_LEN if near is None else (block + 1) * QROWS
        queries, grads = halves(q[rows_of(block), lanes(pair)]), halves(dc[rows_of(block), lanes(pair)])
        scores = mm_nt(keys[pair][:end], jnp.concatenate([queries, query_mask[block]], axis=1))
        return end, queries, grads, scores, mm_nt(v[:end, lanes(pair)], grads)

    beyond = None
    for (pair, block), (end, queries, grads, scores, prob_grad) in ahead(make, items, 1):
        rows = rows_of(block)
        if near is not None:
            scores = add_near(scores, near, pair, block)
        probs = jnp.exp(scores - lse[pair, block : block + 1, :])
        inner = (dc[rows, lanes(pair)].astype(F32) * o[rows, lanes(pair)].astype(F32)).T
        inner = jnp.concatenate(
            [jnp.sum(inner[:64], axis=0, keepdims=True), jnp.sum(inner[64:], axis=0, keepdims=True)], axis=1
        )
        score_grad = low(probs * (prob_grad - inner))
        dk_part, dv_part = mm(score_grad, queries), mm(low(probs), grads)
        if block == 0:
            dk_acc[:end, :], dv_acc[:end, :] = dk_part, dv_part
        else:
            before = end if near is None else end - QROWS
            dk_acc[:before, :] += dk_part[:before]
            dv_acc[:before, :] += dv_part[:before]
            if before < end:
                dk_acc[before:end, :], dv_acc[before:end, :] = dk_part[before:], dv_part[before:]
        dq[rows, lanes(pair)] = low(pair_columns(mm(keys_t[pair][:, :end], score_grad)).T)
        if near is not None:
            wide = score_grad.astype(F32)
            if block == 0:
                near_sum[pair, :QROWS, :] = jnp.zeros((QROWS, 2 * QROWS), F32)
                near_sum[pair, QROWS:, :] = wide
                beyond = jnp.zeros((1, 2 * QROWS), F32)
            else:
                near_sum[pair] += wide[end - 2 * QROWS :, :]
            if block > 1:
                beyond = beyond + jnp.sum(wide[: end - 2 * QROWS, :], axis=0, keepdims=True)
            far_sum[pair] = jnp.broadcast_to(beyond, (8, 2 * QROWS))
        if block == TGT_LEN // QROWS - 1:
            dk[:, lanes(pair)] = low(dk_acc[...])
            dv[:, lanes(pair)] = low(dv_acc[...])


def cross_back_kernel(q, k, v, dc, o, lse, query_mask, key_mask, dq, dk, dv, dk_acc, dv_acc):
    attend_backward(
        q, k, v, dc, o, lse, None, query_mask, key_mask, None, dq, dk, dv, dk_acc, dv_acc, None, None
    )


def self_back_kernel(
    q, k, v, dc, o, lse, near, query_mask, key_mask, far, dq, dk, dv, near_sum, far_sum, dk_acc, dv_acc
):
    attend_backward(
        q, k, v, dc, o, lse, near, query_mask, key_mask, far, dq, dk, dv, dk_acc, dv_acc, near_sum, far_sum
    )


def diagonal_sums(grid):
    width = 2 * QROWS
    group = grid[:8, :]
    for shift in range(8, QROWS, 8):
        group = group + pltpu.roll(grid[shift : shift + 8, :], width - shift, 1)
    row = lax.broadcasted_iota(jnp.int32, group.shape, 0)
    for bit in (1, 2, 4):
        group = jnp.where((row & bit) != 0, pltpu.roll(group, width - bit, 1), group)
    return jnp.sum(group, axis=0, keepdims=True)


def diagonals_kernel(near_sum, far_sum, diag):
    lane = lax.broadcasted_iota(jnp.int32, (1, 2 * QROWS), 1)
    for pair in range(PAIRS):
        for h in range(2):
            part = slice(h * QROWS, (h + 1) * QROWS)
            beyond = jnp.sum(far_sum[pair, 0:1, part], keepdims=True)
            diag[pair, h : h + 1, :] = diagonal_sums(near_sum[pair, :, part].T) + jnp.where(lane == 0, beyond, 0.0)


def second_back_kernel(dq, res1, r2g, gains, w, r1g, csg, gg):
    query_grad = dq[...]
    back = mm_nt(query_grad[:, cols(0)], w[4, 0])
    for c in range(1, COLS):
        back = back + mm_nt(query_grad[:, cols(c)], w[4, c])
    moved, gain_grad = norm_back(res1[...], gains[1:2, :], back)
    gg[...] = gain_grad
    grad = r2g[...] + moved
    r1g[...] = grad
    self_low = low(grad)
    total = mm_nt(self_low[:, cols(0)], w[3, 0])
    for c in range(1, COLS):
        total = total + mm_nt(self_low[:, cols(c)], w[3, c])
    csg[...] = low(total)


def memory_grads_kernel(ring, dk, dv, mem, w, mg, *rest):
    left = mem[...].T
    pieces = [(matrix * COLS + c, (dk, dv)[matrix], c) for matrix in range(2) for c in range(COLS)]
    put_pieces(ring, rest, [(0, piece, left, right[:, cols(c)]) for piece, right, c in pieces])
    total = mm_nt(dk[:, cols(0)], w[5, 0]) + mm_nt(dv[:, cols(0)], w[6, 0])
    for c in range(1, COLS):
        total = total + mm_nt(dk[:, cols(c)], w[5, c]) + mm_nt(dv[:, cols(c)], w[6, c])
    mg[...] = low(total)


def middle_grads_kernel(ring, dq, n2, r1g, ctxs, r2g, ctxc, *rest):
    pieces = []
    for index, (left, right) in enumerate(((ctxs, low(r1g[...])), (n2, dq[...]), (ctxc, low(r2g[...])))):
        left = left[...].T
        pieces += [(1, index * COLS + c, left, right[:, cols(c)]) for c in range(COLS)]
    put_pieces(ring, rest, pieces)


def put_pieces(ring, rest, pieces):
    if not ring:
        for index, (_, _, left, right) in enumerate(pieces):
            rest[0][index] = mm(left, right)
        return
    refs, sender = rest[:-1], Sender(rest[-1])
    for part, piece, left, right in pieces:
        group = refs[: len(refs) // 2], refs[len(refs) // 2 :]
        out = part if len(refs) == 4 else 0
        sender.matrix(group[0][out], group[1][out], part, piece, mm(left, right))


def first_grads_kernel(ring, dq, dk, dv, n1, *rest):
    left = n1[...].T
    pieces = [(right, c) for right in (dq, dk, dv) for c in range(COLS)]
    put_pieces(
        ring,
        rest,
        [(int(i >= 5), i - 5 if i >= 5 else i, left, right[:, cols(c)]) for i, (right, c) in enumerate(pieces)],
    )


def first_back_kernel(dq, dk, dv, tok, r1g, gains, w, ig, gg):
    back = None
    for matrix, right in enumerate((dq, dk, dv)):
        for c in range(COLS):
            term = mm_nt(right[:, cols(c)], w[matrix, c])
            back = term if back is None else back + term
    moved, gain_grad = norm_back(tok[...].astype(F32), gains[0:1, :], back)
    gg[...] = gain_grad
    ig[...] = low(r1g[...] + moved)


ROW_GAINS, ROW_CONTRACT, ROW_EXPAND, ROW_BUCKETS, SUM_ROWS = 8, 11, 12, 18, 24
RUNS = ((0, D), (D, D), (2 * D, FF - 2 * D))


def squares_of(values):
    return values * values + TINY


def row_line(values):
    squares = squares_of(values)
    width = squares.shape[1]
    part = squares[:, :128]
    for start in range(128, width, 128):
        part = part + squares[:, start : start + 128]
    return jnp.sum(part.T, axis=0, keepdims=True) * (1.0 / width)


def share_kernel(counts, *refs):
    shares, start = [], 0
    for count in counts:
        parts = [ref[0].astype(F32) for ref in refs[start : start + count]]
        start += count
        shares.append((parts[0] + parts[1]) + (parts[2] + parts[3]) if count == 4 else parts[0] + parts[1] + parts[2])
    one, two, cross, own = shares
    gate = [one[b] if b < 4 else two[b - 4] for b in range(BLOCKS)]
    lift = [one[4 + b] if b < 4 else two[4 + b] for b in range(BLOCKS)]
    gain_one, gain_two, gain_three, diag, onehot, att, exp, con, sums = refs[start:]
    sums[...] = jnp.zeros_like(sums)

    def keep(out, matrix, row, column, piece):
        rows = piece.reshape(24, WIDE)
        out[matrix, :, cols(column)] = rows
        place = column * WIDE
        sums[row + place // D : row + place // D + 1, place % D : place % D + WIDE] = jnp.sum(
            squares_of(rows), axis=0, keepdims=True
        )

    for c in range(COLS):
        for matrix in range(3):
            keep(att, matrix, matrix, c, own[matrix * COLS + c])
        for index, matrix in enumerate((5, 6, 3, 4, 7)):
            keep(att, matrix, matrix, c, cross[index * COLS + c])
        total = jnp.zeros((1, WIDE), F32)
        for octet in range(8):
            rows = two[4 + octet if octet < 4 else 8 + octet, c]
            con[octet * 8 : octet * 8 + 8, cols(c)] = rows
            total = total + jnp.sum(squares_of(rows), axis=0, keepdims=True)
        sums[ROW_CONTRACT : ROW_CONTRACT + 1, cols(c)] = total
    for b in range(BLOCKS):
        keep(exp, 0, ROW_EXPAND, b, gate[b])
        keep(exp, 1, ROW_EXPAND + 3, b, lift[b])
    for row, gain in enumerate((gain_one, gain_two, gain_three)):
        sums[ROW_GAINS + row : ROW_GAINS + row + 1, :] = gain[...]
    for h in range(2):
        sums[ROW_BUCKETS:SUM_ROWS, h * BUCKETS : (h + 1) * BUCKETS] = jnp.dot(
            diag[:, h, :], onehot[...], precision=lax.Precision.HIGHEST, preferred_element_type=F32
        )


def rows_kernel(att, exp, con, att_rows, exp_rows, con_rows, pair_rows):
    for row, matrix in enumerate((0, 1, 2, 4, 5, 6)):
        att_rows[row : row + 1, :] = row_line(att[matrix])
    for row, matrix in enumerate((3, 7)):
        pair_rows[row : row + 1, :] = row_line(att[matrix])
    for matrix in range(2):
        exp_rows[matrix : matrix + 1, :] = row_line(exp[matrix])
    con_rows[...] = row_line(con[...])


def new_rows(weight, grad, column_stat):
    squares = squares_of(grad)
    row_stat = jnp.mean(squares, axis=-1, keepdims=True)
    scale = jnp.mean(column_stat, axis=-1, keepdims=True)
    second = (row_stat / scale) * column_stat
    return weight.astype(F32) - STEP_RATE * grad * lax.rsqrt(second)


def update_kernel(
    sums, pair_rows, att, exp, con, att_w, exp_w, con_w, att_new, exp_new, con_new, att_cols, exp_cols, con_cols, gains, pairs, buckets
):
    me = my_index()
    square = sums[0:8, :] * (1.0 / D)
    for matrix in range(8):
        att_new[matrix] = new_rows(att_w[matrix], att[matrix], square[matrix : matrix + 1, :])
    for row, matrix in enumerate((0, 1, 2, 4, 5, 6)):
        att_cols[row : row + 1, :] = square[matrix : matrix + 1, :]
    for matrix in range(2):
        first = ROW_EXPAND + 3 * matrix
        line = jnp.concatenate([sums[first + i : first + i + 1, :size] for i, (_, size) in enumerate(RUNS)], axis=1)
        line = line * (1.0 / D)
        exp_cols[matrix : matrix + 1, :] = line
        exp_new[matrix] = new_rows(exp_w[matrix], exp[matrix], line)
    line = sums[ROW_CONTRACT : ROW_CONTRACT + 1, :] * (1.0 / FF)
    con_cols[...] = line
    con_new[...] = new_rows(con_w[...], con[...], line)
    shift = lax.rem(D - me * 24, D)
    gains[...] = pltpu.roll(sums[8:16, :], shift, 1)[0:3, :24]
    turned = pltpu.roll(square, shift, 1)
    pairs[0] = pair_rows[...]
    pairs[1, 0:1, :] = turned[3:4, :24]
    pairs[1, 1:2, :] = turned[7:8, :24]
    lines = sums[16:24, :128].T
    row = lax.broadcasted_iota(jnp.int32, (8, HEADS), 0)
    column = lax.broadcasted_iota(jnp.int32, (8, HEADS), 1)
    total = jnp.zeros((BUCKETS, HEADS), F32)
    for h in range(2):
        pick = jnp.where(column == 2 * (row - (ROW_BUCKETS - 16)) + h, 1.0, 0.0)
        total = total + jnp.dot(
            lines[h * BUCKETS : (h + 1) * BUCKETS, :],
            pick,
            precision=lax.Precision.HIGHEST,
            preferred_element_type=F32,
        )
    buckets[...] = total


def hop(values, mask):
    return lax.ppermute(values, AXES, [(k, k ^ mask) for k in range(32)])


def after(values, *earlier):
    return lax.optimization_barrier((values,) + earlier)[0]


NEXT_Z = (1, 3, 0, 2)


def ring_hop(values):
    return lax.ppermute(values, AXES, [(k, NEXT_Z[k >> 3] * 8 + (k & 7)) for k in range(32)])


def ring_owner(me, steps, mask):
    z = lax.shift_right_logical(me, 3)
    inner = lax.bitwise_and(lax.bitwise_xor(z, lax.shift_right_logical(z, 1)), 1)
    distance = (0, 2 - inner, 3, 1 + inner)[steps]
    return lax.bitwise_xor(me, distance * 8 + mask)


def place_copies(plan, targets, ins, outs, sem):
    me = my_index()
    copies = []
    for ref, (slot, low_piece, high_piece) in zip(ins, plan):
        owner = ring_owner(me, *slot)
        for out, first, last, column in targets:
            begin, end = max(low_piece, first), min(high_piece, last)
            if begin >= end:
                continue
            pieces, into = pl.ds(begin - low_piece, end - begin), pl.ds(begin - first, end - begin)
            if column is None:
                pair = (ref.at[0, pieces], outs[out].at[into, owner])
            else:
                pair = (ref.at[0, pieces, column], outs[out].at[column, owner, into])
            copies.append(pltpu.make_async_copy(*pair, sem.at[len(copies)]))
    return copies


def place_kernel(plan, targets, count, *refs):
    copies = place_copies(plan, targets, refs[:count], refs[count:-1], refs[-1])
    for copy in copies:
        copy.start()
    for copy in copies:
        copy.wait()


def place(arrays, outs, targets):
    return call(
        functools.partial(place_kernel, [a[1:] for a in arrays], targets, len(arrays)),
        [(o, BF16) for o in outs],
        [pl.BlockSpec(memory_space=pl.ANY)] * len(arrays),
        [pltpu.with_memory_space_constraint(a[0], pltpu.HBM) for a in arrays],
        4.5,
        scratch=[pltpu.SemaphoreType.DMA((40 * len(targets),))],
        limit=24,
        spaces=[VMEM] * len(outs),
    )


def make_pieces(attention, expand, contract, gains):
    attention_pieces = attention.reshape(8, 24, COLS, WIDE).transpose(0, 2, 1, 3).reshape(24, 3, 8, WIDE)
    line = lax.dynamic_update_slice_in_dim(jnp.zeros((8, D), BF16), jnp.pad(gains, ((0, 5), (0, 0))), my_index() * 24, 1)
    gain_piece = line.reshape(1, 8, COLS, WIDE).transpose(0, 2, 1, 3)
    first = jnp.concatenate([attention_pieces, gain_piece])
    expand_pieces = expand.reshape(2, 24, BLOCKS, WIDE).transpose(0, 2, 1, 3).reshape(2, BLOCKS, 3, 8, WIDE)
    contract_pieces = contract.reshape(8, 8, COLS, WIDE).transpose(0, 2, 1, 3)
    second = jnp.concatenate([expand_pieces.reshape(2 * BLOCKS, 3, 8, WIDE), contract_pieces])
    return jnp.concatenate([first, second])


HALF = 24


def hop_xy(values):
    return hop(values, 1), hop(values, 4)


def corner_hops(by_x, by_y, *earlier):
    half_x, half_y = by_x[:, :HALF], by_y[:, HALF:]
    if earlier:
        half_x, half_y = lax.optimization_barrier((half_x, half_y) + earlier)[:2]
    return hop(half_x, 4), hop(half_y, 1)


def with_core(values, *earlier):
    return values, hop(after(values, *earlier) if earlier else values, 2)


def parts_of(steps, chunk, by_x, by_y, corner_x, corner_y):
    pieces = chunk[0].shape[1]
    plan = []
    for arrays, mask, first, last in (
        (chunk, 0, 0, pieces),
        (by_x, 1, 0, pieces),
        (by_y, 4, 0, pieces),
        (corner_x, 5, 0, HALF),
        (corner_y, 5, HALF, pieces),
    ):
        plan += [(arrays[core], (steps, mask + 2 * core), first, last) for core in range(2)]
    return plan


WIDE_SHAPES = [((16, 32, 3, 8, WIDE), BF16), ((COLS, 32, 8, 8, WIDE), BF16)]
WIDE_TARGETS = [(0, 25, 41, None)] + [(1, 41, 49, c) for c in range(COLS)]


def overlapping(arrays, first):
    return [a for a in arrays if a[3] > first]


def place_square(arrays):
    square, gains = place(
        [a for a in arrays if a[2] < 25],
        [(24, 32, 3, 8, WIDE), (1, 32, 3, 8, WIDE)],
        [(0, 0, 24, None), (1, 24, 25, None)],
    )
    return square.reshape(8, COLS, D, WIDE), gains


def gather_plain(attention, expand, contract, gains):
    attention, expand, contract, gains = (
        lax.all_gather(attention, AXES, axis=1, tiled=True),
        lax.all_gather(expand, AXES, axis=1, tiled=True),
        lax.all_gather(contract, AXES, axis=0, tiled=True),
        lax.all_gather(gains, AXES, axis=1, tiled=True),
    )
    return (
        attention.reshape(8, D, COLS, WIDE).transpose(0, 2, 1, 3),
        expand.reshape(2, D, BLOCKS, WIDE).transpose(0, 2, 1, 3),
        contract.reshape(FF, COLS, WIDE).transpose(1, 0, 2),
        gains,
    )


def total(*terms):
    result = terms[0].astype(F32)
    for term in terms[1:]:
        result = result + term.astype(F32)
    return result


class Scatter:
    def __init__(self, grads):
        self.own_a, self.own_b, self.sib_a, self.sib_b = grads

    def core(self, *earlier):
        if earlier:
            self.sib_a, self.sib_b = lax.optimization_barrier((self.sib_a, self.sib_b) + earlier)[:2]
        self.from_a, self.from_b = hop(self.sib_a, 2), hop(self.sib_b, 2)

    def pin(self, earlier):
        if earlier:
            self.own_a, self.own_b = lax.optimization_barrier((self.own_a, self.own_b) + earlier)[:2]

    def first(self, *earlier):
        self.pin(earlier)
        send_a = low(total(self.own_a[8:], self.from_a[8:]))
        send_b = low(total(self.own_b[8:], self.from_b[8:]))
        self.a1, self.b1 = hop(send_a, 4), hop(send_b, 1)
        return send_a, send_b

    def halves(self, part, slots):
        if part == 0:
            return total(self.own_a[slots], self.from_a[slots], self.a1[slots])
        return total(self.own_b[slots], self.from_b[slots], self.b1[slots])


class Finish:
    def __init__(self, groups):
        self.groups = groups

    def second(self, *earlier):
        for group in self.groups:
            group.pin(earlier)
        sends = [
            low(jnp.concatenate([group.halves(part, slice(4, 8)) for group in self.groups], axis=1))
            for part in range(2)
        ]
        self.a2, self.b2 = hop(sends[0], 1), hop(sends[1], 4)
        return tuple(sends)

    def sums(self, slots):
        arrays = []
        for part, last in enumerate((self.a2, self.b2)):
            mine = jnp.concatenate([group.halves(part, slots) for group in self.groups], axis=1)
            arrays.append(mine + last[slots].astype(F32))
        return jnp.concatenate(arrays, axis=1)

    def third(self, *earlier):
        for group in self.groups:
            group.pin(earlier)
        self.mine = self.sums(slice(0, 4))
        send = low(self.mine[1:3])
        self.near = hop(send, 8)
        return (send,)

    def fourth(self, *earlier):
        mine = after(self.mine, *earlier)
        send = low(mine[3:4] + self.near[1:2].astype(F32))
        self.parts = [self.mine, self.near, hop(send, 24)]
        return (send,)

    def third_direct(self, *earlier):
        for group in self.groups:
            group.pin(earlier)
        self.mine = self.sums(slice(0, 4))
        send = low(self.mine)
        self.parts = [self.mine] + [hop(send[d : d + 1], 8 * d) for d in (1, 3, 2)]
        return (send,)


def scatter_plain(pieces, shape, axis):
    count = pieces.shape[0]
    if axis == 0:
        whole = pieces.transpose(1, 0, 2).reshape(shape)
    else:
        per = shape[2] // WIDE
        whole = pieces.reshape(shape[0], per, shape[1], WIDE).transpose(0, 2, 1, 3).reshape(shape)
    return lax.psum_scatter(whole, AXES, scatter_dimension=axis, tiled=True)


def sum_ring(values):
    values = values + hop(values, 2)
    values = (values + hop(values, 1)) + (hop(values, 4) + hop(values, 5))
    return (values + hop(values, 8)) + (hop(values, 16) + hop(values, 24))


def factored_stats(grad_shard, total_rows):
    squares = grad_shard * grad_shard + TINY
    return (jnp.mean(squares, axis=-1), jnp.sum(squares, axis=-2) / total_rows)


def factored_update(weight_shard, grad_shard, row_stat, column_stat):
    scale = jnp.mean(column_stat, axis=-1, keepdims=True)[..., None]
    second = row_stat[..., :, None] * column_stat[..., None, :] / scale
    return weight_shard.astype(F32) - STEP_RATE * grad_shard * lax.rsqrt(second)


def without_outputs(stats):
    return jnp.concatenate([stats[0:3], stats[4:7]], axis=0)


def output_pair(stats):
    return jnp.stack([stats[3], stats[7]])


def on_device(
    ring,
    tokens,
    memory,
    target_segments,
    memory_segments,
    attention_weights,
    expand_weights,
    contract_weights,
    norm_gains,
    bucket_table,
    cotangent,
):
    rows = tokens.shape[0]
    spread_buckets = jnp.asarray(diagonal_onehot())
    lines = jnp.dot(
        bucket_table.T.astype(F32), jnp.asarray(tile_onehot()).T, precision=lax.Precision.HIGHEST
    ) + jnp.where(jnp.arange(3 * QROWS) // QROWS == 1, NEG_FILL, 0.0)
    far = jnp.pad(bucket_table[BUCKETS - 1].reshape(PAIRS, 1, 2), ((0, 0), (0, 0), (FAR_LANE, 126 - FAR_LANE)))
    act, act32 = ((rows, D), BF16), ((rows, D), F32)
    none = [None]
    query_mask, self_mask, cross_mask, near_bias = call(
        prepare_kernel,
        [((rows // QROWS, 2 * QROWS, 128), BF16), ((rows, 128), BF16), ((rows, 128), BF16)]
        + [((PAIRS, 2 * QROWS, 2 * QROWS), F32)],
        none * 3,
        (target_segments.reshape(1, rows), memory_segments.reshape(1, rows), lines),
        0.8,
    )
    pair = pair_spec(rows)
    head_acc = VMEM((rows, 128), F32)

    if ring:
        first = make_pieces(attention_weights, expand_weights, contract_weights, norm_gains)[None]
        r1 = ring_hop(first)
        x0, y0 = hop_xy(first)
        x1, y1 = hop_xy(r1)
        r2 = ring_hop(after(r1, near_bias, x0, y0))
        a0, b0 = corner_hops(x0, y0)
        r3 = ring_hop(r2)
        x2, y2 = hop_xy(after(r2, x1, y1))
        a1, b1 = corner_hops(x1, y1, a0, b0)
        x3, y3 = hop_xy(after(r3, x2, y2))
        a2, b2 = corner_hops(x2, y2, x3)
        a3, b3 = corner_hops(x3, y3)
        parts = []
        for steps, chunk, waits in (
            (0, (first, x0, y0, a0, b0), (x1, y1)),
            (1, (r1, x1, y1, a1, b1), (x2, y2)),
            (2, (r2, x2, y2, a2, b2), (x3, y3)),
            (3, (r3, x3, y3, a3, b3), ()),
        ):
            parts += parts_of(steps, *(with_core(values, *waits) for values in chunk))
        square, gains_in = place_square(parts)
        parts = overlapping(parts, 25)
    else:
        square, wide, narrow, gains_in = gather_plain(
            attention_weights, expand_weights, contract_weights, norm_gains
        )
    resident = ()
    if ring:
        square = in_vmem(square)

    n1, q, k, v, kc, vc, gains = call(
        functools.partial(pre_kernel, ring),
        [act] * 6 + [((8, D), F32)],
        none * 5,
        (tokens, memory, gains_in, square, square),
        3.4,
    )
    lse_shape = ((PAIRS, rows // QROWS, 2 * QROWS), F32)
    args = (q, k, v, near_bias, query_mask, self_mask, far)
    specs = [pair] * 3 + [NEAR_SPEC, None, None, FAR_SPEC]
    if ring:
        arrays = [pltpu.with_memory_space_constraint(a[0], pltpu.HBM) for a in parts]
        copies = functools.partial(place_copies, [a[1:] for a in parts], WIDE_TARGETS)
        ctxs, lse_self, wide, narrow = call(
            functools.partial(self_forward_kernel, copies, len(arrays)),
            [act, lse_shape] + WIDE_SHAPES,
            specs + [pl.BlockSpec(memory_space=pl.ANY)] * len(arrays),
            (*args, *arrays),
            5.0,
            grid=(PAIRS // STEP_PAIRS,),
            scratch=[pltpu.SemaphoreType.DMA((len(arrays) * len(WIDE_TARGETS),))],
            out_specs=[pair, LSE_SPEC, None, None],
            spaces=[jax.ShapeDtypeStruct] * 2 + [VMEM] * 2,
        )
        wide = in_vmem(wide.reshape(2, BLOCKS, D, WIDE))
        narrow = in_vmem(narrow.reshape(COLS, FF, WIDE))
        resident = wide, narrow
    else:
        ctxs, lse_self = call(
            functools.partial(self_forward_kernel, None, 0),
            [act, lse_shape],
            specs,
            args,
            5.0,
            grid=(PAIRS // STEP_PAIRS,),
            out_specs=[pair, LSE_SPEC],
        )
    res1, n2, qc = call(
        mid_kernel, [act32, act, act], none * 4, (ctxs, tokens, gains, square), 1.9, resident=resident
    )
    ctxc, lse_cross = call(
        cross_forward_kernel,
        [act, lse_shape],
        [pair] * 3 + [None, None],
        (qc, kc, vc, query_mask, cross_mask),
        5.8,
        grid=(PAIRS // STEP_PAIRS,),
        out_specs=[pair, LSE_SPEC],
        resident=resident,
    )
    res2, n3 = call(late_kernel, [act32, act], none * 4, (ctxc, res1, gains, square), 1.0, resident=resident)
    half = BLOCKS // 2
    hidden_shape = ((rows, FF // 2), BF16)
    if ring:
        grad_outs = grad_shapes(ring, False, half, half), grad_shapes(ring, False, half + 4, half + 4)
        more = [VMEM((2, FF, WIDE), F32)], 20
    else:
        grad_outs = [((half, D, WIDE), F32)] * 2
        grad_outs = [
            (outs, [jax.ShapeDtypeStruct] * len(outs), none * len(outs))
            for outs in (grad_outs, grad_outs + [((COLS, FF, WIDE), F32)])
        ]
        more = [VMEM((2, FF, WIDE), F32)], 40
    plain = [jax.ShapeDtypeStruct] * 3
    middle, dn3, hidden, *first_grads = call(
        functools.partial(ffn_kernel, ring, False),
        [act32, act32, hidden_shape] + grad_outs[0][0],
        none * 7,
        (n3, res2, res2, n3, cotangent, wide, narrow),
        8.0,
        scratch=send_scratch(ring, False),
        limit=more[1],
        spaces=plain + grad_outs[0][1],
        out_specs=none * 3 + grad_outs[0][2],
    )
    if ring:
        ffn_one = Scatter(first_grads)
        ffn_one.core()
        middle = after(middle, *ffn_one.first())
    output, dn3, _, *last_grads = call(
        functools.partial(ffn_kernel, ring, True),
        [act, act32, hidden_shape] + grad_outs[1][0],
        none * 7,
        (n3, middle, dn3, hidden, cotangent, wide, narrow),
        13.0,
        scratch=send_scratch(ring, False) + more[0],
        limit=more[1],
        spaces=plain + grad_outs[1][1],
        out_specs=none * 3 + grad_outs[1][2],
    )
    if ring:
        ffn_two = Scatter(last_grads)
        first_half, ffn = Finish([ffn_one]), Finish([ffn_two])
        sent = first_half.second(dn3)
        ffn_two.core(ffn_one.a1, ffn_one.b1)
        dn3 = after(dn3, *sent)
    r2g, ccg, gain_three = call(
        third_back_kernel,
        [act32, act, ((1, D), F32)],
        none * 5,
        (dn3, res2, cotangent, gains, square),
        1.3,
    )
    if ring:
        ccg = after(ccg, *ffn_two.first(r2g))
    dqc, dkc, dvc = call(
        cross_back_kernel,
        [act] * 3,
        [pair] * 5 + [LSE_SPEC, None, None],
        (qc, kc, vc, ccg, ctxc, lse_cross, query_mask, cross_mask),
        8.8,
        grid=(PAIRS // STEP_PAIRS,),
        scratch=[head_acc, head_acc],
        out_specs=[pair] * 3,
    )
    if ring:
        dkc = after(dkc, *first_half.third(dqc))
    shapes = grad_shapes(ring, False, 6)
    memory_grad, *cross_a = call(
        functools.partial(memory_grads_kernel, ring),
        [act] + shapes[0],
        none * 4,
        (dkc, dvc, memory, square),
        3.9,
        scratch=send_scratch(ring, False),
        spaces=plain[:1] + shapes[1],
        out_specs=none + shapes[2],
    )
    dqc = after(dqc, memory_grad)
    r1g, csg, gain_two = call(
        second_back_kernel,
        [act32, act, ((1, D), F32)],
        none * 5,
        (dqc, res1, r2g, gains, square),
        3.0,
    )
    shapes = grad_shapes(ring, False, 9)
    cross_b = call(
        functools.partial(middle_grads_kernel, ring),
        shapes[0],
        none * 6,
        (dqc, n2, r1g, ctxs, r2g, ctxc),
        2.5,
        scratch=send_scratch(ring, False),
        spaces=shapes[1],
        out_specs=shapes[2],
    )
    if ring:
        cross = Scatter([cross_a[0], cross_b[0], cross_a[1], cross_b[1]])
        cross.core(ffn_two.a1, ffn_two.b1)
        rest = Finish([cross])
        csg = after(csg, *ffn.second(cross_b[0]), *first_half.fourth(cross_b[0]))
    dqs, dks, dvs, near_sum, far_sum = call(
        self_back_kernel,
        [act] * 3 + [((PAIRS, 2 * QROWS, 2 * QROWS), F32), ((PAIRS, 8, 2 * QROWS), F32)],
        [pair] * 5 + [LSE_SPEC, NEAR_SPEC, None, None, FAR_SPEC],
        (q, k, v, csg, ctxs, lse_self, near_bias, query_mask, self_mask, far),
        8.1,
        grid=(PAIRS // STEP_PAIRS,),
        scratch=[head_acc, head_acc],
        out_specs=[pair] * 3 + [NEAR_SPEC, FAR_SUM_SPEC],
    )
    if ring:
        dqs = after(dqs, *cross.first(dqs), *ffn.third(dqs))
    shapes = grad_shapes(ring, False, 5, 4)
    self_grads = call(
        functools.partial(first_grads_kernel, ring),
        shapes[0],
        none * 4,
        (dqs, dks, dvs, n1),
        2.5,
        scratch=send_scratch(ring, False),
        spaces=shapes[1],
        out_specs=shapes[2],
    )
    if ring:
        own = Scatter(self_grads)
        dks = after(dks, self_grads[0])
    input_grad, gain_one = call(
        first_back_kernel,
        [act, ((1, D), F32)],
        none * 7,
        (dqs, dks, dvs, tokens, r1g, gains, square),
        3.4,
    )
    if ring:
        last = Finish([own])
        own.core(ffn.a2, ffn.b2)
        sent = ffn.fourth(input_grad)
        sent = rest.second(*sent)
        sent = own.first(*sent)
        sent = rest.third_direct(*sent)
        sent = last.second(*sent)
        last.third_direct(*sent)
    diag = call(
        diagonals_kernel,
        [((PAIRS, 2, 2 * QROWS), F32)],
        none * 2,
        (after(near_sum, input_grad), far_sum),
        3.0,
    )[0]
    gain_parts = (gain_one, gain_two, gain_three)
    if ring:
        parts = []
        for group in (first_half, ffn, rest, last):
            parts += group.parts
        attention_grad, expand_grad, contract_grad, sums = call(
            functools.partial(share_kernel, [len(group.parts) for group in (first_half, ffn, rest, last)]),
            [((8, 24, D), F32), ((2, 24, FF), F32), ((64, D), F32), ((SUM_ROWS, D), F32)],
            none * (len(parts) + 5),
            (*parts, *gain_parts, diag, spread_buckets),
            1.5,
        )
        sums = sum_ring(sums)
        attention_rows, expand_rows, contract_rows, pair_rows = call(
            rows_kernel,
            [((6, 24), F32), ((2, 24), F32), ((1, 64), F32), ((2, 24), F32)],
            none * 3,
            (attention_grad, expand_grad, contract_grad),
            0.8,
        )
        (
            attention_new,
            expand_new,
            contract_new,
            attention_columns,
            expand_columns,
            contract_columns,
            gains_grad,
            projection_statistics,
            bucket_grad,
        ) = call(
            update_kernel,
            [
                ((8, 24, D), F32),
                ((2, 24, FF), F32),
                ((64, D), F32),
                ((6, D), F32),
                ((2, FF), F32),
                ((1, D), F32),
                ((3, 24), F32),
                ((2, 2, 24), F32),
                ((BUCKETS, HEADS), F32),
            ],
            none * 8,
            (sums, pair_rows, attention_grad, expand_grad, contract_grad, attention_weights, expand_weights, contract_weights),
            1.4,
        )
        contract_rows, contract_columns = contract_rows.reshape(64), contract_columns.reshape(D)
    else:
        bucket_part = jnp.dot(
            spread_buckets.T,
            diag.reshape(HEADS, 2 * QROWS).T,
            precision=lax.Precision.HIGHEST,
            preferred_element_type=F32,
        )
        pieces = jnp.concatenate([self_grads[0], cross_b[0][:6], cross_a[0], cross_b[0][6:]])
        attention_grad = scatter_plain(pieces, (8, D, D), 1)
        expand_pieces = jnp.stack([jnp.concatenate([first_grads[i], last_grads[i]]) for i in range(2)])
        expand_grad = scatter_plain(expand_pieces, (2, D, FF), 1)
        contract_grad = scatter_plain(last_grads[2], (FF, D), 0)
        attention_rows, attention_part = factored_stats(attention_grad, D)
        expand_rows, expand_part = factored_stats(expand_grad, D)
        contract_rows, contract_part = factored_stats(contract_grad, FF)
        attention_columns, expand_columns, contract_columns, bucket_grad, gains_sum = lax.psum(
            (attention_part, expand_part, contract_part, bucket_part, jnp.concatenate(gain_parts)), AXES
        )
        attention_new = factored_update(attention_weights, attention_grad, attention_rows, attention_columns)
        expand_new = factored_update(expand_weights, expand_grad, expand_rows, expand_columns)
        contract_new = factored_update(contract_weights, contract_grad, contract_rows, contract_columns)
        share_width = attention_rows.shape[1]
        share_start = lax.axis_index(AXES) * share_width
        column_share = lax.dynamic_slice_in_dim(attention_columns, share_start, share_width, 1)
        gains_grad = lax.dynamic_slice_in_dim(gains_sum, share_start, share_width, 1)
        projection_statistics = jnp.stack([output_pair(attention_rows), output_pair(column_share)])
        attention_rows, attention_columns = without_outputs(attention_rows), without_outputs(attention_columns)
    return (
        output,
        input_grad,
        memory_grad,
        attention_grad,
        expand_grad,
        contract_grad,
        gains_grad,
        bucket_grad,
        attention_rows,
        attention_columns,
        expand_rows,
        expand_columns,
        contract_rows,
        contract_columns,
        attention_new,
        expand_new,
        contract_new,
        projection_statistics,
    )


def solution(mesh):
    ring = dict(mesh.shape) == {"wide": 16, "narrow": 2}
    rows, both = P(AXES, None), P(None, AXES, None)
    placed = (rows, rows, P(AXES), P(AXES), both, both, rows, P(None, AXES), P(), rows)
    return jax.shard_map(
        functools.partial(on_device, ring),
        mesh=mesh,
        in_specs=placed,
        out_specs=(
            rows,
            rows,
            rows,
            both,
            both,
            rows,
            P(None, AXES),
            P(),
            P(None, AXES),
            P(),
            P(None, AXES),
            P(),
            P(AXES),
            P(),
            both,
            both,
            rows,
            P(None, None, AXES),
        ),
        check_vma=False,
    )
```

```python
import functools
import math

import jax
import jax.numpy as jnp
import numpy as np
from jax import lax
from jax.experimental import pallas as pl
from jax.experimental.pallas import tpu as pltpu
from jax.sharding import PartitionSpec as P

D = 768
HEADS = 12
FF = 2048
BUCKETS = 32
MAX_DIST = 128
TGT_LEN = 512
MEM_LEN = 512
WIDE = 256
COLS = D // WIDE
BLOCKS = FF // WIDE
PAIRS = HEADS // 2
QROWS = 128

NEG_FILL = -(2.0**30)
DOCS = 4
FAR_LANE = 8
EPSILON = 1e-06
TINY = 1e-30
STEP_RATE = 0.01
AXES = ("wide", "narrow")
F32 = jnp.float32
BF16 = jnp.bfloat16
MIB = 1024 * 1024
VMEM = pltpu.VMEM


def bucket_onehot(length, bucket_count, far_limit):
    exact_span = bucket_count // 2
    onehot_rows = np.zeros((length, bucket_count), np.float32)
    for distance in range(length):
        if distance < exact_span:
            bucket_id = distance
        else:
            bucket_id = min(
                bucket_count - 1,
                exact_span
                + int(
                    math.log(distance / exact_span)
                    / math.log(far_limit / exact_span)
                    * (bucket_count - exact_span)
                ),
            )
        onehot_rows[distance, bucket_id] = 1.0
    return onehot_rows


def diagonal_onehot():
    t = np.arange(2 * QROWS)
    distance = np.where(t <= QROWS, QROWS - t, 3 * QROWS - t)
    return bucket_onehot(TGT_LEN, BUCKETS, MAX_DIST)[distance]


def tile_onehot():
    t = np.arange(3 * QROWS)
    distance = np.where(t < QROWS, QROWS + t, t - 2 * QROWS)
    rows = bucket_onehot(TGT_LEN, BUCKETS, MAX_DIST)[np.maximum(distance, 0)]
    rows[:, BUCKETS - 1] -= 1.0
    return np.where((distance >= 0)[:, None], rows, 0.0).astype(np.float32)


def mm(left, right):
    return jnp.dot(left, right, preferred_element_type=F32)


def mm_nt(left, right):
    return lax.dot_general(left, right, (((1,), (1,)), ((), ())), preferred_element_type=F32)


def mm_tn(left, right):
    return lax.dot_general(left, right, (((0,), (0,)), ((), ())), preferred_element_type=F32)


def low(values):
    return values.astype(BF16)


def cols(index):
    return slice(index * WIDE, (index + 1) * WIDE)


def inverse_rms(values):
    return lax.rsqrt(jnp.mean(values * values, axis=-1, keepdims=True) + EPSILON)


def norm_back(values, gain, grad):
    scale = inverse_rms(values)
    gain_grad = jnp.sum(values * scale * grad, axis=0, keepdims=True)
    scaled = gain * grad
    inner = jnp.mean(values * scaled, axis=-1, keepdims=True)
    return scale * scaled - values * (scale * scale * scale * inner), gain_grad


def my_index():
    return lax.axis_index("wide") * 2 + lax.axis_index("narrow")


def in_vmem(values):
    return pltpu.with_memory_space_constraint(values, pltpu.VMEM)


RATE = 1.15e9
SCALE = 1.0


def call(body, outs, in_specs, args, us, grid=None, scratch=(), limit=20, out_specs=None, spaces=None, resident=()):
    kwargs = {} if grid is None else {"grid": grid}
    whole = pl.BlockSpec(memory_space=VMEM)
    count, inner = len(args), body
    if resident:
        args, in_specs = (*args, *resident), [*in_specs, *[None] * len(resident)]
        body = lambda *refs: inner(*refs[:count], *refs[count + len(resident) :])
    spaces = spaces or [jax.ShapeDtypeStruct] * len(outs)
    return pl.pallas_call(
        body,
        out_shape=[space(*o) for space, o in zip(spaces, outs)],
        in_specs=[whole if s is None else s for s in in_specs],
        out_specs=[whole] * len(outs) if out_specs is None else [whole if s is None else s for s in out_specs],
        scratch_shapes=list(scratch),
        compiler_params=pltpu.CompilerParams(vmem_limit_bytes=limit * MIB),
        cost_estimate=pl.CostEstimate(flops=int(us * RATE * SCALE), bytes_accessed=1, transcendentals=0),
        **kwargs,
    )(*args)


def slot_mask(first, slot):
    high, mid, z = slot >> 3, (slot >> 2) & 1, slot & 3
    dy, dx = (high, mid) if first == 0 else (mid, high)
    return z * 8 + dy * 4 + dx


BUFFERS = 4


class Sender:
    def __init__(self, acc, stage=None, sem=None):
        self.acc, self.stage, self.sem = acc, stage, sem
        self.count, self.pending = 0, [[] for _ in range(BUFFERS)]

    def turn(self):
        buffer = self.count % BUFFERS
        self.count += 1
        for copy in self.pending[buffer]:
            copy.wait()
        self.pending[buffer] = []
        return buffer

    def start(self, buffer, source, target):
        index = len(self.pending[buffer])
        copy = pltpu.make_async_copy(source, target, self.sem.at[buffer, index])
        copy.start()
        self.pending[buffer].append(copy)

    def finish(self):
        for pending in self.pending:
            for copy in pending:
                copy.wait()

    def matrix(self, own, sib, first, piece, value):
        buffer = self.turn()
        held = self.acc.at[buffer % self.acc.shape[0]]
        held[...] = value
        me = my_index()
        for index, (out, core) in enumerate(((own, 0), (sib, 2))):
            for slot in range(16):
                owner = lax.bitwise_xor(me, slot_mask(first, slot) + core)
                rows = held[pl.ds(pl.multiple_of(owner * 24, 8), 24), :]
                rows = low(rows.reshape(3, 8, WIDE))
                if self.stage is None:
                    out[slot, piece] = rows
                else:
                    self.stage[buffer, index, slot] = rows
            if self.stage is not None:
                self.start(buffer, self.stage.at[buffer, index], out.at[:, piece])

    def contract(self, outs, column, start, value_of):
        buffer = self.turn()
        me = my_index()
        for index, out in enumerate(outs):
            first, core = index % 2, index // 2 * 2
            for slot in range(16):
                owner = lax.bitwise_xor(me, slot_mask(first, slot) + core)
                rows = value_of(pl.ds(pl.multiple_of(owner * 64 + first * 32, 8), 32))
                out[slot, start : start + 4, column] = low(rows.reshape(4, 8, WIDE))


def send_scratch(ring, staged):
    if not ring:
        return []
    acc = [VMEM((2, D, WIDE), F32)]
    if not staged:
        return acc
    return acc + [VMEM((BUFFERS, 2, 16, 3, 8, WIDE), BF16), pltpu.SemaphoreType.DMA((BUFFERS, 2))]


def grad_shapes(ring, staged, *pieces):
    if not ring:
        return [((sum(pieces), D, WIDE), F32)], [jax.ShapeDtypeStruct], [None]
    shapes = [((16, n, 3, 8, WIDE), BF16) for n in pieces] * 2
    space, spec = (pltpu.HBM, pl.BlockSpec(memory_space=pl.ANY)) if staged else (VMEM, None)
    return shapes, [space] * len(shapes), [spec] * len(shapes)


def pre_kernel(ring, tok, mem, gains_in, w, wm, n1, q, k, v, kc, vc, gains):
    if ring:
        for c in range(COLS):
            gains[:, cols(c)] = jnp.sum(gains_in[0, :, c].astype(F32), axis=0)
    else:
        gains[...] = jnp.concatenate([gains_in[...].astype(F32), jnp.zeros((5, D), F32)], axis=0)
    x = tok[...].astype(F32)
    normed = low(x * inverse_rms(x) * gains[0:1, :])
    n1[...] = normed
    memory = mem[...]
    for c in range(COLS):
        q[:, cols(c)] = low(mm(normed, w[0, c]))
        k[:, cols(c)] = low(mm(normed, w[1, c]))
        v[:, cols(c)] = low(mm(normed, w[2, c]))
        kc[:, cols(c)] = low(mm(memory, wm[5, c]))
        vc[:, cols(c)] = low(mm(memory, wm[6, c]))


def halves(block):
    lane = lax.broadcasted_iota(jnp.int32, block.shape, 1)
    zero = jnp.zeros_like(block)
    return jnp.concatenate([jnp.where(lane < 64, block, zero), jnp.where(lane < 64, zero, block)], axis=0)


def prepare_kernel(target, memory, line, query_mask, self_mask, cross_mask, near):
    document = lax.broadcasted_iota(jnp.int32, (128, target.shape[1]), 0)
    real = document < DOCS
    self_mask[...] = low(jnp.where(real & (document == target[...]), 1.0, 0.0).T)
    cross_mask[...] = low(jnp.where(real & (document == memory[...]), 1.0, 0.0).T)
    other = jnp.where(real & (document != target[...]), NEG_FILL, 0.0).T
    lane = lax.broadcasted_iota(jnp.int32, (QROWS, 128), 1)
    for block in range(TGT_LEN // QROWS):
        for h in range(2):
            rows = other[block * QROWS : (block + 1) * QROWS, :]
            query_mask[block, h * QROWS : (h + 1) * QROWS, :] = low(jnp.where(lane == FAR_LANE + h, 1.0, rows))
    for head in range(HEADS):
        tile = jnp.broadcast_to(line[head : head + 1, :], (2 * QROWS, 3 * QROWS))
        tile = pltpu.roll(tile, 0, 1, stride=1, stride_axis=0)[:, :QROWS]
        near[head // 2, :, (head % 2) * QROWS : (head % 2 + 1) * QROWS] = tile


def add_near(scores, near, pair, block):
    if block == 0:
        return scores + near[pair, QROWS:, :]
    start = scores.shape[0] - 2 * QROWS
    if start == 0:
        return scores + near[pair]
    return jnp.concatenate([scores[:start], scores[start:] + near[pair]], axis=0)


def pair_columns(turned):
    return jnp.concatenate([turned[:64, :QROWS], turned[64:128, QROWS:]], axis=0)


def lanes(pair):
    return slice(pair * 128, (pair + 1) * 128)


def rows_of(block):
    return slice(block * QROWS, (block + 1) * QROWS)


def masked_keys(k, key_mask, far, pair):
    mask = key_mask[...] if far is None else key_mask[...] + far[pair]
    return jnp.concatenate([k[:, lanes(pair)], mask], axis=1)


def ahead(make, items, depth):
    ready = [make(item) for item in items[:depth]]
    for index, item in enumerate(items):
        if index + depth < len(items):
            ready.append(make(items[index + depth]))
        yield item, ready.pop(0)


def with_ones(values):
    turned = values.T
    return jnp.concatenate([turned, jnp.ones((16, turned.shape[1]), turned.dtype)], axis=0)


def attend_forward(q, k, v, near, query_mask, key_mask, far, out, lse):
    count = q.shape[1] // 128
    keys = [masked_keys(k, key_mask, far, pair) for pair in range(count)]
    values_t = [with_ones(v[:, lanes(pair)]) for pair in range(count)]
    items = [(pair, block) for pair in range(count) for block in range(TGT_LEN // QROWS)]

    def make(item):
        pair, block = item
        end = MEM_LEN if near is None else (block + 1) * QROWS
        queries = jnp.concatenate([halves(q[rows_of(block), lanes(pair)]), query_mask[block]], axis=1)
        return mm_nt(keys[pair][:end], queries)

    for (pair, block), scores in ahead(make, items, 2):
        if near is not None:
            scores = add_near(scores, near, pair, block)
        top = jnp.max(scores, axis=0, keepdims=True)
        raised = low(jnp.exp(scores - top))
        context = mm(values_t[pair][:, : scores.shape[0]], raised)
        sums = context[128:129, :]
        lse[pair, block : block + 1, :] = top + jnp.log(sums)
        context = pair_columns(context * (1.0 / sums))
        out[rows_of(block), lanes(pair)] = low(context.T)


def self_forward_kernel(copies, count, q, k, v, near, query_mask, key_mask, far, *rest):
    out, lse = rest[count : count + 2]
    if copies is not None:
        started = copies(rest[:count], rest[count + 2 : -1], rest[-1])

        @pl.when(pl.program_id(0) == 0)
        def _():
            for copy in started:
                copy.start()

    attend_forward(q, k, v, near, query_mask, key_mask, far, out, lse)
    if copies is not None:

        @pl.when(pl.program_id(0) == pl.num_programs(0) - 1)
        def _():
            for copy in started:
                copy.wait()


def cross_forward_kernel(q, k, v, query_mask, key_mask, out, lse):
    attend_forward(q, k, v, None, query_mask, key_mask, None, out, lse)


def pair_spec(pairs):
    return pl.BlockSpec((TGT_LEN, 128 * pairs), lambda p: (0, p))


def step_spec(pairs, *dims):
    return pl.BlockSpec((pairs, *dims), lambda p: (p, 0, 0))


def near_spec(pairs):
    return step_spec(pairs, 2 * QROWS, 2 * QROWS)


def lse_spec(pairs):
    return step_spec(pairs, TGT_LEN // QROWS, 2 * QROWS)


def far_spec(pairs):
    return step_spec(pairs, 1, 128)


def mid_kernel(ctx, tok, gains, w, res, n2, qc):
    context = ctx[...]
    for c in range(COLS):
        res[:, cols(c)] = tok[:, cols(c)].astype(F32) + mm(context, w[3, c])
    x = res[...]
    normed = low(x * inverse_rms(x) * gains[1:2, :])
    n2[...] = normed
    for c in range(COLS):
        qc[:, cols(c)] = low(mm(normed, w[4, c]))


def late_kernel(ctx, res1, gains, w, res2, n3):
    context = ctx[...]
    for c in range(COLS):
        res2[:, cols(c)] = res1[:, cols(c)] + mm(context, w[7, c])
    x = res2[...]
    n3[...] = low(x * inverse_rms(x) * gains[2:3, :])


def gelu_pair(gate):
    rate = math.sqrt(2.0 / math.pi)
    square = gate * gate
    bend = jnp.tanh(rate * gate * (1.0 + 0.044715 * square))
    half = 0.5 * (1.0 + bend)
    slope = half + 0.5 * gate * (1.0 - bend * bend) * rate * (1.0 + 3.0 * 0.044715 * square)
    return gate * half, slope


def ffn_kernel(ring, last, n3, before, dn3_before, hidden_before, cot, wide, narrow, out, dn3, hidden, *rest):
    half = BLOCKS // 2
    if ring:
        grads, rest = rest[:4], rest[4:]
        own_a, own_b, sib_a, sib_b = grads
        sender = Sender(rest[0])
    else:
        grads = rest[:3] if last else rest[:2]
    blocks = list(range(half, BLOCKS)) if last else list(range(half))
    normed, turned = n3[...], n3[...].T
    span = slice(blocks[0] * WIDE, (blocks[-1] + 1) * WIDE)

    def make(block):
        rows = slice(block * WIDE, (block + 1) * WIDE)
        back = mm_nt(cot[:, cols(0)], narrow[0, rows, :])
        for c in range(1, COLS):
            back = back + mm_nt(cot[:, cols(c)], narrow[c, rows, :])
        return mm(normed, wide[0, block]), mm(normed, wide[1, block]), back

    for index, (block, (gate, lift, back)) in enumerate(ahead(make, blocks, 1)):
        active, slope = gelu_pair(gate)
        hidden[:, cols(index)] = low(active * lift)
        gate_grad = low(back * lift * slope)
        lift_grad = low(back * active)
        part = mm_nt(gate_grad, wide[0, block]) + mm_nt(lift_grad, wide[1, block])
        if index == 0:
            dn3[...] = dn3_before[...] + part if last else part
        else:
            dn3[...] += part
        if ring:
            sender.matrix(own_a, sib_a, 0, index, mm(turned, gate_grad))
            sender.matrix(own_b, sib_b, 1, index, mm(turned, lift_grad))
        else:
            grads[0][index] = mm(turned, gate_grad)
            grads[1][index] = mm(turned, lift_grad)
    for c in range(COLS):
        total = before[:, cols(c)] + mm(hidden[...], narrow[c, span, :])
        out[:, cols(c)] = low(total) if last else total
    if last:
        con_acc = rest[-1]
        first_t, last_t = hidden_before[...].T, hidden[...].T
        for c in range(COLS):
            for rows, left in ((slice(0, FF // 2), first_t), (slice(FF // 2, FF), last_t)):
                con_acc[c % 2, rows, :] = mm(left, cot[:, cols(c)])
            if ring:
                sender.contract((own_a, own_b, sib_a, sib_b), c, half, lambda rows, c=c: con_acc[c % 2, rows, :])
            else:
                grads[2][c] = con_acc[c % 2]
    if ring:
        sender.finish()


def third_back_kernel(dn3, res2, cot, gains, w, r2g, ccg, gg):
    back, gain_grad = norm_back(res2[...], gains[2:3, :], dn3[...])
    gg[...] = gain_grad
    grad = cot[...].astype(F32) + back
    r2g[...] = grad
    cross_low = low(grad)
    total = mm_nt(cross_low[:, cols(0)], w[7, 0])
    for c in range(1, COLS):
        total = total + mm_nt(cross_low[:, cols(c)], w[7, c])
    ccg[...] = low(total)


def attend_backward(q, k, v, dc, o, lse, near, query_mask, key_mask, far, dq, dk, dv, dk_acc, dv_acc, near_sum, far_sum):
    count = q.shape[1] // 128
    keys = [masked_keys(k, key_mask, far, pair) for pair in range(count)]
    keys_t = [k[:, lanes(pair)].T for pair in range(count)]
    items = [(pair, block) for pair in range(count) for block in range(TGT_LEN // QROWS)]

    def make(item):
        pair, block = item
        end = MEM_LEN if near is None else (block + 1) * QROWS
        queries, grads = halves(q[rows_of(block), lanes(pair)]), halves(dc[rows_of(block), lanes(pair)])
        scores = mm_nt(keys[pair][:end], jnp.concatenate([queries, query_mask[block]], axis=1))
        return end, queries, grads, scores, mm_nt(v[:end, lanes(pair)], grads)

    beyond = None
    for (pair, block), (end, queries, grads, scores, prob_grad) in ahead(make, items, 1):
        rows = rows_of(block)
        if near is not None:
            scores = add_near(scores, near, pair, block)
        probs = jnp.exp(scores - lse[pair, block : block + 1, :])
        inner = (dc[rows, lanes(pair)].astype(F32) * o[rows, lanes(pair)].astype(F32)).T
        inner = jnp.concatenate(
            [jnp.sum(inner[:64], axis=0, keepdims=True), jnp.sum(inner[64:], axis=0, keepdims=True)], axis=1
        )
        score_grad = low(probs * (prob_grad - inner))
        dk_part, dv_part = mm(score_grad, queries), mm(low(probs), grads)
        if block == 0:
            dk_acc[:end, :], dv_acc[:end, :] = dk_part, dv_part
        else:
            before = end if near is None else end - QROWS
            dk_acc[:before, :] += dk_part[:before]
            dv_acc[:before, :] += dv_part[:before]
            if before < end:
                dk_acc[before:end, :], dv_acc[before:end, :] = dk_part[before:], dv_part[before:]
        dq[rows, lanes(pair)] = low(pair_columns(mm(keys_t[pair][:, :end], score_grad)).T)
        if near is not None:
            wide = score_grad.astype(F32)
            if block == 0:
                near_sum[pair, :QROWS, :] = jnp.zeros((QROWS, 2 * QROWS), F32)
                near_sum[pair, QROWS:, :] = wide
                beyond = jnp.zeros((1, 2 * QROWS), F32)
            else:
                near_sum[pair] += wide[end - 2 * QROWS :, :]
            if block > 1:
                beyond = beyond + jnp.sum(wide[: end - 2 * QROWS, :], axis=0, keepdims=True)
            far_sum[pair] = jnp.broadcast_to(beyond, (8, 2 * QROWS))
        if block == TGT_LEN // QROWS - 1:
            dk[:, lanes(pair)] = low(dk_acc[...])
            dv[:, lanes(pair)] = low(dv_acc[...])


def cross_back_kernel(q, k, v, dc, o, lse, query_mask, key_mask, dq, dk, dv, dk_acc, dv_acc):
    attend_backward(
        q, k, v, dc, o, lse, None, query_mask, key_mask, None, dq, dk, dv, dk_acc, dv_acc, None, None
    )


def self_back_kernel(
    q, k, v, dc, o, lse, near, query_mask, key_mask, far, dq, dk, dv, near_sum, far_sum, dk_acc, dv_acc
):
    attend_backward(
        q, k, v, dc, o, lse, near, query_mask, key_mask, far, dq, dk, dv, dk_acc, dv_acc, near_sum, far_sum
    )


def diagonal_sums(grid):
    width = 2 * QROWS
    group = grid[:8, :]
    for shift in range(8, QROWS, 8):
        group = group + pltpu.roll(grid[shift : shift + 8, :], width - shift, 1)
    row = lax.broadcasted_iota(jnp.int32, group.shape, 0)
    for bit in (1, 2, 4):
        group = jnp.where((row & bit) != 0, pltpu.roll(group, width - bit, 1), group)
    return jnp.sum(group, axis=0, keepdims=True)


def diagonals_kernel(near_sum, far_sum, diag):
    lane = lax.broadcasted_iota(jnp.int32, (1, 2 * QROWS), 1)
    for pair in range(PAIRS):
        for h in range(2):
            part = slice(h * QROWS, (h + 1) * QROWS)
            beyond = jnp.sum(far_sum[pair, 0:1, part], keepdims=True)
            diag[pair, h : h + 1, :] = diagonal_sums(near_sum[pair, :, part].T) + jnp.where(lane == 0, beyond, 0.0)


def second_back_kernel(dq, res1, r2g, gains, w, r1g, csg, gg):
    query_grad = dq[...]
    back = mm_nt(query_grad[:, cols(0)], w[4, 0])
    for c in range(1, COLS):
        back = back + mm_nt(query_grad[:, cols(c)], w[4, c])
    moved, gain_grad = norm_back(res1[...], gains[1:2, :], back)
    gg[...] = gain_grad
    grad = r2g[...] + moved
    r1g[...] = grad
    self_low = low(grad)
    total = mm_nt(self_low[:, cols(0)], w[3, 0])
    for c in range(1, COLS):
        total = total + mm_nt(self_low[:, cols(c)], w[3, c])
    csg[...] = low(total)


def memory_grads_kernel(ring, dk, dv, mem, w, mg, *rest):
    left = mem[...].T
    pieces = [(matrix * COLS + c, (dk, dv)[matrix], c) for matrix in range(2) for c in range(COLS)]
    put_pieces(ring, rest, [(0, piece, left, right[:, cols(c)]) for piece, right, c in pieces])
    total = mm_nt(dk[:, cols(0)], w[5, 0]) + mm_nt(dv[:, cols(0)], w[6, 0])
    for c in range(1, COLS):
        total = total + mm_nt(dk[:, cols(c)], w[5, c]) + mm_nt(dv[:, cols(c)], w[6, c])
    mg[...] = low(total)


def middle_grads_kernel(ring, dq, n2, r1g, ctxs, r2g, ctxc, *rest):
    pieces = []
    for index, (left, right) in enumerate(((ctxs, low(r1g[...])), (n2, dq[...]), (ctxc, low(r2g[...])))):
        left = left[...].T
        pieces += [(1, index * COLS + c, left, right[:, cols(c)]) for c in range(COLS)]
    put_pieces(ring, rest, pieces)


def put_pieces(ring, rest, pieces):
    if not ring:
        for index, (_, _, left, right) in enumerate(pieces):
            rest[0][index] = mm(left, right)
        return
    refs, sender = rest[:-1], Sender(rest[-1])
    for part, piece, left, right in pieces:
        group = refs[: len(refs) // 2], refs[len(refs) // 2 :]
        out = part if len(refs) == 4 else 0
        sender.matrix(group[0][out], group[1][out], part, piece, mm(left, right))


def first_grads_kernel(ring, dq, dk, dv, n1, *rest):
    left = n1[...].T
    pieces = [(right, c) for right in (dq, dk, dv) for c in range(COLS)]
    put_pieces(
        ring,
        rest,
        [(int(i >= 5), i - 5 if i >= 5 else i, left, right[:, cols(c)]) for i, (right, c) in enumerate(pieces)],
    )


def first_back_kernel(dq, dk, dv, tok, r1g, gains, w, ig, gg):
    back = None
    for matrix, right in enumerate((dq, dk, dv)):
        for c in range(COLS):
            term = mm_nt(right[:, cols(c)], w[matrix, c])
            back = term if back is None else back + term
    moved, gain_grad = norm_back(tok[...].astype(F32), gains[0:1, :], back)
    gg[...] = gain_grad
    ig[...] = low(r1g[...] + moved)


ROW_GAINS, ROW_CONTRACT, ROW_EXPAND, ROW_BUCKETS, SUM_ROWS = 8, 11, 12, 18, 24
RUNS = ((0, D), (D, D), (2 * D, FF - 2 * D))


def squares_of(values):
    return values * values + TINY


def row_line(values):
    squares = squares_of(values)
    width = squares.shape[1]
    part = squares[:, :128]
    for start in range(128, width, 128):
        part = part + squares[:, start : start + 128]
    return jnp.sum(part.T, axis=0, keepdims=True) * (1.0 / width)


def share_kernel(counts, *refs):
    shares, start = [], 0
    for count in counts:
        parts = [ref[0].astype(F32) for ref in refs[start : start + count]]
        start += count
        shares.append((parts[0] + parts[1]) + (parts[2] + parts[3]) if count == 4 else parts[0] + parts[1] + parts[2])
    one, two, cross, own = shares
    gate = [one[b] if b < 4 else two[b - 4] for b in range(BLOCKS)]
    lift = [one[4 + b] if b < 4 else two[4 + b] for b in range(BLOCKS)]
    gain_one, gain_two, gain_three, diag, onehot, att, exp, con, sums = refs[start:]
    sums[...] = jnp.zeros_like(sums)

    def keep(out, matrix, row, column, piece):
        rows = piece.reshape(24, WIDE)
        out[matrix, :, cols(column)] = rows
        place = column * WIDE
        sums[row + place // D : row + place // D + 1, place % D : place % D + WIDE] = jnp.sum(
            squares_of(rows), axis=0, keepdims=True
        )

    for c in range(COLS):
        for matrix in range(3):
            keep(att, matrix, matrix, c, own[matrix * COLS + c])
        for index, matrix in enumerate((5, 6, 3, 4, 7)):
            keep(att, matrix, matrix, c, cross[index * COLS + c])
        total = jnp.zeros((1, WIDE), F32)
        for octet in range(8):
            rows = two[4 + octet if octet < 4 else 8 + octet, c]
            con[octet * 8 : octet * 8 + 8, cols(c)] = rows
            total = total + jnp.sum(squares_of(rows), axis=0, keepdims=True)
        sums[ROW_CONTRACT : ROW_CONTRACT + 1, cols(c)] = total
    for b in range(BLOCKS):
        keep(exp, 0, ROW_EXPAND, b, gate[b])
        keep(exp, 1, ROW_EXPAND + 3, b, lift[b])
    for row, gain in enumerate((gain_one, gain_two, gain_three)):
        sums[ROW_GAINS + row : ROW_GAINS + row + 1, :] = gain[...]
    for h in range(2):
        sums[ROW_BUCKETS:SUM_ROWS, h * BUCKETS : (h + 1) * BUCKETS] = jnp.dot(
            diag[:, h, :], onehot[...], precision=lax.Precision.HIGHEST, preferred_element_type=F32
        )


def rows_kernel(att, exp, con, att_rows, exp_rows, con_rows, pair_rows):
    for row, matrix in enumerate((0, 1, 2, 4, 5, 6)):
        att_rows[row : row + 1, :] = row_line(att[matrix])
    for row, matrix in enumerate((3, 7)):
        pair_rows[row : row + 1, :] = row_line(att[matrix])
    for matrix in range(2):
        exp_rows[matrix : matrix + 1, :] = row_line(exp[matrix])
    con_rows[...] = row_line(con[...])


def new_rows(weight, grad, column_stat):
    squares = squares_of(grad)
    row_stat = jnp.mean(squares, axis=-1, keepdims=True)
    scale = jnp.mean(column_stat, axis=-1, keepdims=True)
    second = (row_stat / scale) * column_stat
    return weight.astype(F32) - STEP_RATE * grad * lax.rsqrt(second)


def update_kernel(
    sums, pair_rows, att, exp, con, att_w, exp_w, con_w, att_new, exp_new, con_new, att_cols, exp_cols, con_cols, gains, pairs, buckets
):
    me = my_index()
    square = sums[0:8, :] * (1.0 / D)
    for matrix in range(8):
        att_new[matrix] = new_rows(att_w[matrix], att[matrix], square[matrix : matrix + 1, :])
    for row, matrix in enumerate((0, 1, 2, 4, 5, 6)):
        att_cols[row : row + 1, :] = square[matrix : matrix + 1, :]
    for matrix in range(2):
        first = ROW_EXPAND + 3 * matrix
        line = jnp.concatenate([sums[first + i : first + i + 1, :size] for i, (_, size) in enumerate(RUNS)], axis=1)
        line = line * (1.0 / D)
        exp_cols[matrix : matrix + 1, :] = line
        exp_new[matrix] = new_rows(exp_w[matrix], exp[matrix], line)
    line = sums[ROW_CONTRACT : ROW_CONTRACT + 1, :] * (1.0 / FF)
    con_cols[...] = line
    con_new[...] = new_rows(con_w[...], con[...], line)
    shift = lax.rem(D - me * 24, D)
    gains[...] = pltpu.roll(sums[8:16, :], shift, 1)[0:3, :24]
    turned = pltpu.roll(square, shift, 1)
    pairs[0] = pair_rows[...]
    pairs[1, 0:1, :] = turned[3:4, :24]
    pairs[1, 1:2, :] = turned[7:8, :24]
    lines = sums[16:24, :128].T
    row = lax.broadcasted_iota(jnp.int32, (8, HEADS), 0)
    column = lax.broadcasted_iota(jnp.int32, (8, HEADS), 1)
    total = jnp.zeros((BUCKETS, HEADS), F32)
    for h in range(2):
        pick = jnp.where(column == 2 * (row - (ROW_BUCKETS - 16)) + h, 1.0, 0.0)
        total = total + jnp.dot(
            lines[h * BUCKETS : (h + 1) * BUCKETS, :],
            pick,
            precision=lax.Precision.HIGHEST,
            preferred_element_type=F32,
        )
    buckets[...] = total


def hop(values, mask):
    return lax.ppermute(values, AXES, [(k, k ^ mask) for k in range(32)])


def after(values, *earlier):
    return lax.optimization_barrier((values,) + earlier)[0]


NEXT_Z = (1, 3, 0, 2)


def ring_hop(values):
    return lax.ppermute(values, AXES, [(k, NEXT_Z[k >> 3] * 8 + (k & 7)) for k in range(32)])


def ring_owner(me, steps, mask):
    z = lax.shift_right_logical(me, 3)
    inner = lax.bitwise_and(lax.bitwise_xor(z, lax.shift_right_logical(z, 1)), 1)
    distance = (0, 2 - inner, 3, 1 + inner)[steps]
    return lax.bitwise_xor(me, distance * 8 + mask)


def place_copies(plan, targets, ins, outs, sem):
    me = my_index()
    copies = []
    for ref, (slot, low_piece, high_piece) in zip(ins, plan):
        owner = ring_owner(me, *slot)
        for out, first, last, column in targets:
            begin, end = max(low_piece, first), min(high_piece, last)
            if begin >= end:
                continue
            pieces, into = pl.ds(begin - low_piece, end - begin), pl.ds(begin - first, end - begin)
            if column is None:
                pair = (ref.at[0, pieces], outs[out].at[into, owner])
            else:
                pair = (ref.at[0, pieces, column], outs[out].at[column, owner, into])
            copies.append(pltpu.make_async_copy(*pair, sem.at[len(copies)]))
    return copies


def place_kernel(plan, targets, count, *refs):
    copies = place_copies(plan, targets, refs[:count], refs[count:-1], refs[-1])
    for copy in copies:
        copy.start()
    for copy in copies:
        copy.wait()


def place(arrays, outs, targets):
    return call(
        functools.partial(place_kernel, [a[1:] for a in arrays], targets, len(arrays)),
        [(o, BF16) for o in outs],
        [pl.BlockSpec(memory_space=pl.ANY)] * len(arrays),
        [pltpu.with_memory_space_constraint(a[0], pltpu.HBM) for a in arrays],
        4.5,
        scratch=[pltpu.SemaphoreType.DMA((40 * len(targets),))],
        limit=24,
        spaces=[VMEM] * len(outs),
    )


def make_pieces(attention, expand, contract, gains):
    attention_pieces = attention.reshape(8, 24, COLS, WIDE).transpose(0, 2, 1, 3).reshape(24, 3, 8, WIDE)
    line = lax.dynamic_update_slice_in_dim(jnp.zeros((8, D), BF16), jnp.pad(gains, ((0, 5), (0, 0))), my_index() * 24, 1)
    gain_piece = line.reshape(1, 8, COLS, WIDE).transpose(0, 2, 1, 3)
    first = jnp.concatenate([attention_pieces, gain_piece])
    expand_pieces = expand.reshape(2, 24, BLOCKS, WIDE).transpose(0, 2, 1, 3).reshape(2, BLOCKS, 3, 8, WIDE)
    contract_pieces = contract.reshape(8, 8, COLS, WIDE).transpose(0, 2, 1, 3)
    second = jnp.concatenate([expand_pieces.reshape(2 * BLOCKS, 3, 8, WIDE), contract_pieces])
    return jnp.concatenate([first, second])


HALF = 24


def hop_xy(values):
    return hop(values, 1), hop(values, 4)


def corner_hops(by_x, by_y, *earlier):
    half_x, half_y = by_x[:, :HALF], by_y[:, HALF:]
    if earlier:
        half_x, half_y = lax.optimization_barrier((half_x, half_y) + earlier)[:2]
    return hop(half_x, 4), hop(half_y, 1)


def with_core(values, *earlier):
    return values, hop(after(values, *earlier) if earlier else values, 2)


def parts_of(steps, chunk, by_x, by_y, corner_x, corner_y):
    pieces = chunk[0].shape[1]
    plan = []
    for arrays, mask, first, last in (
        (chunk, 0, 0, pieces),
        (by_x, 1, 0, pieces),
        (by_y, 4, 0, pieces),
        (corner_x, 5, 0, HALF),
        (corner_y, 5, HALF, pieces),
    ):
        plan += [(arrays[core], (steps, mask + 2 * core), first, last) for core in range(2)]
    return plan


WIDE_SHAPES = [((16, 32, 3, 8, WIDE), BF16), ((COLS, 32, 8, 8, WIDE), BF16)]
WIDE_TARGETS = [(0, 25, 41, None)] + [(1, 41, 49, c) for c in range(COLS)]


def overlapping(arrays, first):
    return [a for a in arrays if a[3] > first]


def place_square(arrays):
    square, gains = place(
        [a for a in arrays if a[2] < 25],
        [(24, 32, 3, 8, WIDE), (1, 32, 3, 8, WIDE)],
        [(0, 0, 24, None), (1, 24, 25, None)],
    )
    return square.reshape(8, COLS, D, WIDE), gains


def gather_plain(attention, expand, contract, gains):
    attention, expand, contract, gains = (
        lax.all_gather(attention, AXES, axis=1, tiled=True),
        lax.all_gather(expand, AXES, axis=1, tiled=True),
        lax.all_gather(contract, AXES, axis=0, tiled=True),
        lax.all_gather(gains, AXES, axis=1, tiled=True),
    )
    return (
        attention.reshape(8, D, COLS, WIDE).transpose(0, 2, 1, 3),
        expand.reshape(2, D, BLOCKS, WIDE).transpose(0, 2, 1, 3),
        contract.reshape(FF, COLS, WIDE).transpose(1, 0, 2),
        gains,
    )


def total(*terms):
    result = terms[0].astype(F32)
    for term in terms[1:]:
        result = result + term.astype(F32)
    return result


class Scatter:
    def __init__(self, grads):
        self.own_a, self.own_b, self.sib_a, self.sib_b = grads

    def core(self, *earlier):
        if earlier:
            self.sib_a, self.sib_b = lax.optimization_barrier((self.sib_a, self.sib_b) + earlier)[:2]
        self.from_a, self.from_b = hop(self.sib_a, 2), hop(self.sib_b, 2)

    def pin(self, earlier):
        if earlier:
            self.own_a, self.own_b = lax.optimization_barrier((self.own_a, self.own_b) + earlier)[:2]

    def first(self, *earlier):
        self.pin(earlier)
        send_a = low(total(self.own_a[8:], self.from_a[8:]))
        send_b = low(total(self.own_b[8:], self.from_b[8:]))
        self.a1, self.b1 = hop(send_a, 4), hop(send_b, 1)
        return send_a, send_b

    def halves(self, part, slots):
        if part == 0:
            return total(self.own_a[slots], self.from_a[slots], self.a1[slots])
        return total(self.own_b[slots], self.from_b[slots], self.b1[slots])


class Finish:
    def __init__(self, groups):
        self.groups = groups

    def second(self, *earlier):
        for group in self.groups:
            group.pin(earlier)
        sends = [
            low(jnp.concatenate([group.halves(part, slice(4, 8)) for group in self.groups], axis=1))
            for part in range(2)
        ]
        self.a2, self.b2 = hop(sends[0], 1), hop(sends[1], 4)
        return tuple(sends)

    def sums(self, slots):
        arrays = []
        for part, last in enumerate((self.a2, self.b2)):
            mine = jnp.concatenate([group.halves(part, slots) for group in self.groups], axis=1)
            arrays.append(mine + last[slots].astype(F32))
        return jnp.concatenate(arrays, axis=1)

    def third(self, *earlier):
        for group in self.groups:
            group.pin(earlier)
        self.mine = self.sums(slice(0, 4))
        send = low(self.mine[1:3])
        self.near = hop(send, 8)
        return (send,)

    def fourth(self, *earlier):
        mine = after(self.mine, *earlier)
        send = low(mine[3:4] + self.near[1:2].astype(F32))
        self.parts = [self.mine, self.near, hop(send, 24)]
        return (send,)

    def third_direct(self, *earlier):
        for group in self.groups:
            group.pin(earlier)
        self.mine = self.sums(slice(0, 4))
        send = low(self.mine)
        self.parts = [self.mine] + [hop(send[d : d + 1], 8 * d) for d in (1, 3, 2)]
        return (send,)


def scatter_plain(pieces, shape, axis):
    count = pieces.shape[0]
    if axis == 0:
        whole = pieces.transpose(1, 0, 2).reshape(shape)
    else:
        per = shape[2] // WIDE
        whole = pieces.reshape(shape[0], per, shape[1], WIDE).transpose(0, 2, 1, 3).reshape(shape)
    return lax.psum_scatter(whole, AXES, scatter_dimension=axis, tiled=True)


def sum_ring(values):
    values = values + hop(values, 2)
    values = (values + hop(values, 1)) + (hop(values, 4) + hop(values, 5))
    return (values + hop(values, 8)) + (hop(values, 16) + hop(values, 24))


def factored_stats(grad_shard, total_rows):
    squares = grad_shard * grad_shard + TINY
    return (jnp.mean(squares, axis=-1), jnp.sum(squares, axis=-2) / total_rows)


def factored_update(weight_shard, grad_shard, row_stat, column_stat):
    scale = jnp.mean(column_stat, axis=-1, keepdims=True)[..., None]
    second = row_stat[..., :, None] * column_stat[..., None, :] / scale
    return weight_shard.astype(F32) - STEP_RATE * grad_shard * lax.rsqrt(second)


def without_outputs(stats):
    return jnp.concatenate([stats[0:3], stats[4:7]], axis=0)


def output_pair(stats):
    return jnp.stack([stats[3], stats[7]])


def on_device(
    ring,
    tokens,
    memory,
    target_segments,
    memory_segments,
    attention_weights,
    expand_weights,
    contract_weights,
    norm_gains,
    bucket_table,
    cotangent,
):
    rows = tokens.shape[0]
    spread_buckets = jnp.asarray(diagonal_onehot())
    lines = jnp.dot(
        bucket_table.T.astype(F32), jnp.asarray(tile_onehot()).T, precision=lax.Precision.HIGHEST
    ) + jnp.where(jnp.arange(3 * QROWS) // QROWS == 1, NEG_FILL, 0.0)
    far = jnp.pad(bucket_table[BUCKETS - 1].reshape(PAIRS, 1, 2), ((0, 0), (0, 0), (FAR_LANE, 126 - FAR_LANE)))
    act, act32 = ((rows, D), BF16), ((rows, D), F32)
    none = [None]
    query_mask, self_mask, cross_mask, near_bias = call(
        prepare_kernel,
        [((rows // QROWS, 2 * QROWS, 128), BF16), ((rows, 128), BF16), ((rows, 128), BF16)]
        + [((PAIRS, 2 * QROWS, 2 * QROWS), F32)],
        none * 3,
        (target_segments.reshape(1, rows), memory_segments.reshape(1, rows), lines),
        0.8,
    )
    head_acc = VMEM((rows, 128), F32)

    if ring:
        first = make_pieces(attention_weights, expand_weights, contract_weights, norm_gains)[None]
        r1 = ring_hop(first)
        x0, y0 = hop_xy(first)
        x1, y1 = hop_xy(r1)
        r2 = ring_hop(after(r1, near_bias, x0, y0))
        a0, b0 = corner_hops(x0, y0)
        r3 = ring_hop(r2)
        x2, y2 = hop_xy(after(r2, x1, y1))
        a1, b1 = corner_hops(x1, y1, a0, b0)
        x3, y3 = hop_xy(after(r3, x2, y2))
        a2, b2 = corner_hops(x2, y2, x3)
        a3, b3 = corner_hops(x3, y3)
        parts = []
        for steps, chunk, waits in (
            (0, (first, x0, y0, a0, b0), (x1, y1)),
            (1, (r1, x1, y1, a1, b1), (x2, y2)),
            (2, (r2, x2, y2, a2, b2), (x3, y3)),
            (3, (r3, x3, y3, a3, b3), ()),
        ):
            parts += parts_of(steps, *(with_core(values, *waits) for values in chunk))
        square, gains_in = place_square(parts)
        parts = overlapping(parts, 25)
    else:
        square, wide, narrow, gains_in = gather_plain(
            attention_weights, expand_weights, contract_weights, norm_gains
        )
    resident = ()
    if ring:
        square = in_vmem(square)

    n1, q, k, v, kc, vc, gains = call(
        functools.partial(pre_kernel, ring),
        [act] * 6 + [((8, D), F32)],
        none * 5,
        (tokens, memory, gains_in, square, square),
        3.4,
    )
    lse_shape = ((PAIRS, rows // QROWS, 2 * QROWS), F32)
    args = (q, k, v, near_bias, query_mask, self_mask, far)
    specs = [pair_spec(3)] * 3 + [near_spec(3), None, None, far_spec(3)]
    if ring:
        arrays = [pltpu.with_memory_space_constraint(a[0], pltpu.HBM) for a in parts]
        copies = functools.partial(place_copies, [a[1:] for a in parts], WIDE_TARGETS)
        ctxs, lse_self, wide, narrow = call(
            functools.partial(self_forward_kernel, copies, len(arrays)),
            [act, lse_shape] + WIDE_SHAPES,
            specs + [pl.BlockSpec(memory_space=pl.ANY)] * len(arrays),
            (*args, *arrays),
            5.0,
            grid=(PAIRS // 3,),
            scratch=[pltpu.SemaphoreType.DMA((len(arrays) * len(WIDE_TARGETS),))],
            out_specs=[pair_spec(3), lse_spec(3), None, None],
            spaces=[jax.ShapeDtypeStruct] * 2 + [VMEM] * 2,
        )
        wide = in_vmem(wide.reshape(2, BLOCKS, D, WIDE))
        narrow = in_vmem(narrow.reshape(COLS, FF, WIDE))
        resident = wide, narrow
    else:
        ctxs, lse_self = call(
            functools.partial(self_forward_kernel, None, 0),
            [act, lse_shape],
            specs,
            args,
            5.0,
            grid=(PAIRS // 3,),
            out_specs=[pair_spec(3), lse_spec(3)],
        )
    res1, n2, qc = call(
        mid_kernel, [act32, act, act], none * 4, (ctxs, tokens, gains, square), 1.9, resident=resident
    )
    ctxc, lse_cross = call(
        cross_forward_kernel,
        [act, lse_shape],
        [pair_spec(PAIRS)] * 3 + [None, None],
        (qc, kc, vc, query_mask, cross_mask),
        5.8,
        grid=(1,),
        out_specs=[pair_spec(PAIRS), lse_spec(PAIRS)],
        resident=resident,
    )
    res2, n3 = call(late_kernel, [act32, act], none * 4, (ctxc, res1, gains, square), 1.0, resident=resident)
    half = BLOCKS // 2
    hidden_shape = ((rows, FF // 2), BF16)
    if ring:
        grad_outs = grad_shapes(ring, False, half, half), grad_shapes(ring, False, half + 4, half + 4)
        more = [VMEM((2, FF, WIDE), F32)], 20
    else:
        grad_outs = [((half, D, WIDE), F32)] * 2
        grad_outs = [
            (outs, [jax.ShapeDtypeStruct] * len(outs), none * len(outs))
            for outs in (grad_outs, grad_outs + [((COLS, FF, WIDE), F32)])
        ]
        more = [VMEM((2, FF, WIDE), F32)], 40
    plain = [jax.ShapeDtypeStruct] * 3
    middle, dn3, hidden, *first_grads = call(
        functools.partial(ffn_kernel, ring, False),
        [act32, act32, hidden_shape] + grad_outs[0][0],
        none * 7,
        (n3, res2, res2, n3, cotangent, wide, narrow),
        8.0,
        scratch=send_scratch(ring, False),
        limit=more[1],
        spaces=plain + grad_outs[0][1],
        out_specs=none * 3 + grad_outs[0][2],
    )
    if ring:
        ffn_one = Scatter(first_grads)
        ffn_one.core()
        middle = after(middle, *ffn_one.first())
    output, dn3, _, *last_grads = call(
        functools.partial(ffn_kernel, ring, True),
        [act, act32, hidden_shape] + grad_outs[1][0],
        none * 7,
        (n3, middle, dn3, hidden, cotangent, wide, narrow),
        13.0,
        scratch=send_scratch(ring, False) + more[0],
        limit=more[1],
        spaces=plain + grad_outs[1][1],
        out_specs=none * 3 + grad_outs[1][2],
    )
    if ring:
        ffn_two = Scatter(last_grads)
        first_half, ffn = Finish([ffn_one]), Finish([ffn_two])
        sent = first_half.second(dn3)
        ffn_two.core(ffn_one.a1, ffn_one.b1)
        dn3 = after(dn3, *sent)
    r2g, ccg, gain_three = call(
        third_back_kernel,
        [act32, act, ((1, D), F32)],
        none * 5,
        (dn3, res2, cotangent, gains, square),
        1.3,
    )
    if ring:
        ccg = after(ccg, *ffn_two.first(r2g))
    dqc, dkc, dvc = call(
        cross_back_kernel,
        [act] * 3,
        [pair_spec(PAIRS)] * 5 + [lse_spec(PAIRS), None, None],
        (qc, kc, vc, ccg, ctxc, lse_cross, query_mask, cross_mask),
        8.8,
        grid=(1,),
        scratch=[head_acc, head_acc],
        out_specs=[pair_spec(PAIRS)] * 3,
    )
    if ring:
        dkc = after(dkc, *first_half.third(dqc))
    shapes = grad_shapes(ring, False, 6)
    memory_grad, *cross_a = call(
        functools.partial(memory_grads_kernel, ring),
        [act] + shapes[0],
        none * 4,
        (dkc, dvc, memory, square),
        3.9,
        scratch=send_scratch(ring, False),
        spaces=plain[:1] + shapes[1],
        out_specs=none + shapes[2],
    )
    dqc = after(dqc, memory_grad)
    r1g, csg, gain_two = call(
        second_back_kernel,
        [act32, act, ((1, D), F32)],
        none * 5,
        (dqc, res1, r2g, gains, square),
        3.0,
    )
    shapes = grad_shapes(ring, False, 9)
    cross_b = call(
        functools.partial(middle_grads_kernel, ring),
        shapes[0],
        none * 6,
        (dqc, n2, r1g, ctxs, r2g, ctxc),
        2.5,
        scratch=send_scratch(ring, False),
        spaces=shapes[1],
        out_specs=shapes[2],
    )
    if ring:
        cross = Scatter([cross_a[0], cross_b[0], cross_a[1], cross_b[1]])
        cross.core(ffn_two.a1, ffn_two.b1)
        rest = Finish([cross])
        csg = after(csg, *ffn.second(cross_b[0]), *first_half.fourth(cross_b[0]))
    dqs, dks, dvs, near_sum, far_sum = call(
        self_back_kernel,
        [act] * 3 + [((PAIRS, 2 * QROWS, 2 * QROWS), F32), ((PAIRS, 8, 2 * QROWS), F32)],
        [pair_spec(PAIRS)] * 5 + [lse_spec(PAIRS), near_spec(PAIRS), None, None, far_spec(PAIRS)],
        (q, k, v, csg, ctxs, lse_self, near_bias, query_mask, self_mask, far),
        8.1,
        grid=(1,),
        scratch=[head_acc, head_acc],
        out_specs=[pair_spec(PAIRS)] * 3 + [near_spec(PAIRS), step_spec(PAIRS, 8, 2 * QROWS)],
    )
    if ring:
        dqs = after(dqs, *cross.first(dqs), *ffn.third(dqs))
    shapes = grad_shapes(ring, False, 5, 4)
    self_grads = call(
        functools.partial(first_grads_kernel, ring),
        shapes[0],
        none * 4,
        (dqs, dks, dvs, n1),
        2.5,
        scratch=send_scratch(ring, False),
        spaces=shapes[1],
        out_specs=shapes[2],
    )
    if ring:
        own = Scatter(self_grads)
        dks = after(dks, self_grads[0])
    input_grad, gain_one = call(
        first_back_kernel,
        [act, ((1, D), F32)],
        none * 7,
        (dqs, dks, dvs, tokens, r1g, gains, square),
        3.4,
    )
    if ring:
        last = Finish([own])
        own.core(ffn.a2, ffn.b2)
        sent = ffn.fourth(input_grad)
        sent = rest.second(*sent)
        sent = own.first(*sent)
        sent = rest.third_direct(*sent)
        sent = last.second(*sent)
        last.third_direct(*sent)
    diag = call(
        diagonals_kernel,
        [((PAIRS, 2, 2 * QROWS), F32)],
        none * 2,
        (after(near_sum, input_grad), far_sum),
        3.0,
    )[0]
    gain_parts = (gain_one, gain_two, gain_three)
    if ring:
        parts = []
        for group in (first_half, ffn, rest, last):
            parts += group.parts
        attention_grad, expand_grad, contract_grad, sums = call(
            functools.partial(share_kernel, [len(group.parts) for group in (first_half, ffn, rest, last)]),
            [((8, 24, D), F32), ((2, 24, FF), F32), ((64, D), F32), ((SUM_ROWS, D), F32)],
            none * (len(parts) + 5),
            (*parts, *gain_parts, diag, spread_buckets),
            1.5,
        )
        sums = sum_ring(sums)
        attention_rows, expand_rows, contract_rows, pair_rows = call(
            rows_kernel,
            [((6, 24), F32), ((2, 24), F32), ((1, 64), F32), ((2, 24), F32)],
            none * 3,
            (attention_grad, expand_grad, contract_grad),
            0.8,
        )
        (
            attention_new,
            expand_new,
            contract_new,
            attention_columns,
            expand_columns,
            contract_columns,
            gains_grad,
            projection_statistics,
            bucket_grad,
        ) = call(
            update_kernel,
            [
                ((8, 24, D), F32),
                ((2, 24, FF), F32),
                ((64, D), F32),
                ((6, D), F32),
                ((2, FF), F32),
                ((1, D), F32),
                ((3, 24), F32),
                ((2, 2, 24), F32),
                ((BUCKETS, HEADS), F32),
            ],
            none * 8,
            (sums, pair_rows, attention_grad, expand_grad, contract_grad, attention_weights, expand_weights, contract_weights),
            1.4,
        )
        contract_rows, contract_columns = contract_rows.reshape(64), contract_columns.reshape(D)
    else:
        bucket_part = jnp.dot(
            spread_buckets.T,
            diag.reshape(HEADS, 2 * QROWS).T,
            precision=lax.Precision.HIGHEST,
            preferred_element_type=F32,
        )
        pieces = jnp.concatenate([self_grads[0], cross_b[0][:6], cross_a[0], cross_b[0][6:]])
        attention_grad = scatter_plain(pieces, (8, D, D), 1)
        expand_pieces = jnp.stack([jnp.concatenate([first_grads[i], last_grads[i]]) for i in range(2)])
        expand_grad = scatter_plain(expand_pieces, (2, D, FF), 1)
        contract_grad = scatter_plain(last_grads[2], (FF, D), 0)
        attention_rows, attention_part = factored_stats(attention_grad, D)
        expand_rows, expand_part = factored_stats(expand_grad, D)
        contract_rows, contract_part = factored_stats(contract_grad, FF)
        attention_columns, expand_columns, contract_columns, bucket_grad, gains_sum = lax.psum(
            (attention_part, expand_part, contract_part, bucket_part, jnp.concatenate(gain_parts)), AXES
        )
        attention_new = factored_update(attention_weights, attention_grad, attention_rows, attention_columns)
        expand_new = factored_update(expand_weights, expand_grad, expand_rows, expand_columns)
        contract_new = factored_update(contract_weights, contract_grad, contract_rows, contract_columns)
        share_width = attention_rows.shape[1]
        share_start = lax.axis_index(AXES) * share_width
        column_share = lax.dynamic_slice_in_dim(attention_columns, share_start, share_width, 1)
        gains_grad = lax.dynamic_slice_in_dim(gains_sum, share_start, share_width, 1)
        projection_statistics = jnp.stack([output_pair(attention_rows), output_pair(column_share)])
        attention_rows, attention_columns = without_outputs(attention_rows), without_outputs(attention_columns)
    return (
        output,
        input_grad,
        memory_grad,
        attention_grad,
        expand_grad,
        contract_grad,
        gains_grad,
        bucket_grad,
        attention_rows,
        attention_columns,
        expand_rows,
        expand_columns,
        contract_rows,
        contract_columns,
        attention_new,
        expand_new,
        contract_new,
        projection_statistics,
    )


def solution(mesh):
    ring = dict(mesh.shape) == {"wide": 16, "narrow": 2}
    rows, both = P(AXES, None), P(None, AXES, None)
    placed = (rows, rows, P(AXES), P(AXES), both, both, rows, P(None, AXES), P(), rows)
    return jax.shard_map(
        functools.partial(on_device, ring),
        mesh=mesh,
        in_specs=placed,
        out_specs=(
            rows,
            rows,
            rows,
            both,
            both,
            rows,
            P(None, AXES),
            P(),
            P(None, AXES),
            P(),
            P(None, AXES),
            P(),
            P(AXES),
            P(),
            both,
            both,
            rows,
            P(None, None, AXES),
        ),
        check_vma=False,
    )
```

```python
import functools
import math

import jax
import jax.numpy as jnp
import numpy as np
from jax import lax
from jax.experimental import pallas as pl
from jax.experimental.pallas import tpu as pltpu
from jax.sharding import PartitionSpec as P

D = 768
HEADS = 12
FF = 2048
BUCKETS = 32
MAX_DIST = 128
TGT_LEN = 512
MEM_LEN = 512
WIDE = 256
COLS = D // WIDE
BLOCKS = FF // WIDE
PAIRS = HEADS // 2
QROWS = 128

NEG_FILL = -(2.0**30)
DOCS = 4
FAR_LANE = 8
EPSILON = 1e-06
TINY = 1e-30
STEP_RATE = 0.01
AXES = ("wide", "narrow")
F32 = jnp.float32
BF16 = jnp.bfloat16
MIB = 1024 * 1024
VMEM = pltpu.VMEM


def bucket_onehot(length, bucket_count, far_limit):
    exact_span = bucket_count // 2
    onehot_rows = np.zeros((length, bucket_count), np.float32)
    for distance in range(length):
        if distance < exact_span:
            bucket_id = distance
        else:
            bucket_id = min(
                bucket_count - 1,
                exact_span
                + int(
                    math.log(distance / exact_span)
                    / math.log(far_limit / exact_span)
                    * (bucket_count - exact_span)
                ),
            )
        onehot_rows[distance, bucket_id] = 1.0
    return onehot_rows


def diagonal_onehot():
    t = np.arange(2 * QROWS)
    distance = np.where(t <= QROWS, QROWS - t, 3 * QROWS - t)
    return bucket_onehot(TGT_LEN, BUCKETS, MAX_DIST)[distance]


def tile_onehot():
    t = np.arange(3 * QROWS)
    distance = np.where(t < QROWS, QROWS + t, t - 2 * QROWS)
    rows = bucket_onehot(TGT_LEN, BUCKETS, MAX_DIST)[np.maximum(distance, 0)]
    rows[:, BUCKETS - 1] -= 1.0
    return np.where((distance >= 0)[:, None], rows, 0.0).astype(np.float32)


def mm(left, right):
    return jnp.dot(left, right, preferred_element_type=F32)


def mm_nt(left, right):
    return lax.dot_general(left, right, (((1,), (1,)), ((), ())), preferred_element_type=F32)


def mm_tn(left, right):
    return lax.dot_general(left, right, (((0,), (0,)), ((), ())), preferred_element_type=F32)


def low(values):
    return values.astype(BF16)


def cols(index):
    return slice(index * WIDE, (index + 1) * WIDE)


def inverse_rms(values):
    return lax.rsqrt(jnp.mean(values * values, axis=-1, keepdims=True) + EPSILON)


def norm_back(values, gain, grad):
    scale = inverse_rms(values)
    gain_grad = jnp.sum(values * scale * grad, axis=0, keepdims=True)
    scaled = gain * grad
    inner = jnp.mean(values * scaled, axis=-1, keepdims=True)
    return scale * scaled - values * (scale * scale * scale * inner), gain_grad


def my_index():
    return lax.axis_index("wide") * 2 + lax.axis_index("narrow")


def in_vmem(values):
    return pltpu.with_memory_space_constraint(values, pltpu.VMEM)


RATE = 1.15e9
SCALE = 1.0


def call(body, outs, in_specs, args, us, grid=None, scratch=(), limit=20, out_specs=None, spaces=None, resident=()):
    kwargs = {} if grid is None else {"grid": grid}
    whole = pl.BlockSpec(memory_space=VMEM)
    count, inner = len(args), body
    if resident:
        args, in_specs = (*args, *resident), [*in_specs, *[None] * len(resident)]
        body = lambda *refs: inner(*refs[:count], *refs[count + len(resident) :])
    spaces = spaces or [jax.ShapeDtypeStruct] * len(outs)
    return pl.pallas_call(
        body,
        out_shape=[space(*o) for space, o in zip(spaces, outs)],
        in_specs=[whole if s is None else s for s in in_specs],
        out_specs=[whole] * len(outs) if out_specs is None else [whole if s is None else s for s in out_specs],
        scratch_shapes=list(scratch),
        compiler_params=pltpu.CompilerParams(vmem_limit_bytes=limit * MIB),
        cost_estimate=pl.CostEstimate(flops=int(us * RATE * SCALE), bytes_accessed=1, transcendentals=0),
        **kwargs,
    )(*args)


def slot_mask(first, slot):
    high, mid, z = slot >> 3, (slot >> 2) & 1, slot & 3
    dy, dx = (high, mid) if first == 0 else (mid, high)
    return z * 8 + dy * 4 + dx


BUFFERS = 4


class Sender:
    def __init__(self, acc, stage=None, sem=None):
        self.acc, self.stage, self.sem = acc, stage, sem
        self.count, self.pending = 0, [[] for _ in range(BUFFERS)]

    def turn(self):
        buffer = self.count % BUFFERS
        self.count += 1
        for copy in self.pending[buffer]:
            copy.wait()
        self.pending[buffer] = []
        return buffer

    def start(self, buffer, source, target):
        index = len(self.pending[buffer])
        copy = pltpu.make_async_copy(source, target, self.sem.at[buffer, index])
        copy.start()
        self.pending[buffer].append(copy)

    def finish(self):
        for pending in self.pending:
            for copy in pending:
                copy.wait()

    def matrix(self, own, sib, first, piece, value):
        buffer = self.turn()
        held = self.acc.at[buffer % self.acc.shape[0]]
        held[...] = value
        me = my_index()
        for index, (out, core) in enumerate(((own, 0), (sib, 2))):
            for slot in range(16):
                owner = lax.bitwise_xor(me, slot_mask(first, slot) + core)
                rows = held[pl.ds(pl.multiple_of(owner * 24, 8), 24), :]
                rows = low(rows.reshape(3, 8, WIDE))
                if self.stage is None:
                    out[slot, piece] = rows
                else:
                    self.stage[buffer, index, slot] = rows
            if self.stage is not None:
                self.start(buffer, self.stage.at[buffer, index], out.at[:, piece])

    def contract(self, outs, column, start, value_of):
        buffer = self.turn()
        me = my_index()
        for index, out in enumerate(outs):
            first, core = index % 2, index // 2 * 2
            for slot in range(16):
                owner = lax.bitwise_xor(me, slot_mask(first, slot) + core)
                rows = value_of(pl.ds(pl.multiple_of(owner * 64 + first * 32, 8), 32))
                out[slot, start : start + 4, column] = low(rows.reshape(4, 8, WIDE))


def send_scratch(ring, staged):
    if not ring:
        return []
    acc = [VMEM((2, D, WIDE), F32)]
    if not staged:
        return acc
    return acc + [VMEM((BUFFERS, 2, 16, 3, 8, WIDE), BF16), pltpu.SemaphoreType.DMA((BUFFERS, 2))]


def grad_shapes(ring, staged, *pieces):
    if not ring:
        return [((sum(pieces), D, WIDE), F32)], [jax.ShapeDtypeStruct], [None]
    shapes = [((16, n, 3, 8, WIDE), BF16) for n in pieces] * 2
    space, spec = (pltpu.HBM, pl.BlockSpec(memory_space=pl.ANY)) if staged else (VMEM, None)
    return shapes, [space] * len(shapes), [spec] * len(shapes)


def pre_kernel(ring, tok, mem, gains_in, w, wm, n1, q, k, v, kc, vc, gains):
    if ring:
        for c in range(COLS):
            gains[:, cols(c)] = jnp.sum(gains_in[0, :, c].astype(F32), axis=0)
    else:
        gains[...] = jnp.concatenate([gains_in[...].astype(F32), jnp.zeros((5, D), F32)], axis=0)
    x = tok[...].astype(F32)
    normed = low(x * inverse_rms(x) * gains[0:1, :])
    n1[...] = normed
    memory = mem[...]
    for c in range(COLS):
        q[:, cols(c)] = low(mm(normed, w[0, c]))
        k[:, cols(c)] = low(mm(normed, w[1, c]))
        v[:, cols(c)] = low(mm(normed, w[2, c]))
        kc[:, cols(c)] = low(mm(memory, wm[5, c]))
        vc[:, cols(c)] = low(mm(memory, wm[6, c]))


def halves(block):
    lane = lax.broadcasted_iota(jnp.int32, block.shape, 1)
    zero = jnp.zeros_like(block)
    return jnp.concatenate([jnp.where(lane < 64, block, zero), jnp.where(lane < 64, zero, block)], axis=0)


def prepare_kernel(target, memory, line, query_mask, self_mask, cross_mask, near):
    document = lax.broadcasted_iota(jnp.int32, (128, target.shape[1]), 0)
    real = document < DOCS
    self_mask[...] = low(jnp.where(real & (document == target[...]), 1.0, 0.0).T)
    cross_mask[...] = low(jnp.where(real & (document == memory[...]), 1.0, 0.0).T)
    other = jnp.where(real & (document != target[...]), NEG_FILL, 0.0).T
    lane = lax.broadcasted_iota(jnp.int32, (QROWS, 128), 1)
    for block in range(TGT_LEN // QROWS):
        for h in range(2):
            rows = other[block * QROWS : (block + 1) * QROWS, :]
            query_mask[block, h * QROWS : (h + 1) * QROWS, :] = low(jnp.where(lane == FAR_LANE + h, 1.0, rows))
    for head in range(HEADS):
        tile = jnp.broadcast_to(line[head : head + 1, :], (2 * QROWS, 3 * QROWS))
        tile = pltpu.roll(tile, 0, 1, stride=1, stride_axis=0)[:, :QROWS]
        near[head // 2, :, (head % 2) * QROWS : (head % 2 + 1) * QROWS] = tile


def add_near(scores, near, pair, block):
    if block == 0:
        return scores + near[pair, QROWS:, :]
    start = scores.shape[0] - 2 * QROWS
    if start == 0:
        return scores + near[pair]
    return jnp.concatenate([scores[:start], scores[start:] + near[pair]], axis=0)


def pair_columns(turned):
    return jnp.concatenate([turned[:64, :QROWS], turned[64:128, QROWS:]], axis=0)


def lanes(pair):
    return slice(pair * 128, (pair + 1) * 128)


def rows_of(block):
    return slice(block * QROWS, (block + 1) * QROWS)


def masked_keys(k, key_mask, far, pair):
    mask = key_mask[...] if far is None else key_mask[...] + far[pair]
    return jnp.concatenate([k[:, lanes(pair)], mask], axis=1)


def ahead(make, items, depth):
    ready = [make(item) for item in items[:depth]]
    for index, item in enumerate(items):
        if index + depth < len(items):
            ready.append(make(items[index + depth]))
        yield item, ready.pop(0)


def with_ones(values):
    turned = values.T
    return jnp.concatenate([turned, jnp.ones((16, turned.shape[1]), turned.dtype)], axis=0)


def attend_forward(q, k, v, near, query_mask, key_mask, far, out, lse):
    count = q.shape[1] // 128
    keys = [masked_keys(k, key_mask, far, pair) for pair in range(count)]
    values_t = [with_ones(v[:, lanes(pair)]) for pair in range(count)]
    items = [(pair, block) for pair in range(count) for block in range(TGT_LEN // QROWS)]

    def make(item):
        pair, block = item
        end = MEM_LEN if near is None else (block + 1) * QROWS
        queries = jnp.concatenate([halves(q[rows_of(block), lanes(pair)]), query_mask[block]], axis=1)
        return mm_nt(keys[pair][:end], queries)

    for (pair, block), scores in ahead(make, items, 2):
        if near is not None:
            scores = add_near(scores, near, pair, block)
        top = jnp.max(scores, axis=0, keepdims=True)
        raised = low(jnp.exp(scores - top))
        context = mm(values_t[pair][:, : scores.shape[0]], raised)
        sums = context[128:129, :]
        lse[pair, block : block + 1, :] = top + jnp.log(sums)
        context = pair_columns(context * (1.0 / sums))
        out[rows_of(block), lanes(pair)] = low(context.T)


def self_forward_kernel(copies, count, q, k, v, near, query_mask, key_mask, far, *rest):
    out, lse = rest[count : count + 2]
    if copies is not None:
        started = copies(rest[:count], rest[count + 2 : -1], rest[-1])

        @pl.when(pl.program_id(0) == 0)
        def _():
            for copy in started:
                copy.start()

    attend_forward(q, k, v, near, query_mask, key_mask, far, out, lse)
    if copies is not None:

        @pl.when(pl.program_id(0) == pl.num_programs(0) - 1)
        def _():
            for copy in started:
                copy.wait()


def cross_forward_kernel(q, k, v, query_mask, key_mask, out, lse):
    attend_forward(q, k, v, None, query_mask, key_mask, None, out, lse)


def pair_spec(pairs):
    return pl.BlockSpec((TGT_LEN, 128 * pairs), lambda p: (0, p))


def step_spec(pairs, *dims):
    return pl.BlockSpec((pairs, *dims), lambda p: (p, 0, 0))


def near_spec(pairs):
    return step_spec(pairs, 2 * QROWS, 2 * QROWS)


def lse_spec(pairs):
    return step_spec(pairs, TGT_LEN // QROWS, 2 * QROWS)


def far_spec(pairs):
    return step_spec(pairs, 1, 128)


def mid_kernel(ctx, tok, gains, w, res, n2, qc):
    context = ctx[...]
    for c in range(COLS):
        res[:, cols(c)] = tok[:, cols(c)].astype(F32) + mm(context, w[3, c])
    x = res[...]
    normed = low(x * inverse_rms(x) * gains[1:2, :])
    n2[...] = normed
    for c in range(COLS):
        qc[:, cols(c)] = low(mm(normed, w[4, c]))


def late_kernel(ctx, res1, gains, w, res2, n3):
    context = ctx[...]
    for c in range(COLS):
        res2[:, cols(c)] = res1[:, cols(c)] + mm(context, w[7, c])
    x = res2[...]
    n3[...] = low(x * inverse_rms(x) * gains[2:3, :])


def gelu_pair(gate):
    rate = math.sqrt(2.0 / math.pi)
    square = gate * gate
    bend = jnp.tanh(rate * gate * (1.0 + 0.044715 * square))
    half = 0.5 * (1.0 + bend)
    slope = half + 0.5 * gate * (1.0 - bend * bend) * rate * (1.0 + 3.0 * 0.044715 * square)
    return gate * half, slope


def ffn_kernel(ring, last, n3, before, dn3_before, hidden_before, cot, wide, narrow, out, dn3, hidden, *rest):
    half = BLOCKS // 2
    if ring:
        grads, rest = rest[:4], rest[4:]
        own_a, own_b, sib_a, sib_b = grads
        sender = Sender(rest[0])
    else:
        grads = rest[:3] if last else rest[:2]
    blocks = list(range(half, BLOCKS)) if last else list(range(half))
    normed, turned = n3[...], n3[...].T
    span = slice(blocks[0] * WIDE, (blocks[-1] + 1) * WIDE)

    def make(block):
        rows = slice(block * WIDE, (block + 1) * WIDE)
        back = mm_nt(cot[:, cols(0)], narrow[0, rows, :])
        for c in range(1, COLS):
            back = back + mm_nt(cot[:, cols(c)], narrow[c, rows, :])
        return mm(normed, wide[0, block]), mm(normed, wide[1, block]), back

    for index, (block, (gate, lift, back)) in enumerate(ahead(make, blocks, 1)):
        active, slope = gelu_pair(gate)
        hidden[:, cols(index)] = low(active * lift)
        gate_grad = low(back * lift * slope)
        lift_grad = low(back * active)
        part = mm_nt(gate_grad, wide[0, block]) + mm_nt(lift_grad, wide[1, block])
        if index == 0:
            dn3[...] = dn3_before[...] + part if last else part
        else:
            dn3[...] += part
        if ring:
            sender.matrix(own_a, sib_a, 0, index, mm(turned, gate_grad))
            sender.matrix(own_b, sib_b, 1, index, mm(turned, lift_grad))
        else:
            grads[0][index] = mm(turned, gate_grad)
            grads[1][index] = mm(turned, lift_grad)
    for c in range(COLS):
        total = before[:, cols(c)] + mm(hidden[...], narrow[c, span, :])
        out[:, cols(c)] = low(total) if last else total
    if last:
        con_acc = rest[-1]
        first_t, last_t = hidden_before[...].T, hidden[...].T
        for c in range(COLS):
            for rows, left in ((slice(0, FF // 2), first_t), (slice(FF // 2, FF), last_t)):
                con_acc[c % 2, rows, :] = mm(left, cot[:, cols(c)])
            if ring:
                sender.contract((own_a, own_b, sib_a, sib_b), c, half, lambda rows, c=c: con_acc[c % 2, rows, :])
            else:
                grads[2][c] = con_acc[c % 2]
    if ring:
        sender.finish()


def third_back_kernel(dn3, res2, cot, gains, w, r2g, ccg, gg):
    back, gain_grad = norm_back(res2[...], gains[2:3, :], dn3[...])
    gg[...] = gain_grad
    grad = cot[...].astype(F32) + back
    r2g[...] = grad
    cross_low = low(grad)
    total = mm_nt(cross_low[:, cols(0)], w[7, 0])
    for c in range(1, COLS):
        total = total + mm_nt(cross_low[:, cols(c)], w[7, c])
    ccg[...] = low(total)


def attend_backward(q, k, v, dc, o, lse, near, query_mask, key_mask, far, dq, dk, dv, dk_acc, dv_acc, near_sum, far_sum):
    count = q.shape[1] // 128
    keys = [masked_keys(k, key_mask, far, pair) for pair in range(count)]
    keys_t = [k[:, lanes(pair)].T for pair in range(count)]
    items = [(pair, block) for pair in range(count) for block in range(TGT_LEN // QROWS)]

    def make(item):
        pair, block = item
        end = MEM_LEN if near is None else (block + 1) * QROWS
        queries, grads = halves(q[rows_of(block), lanes(pair)]), halves(dc[rows_of(block), lanes(pair)])
        scores = mm_nt(keys[pair][:end], jnp.concatenate([queries, query_mask[block]], axis=1))
        return end, queries, grads, scores, mm_nt(v[:end, lanes(pair)], grads)

    beyond = None
    for (pair, block), (end, queries, grads, scores, prob_grad) in ahead(make, items, 1):
        rows = rows_of(block)
        if near is not None:
            scores = add_near(scores, near, pair, block)
        probs = jnp.exp(scores - lse[pair, block : block + 1, :])
        inner = (dc[rows, lanes(pair)].astype(F32) * o[rows, lanes(pair)].astype(F32)).T
        inner = jnp.concatenate(
            [jnp.sum(inner[:64], axis=0, keepdims=True), jnp.sum(inner[64:], axis=0, keepdims=True)], axis=1
        )
        score_grad = low(probs * (prob_grad - inner))
        dk_part, dv_part = mm(score_grad, queries), mm(low(probs), grads)
        if block == 0:
            dk_acc[:end, :], dv_acc[:end, :] = dk_part, dv_part
        else:
            before = end if near is None else end - QROWS
            dk_acc[:before, :] += dk_part[:before]
            dv_acc[:before, :] += dv_part[:before]
            if before < end:
                dk_acc[before:end, :], dv_acc[before:end, :] = dk_part[before:], dv_part[before:]
        dq[rows, lanes(pair)] = low(pair_columns(mm(keys_t[pair][:, :end], score_grad)).T)
        if near is not None:
            wide = score_grad.astype(F32)
            if block == 0:
                near_sum[pair, :QROWS, :] = jnp.zeros((QROWS, 2 * QROWS), F32)
                near_sum[pair, QROWS:, :] = wide
                beyond = jnp.zeros((1, 2 * QROWS), F32)
            else:
                near_sum[pair] += wide[end - 2 * QROWS :, :]
            if block > 1:
                beyond = beyond + jnp.sum(wide[: end - 2 * QROWS, :], axis=0, keepdims=True)
            far_sum[pair] = jnp.broadcast_to(beyond, (8, 2 * QROWS))
        if block == TGT_LEN // QROWS - 1:
            dk[:, lanes(pair)] = low(dk_acc[...])
            dv[:, lanes(pair)] = low(dv_acc[...])


def cross_back_kernel(q, k, v, dc, o, lse, query_mask, key_mask, dq, dk, dv, dk_acc, dv_acc):
    attend_backward(
        q, k, v, dc, o, lse, None, query_mask, key_mask, None, dq, dk, dv, dk_acc, dv_acc, None, None
    )


def self_back_kernel(
    q, k, v, dc, o, lse, near, query_mask, key_mask, far, dq, dk, dv, near_sum, far_sum, dk_acc, dv_acc
):
    attend_backward(
        q, k, v, dc, o, lse, near, query_mask, key_mask, far, dq, dk, dv, dk_acc, dv_acc, near_sum, far_sum
    )


def diagonal_sums(grid):
    width = 2 * QROWS
    group = grid[:8, :]
    for shift in range(8, QROWS, 8):
        group = group + pltpu.roll(grid[shift : shift + 8, :], width - shift, 1)
    row = lax.broadcasted_iota(jnp.int32, group.shape, 0)
    for bit in (1, 2, 4):
        group = jnp.where((row & bit) != 0, pltpu.roll(group, width - bit, 1), group)
    return jnp.sum(group, axis=0, keepdims=True)


def diagonals_kernel(near_sum, far_sum, diag):
    lane = lax.broadcasted_iota(jnp.int32, (1, 2 * QROWS), 1)
    for pair in range(PAIRS):
        for h in range(2):
            part = slice(h * QROWS, (h + 1) * QROWS)
            beyond = jnp.sum(far_sum[pair, 0:1, part], keepdims=True)
            diag[pair, h : h + 1, :] = diagonal_sums(near_sum[pair, :, part].T) + jnp.where(lane == 0, beyond, 0.0)


def second_back_kernel(dq, res1, r2g, gains, w, r1g, csg, gg):
    query_grad = dq[...]
    back = mm_nt(query_grad[:, cols(0)], w[4, 0])
    for c in range(1, COLS):
        back = back + mm_nt(query_grad[:, cols(c)], w[4, c])
    moved, gain_grad = norm_back(res1[...], gains[1:2, :], back)
    gg[...] = gain_grad
    grad = r2g[...] + moved
    r1g[...] = grad
    self_low = low(grad)
    total = mm_nt(self_low[:, cols(0)], w[3, 0])
    for c in range(1, COLS):
        total = total + mm_nt(self_low[:, cols(c)], w[3, c])
    csg[...] = low(total)


def memory_grads_kernel(ring, dk, dv, mem, w, mg, *rest):
    left = mem[...].T
    pieces = [(matrix * COLS + c, (dk, dv)[matrix], c) for matrix in range(2) for c in range(COLS)]
    put_pieces(ring, rest, [(0, piece, left, right[:, cols(c)]) for piece, right, c in pieces])
    total = mm_nt(dk[:, cols(0)], w[5, 0]) + mm_nt(dv[:, cols(0)], w[6, 0])
    for c in range(1, COLS):
        total = total + mm_nt(dk[:, cols(c)], w[5, c]) + mm_nt(dv[:, cols(c)], w[6, c])
    mg[...] = low(total)


def middle_grads_kernel(ring, dq, n2, r1g, ctxs, r2g, ctxc, *rest):
    pieces = []
    for index, (left, right) in enumerate(((ctxs, low(r1g[...])), (n2, dq[...]), (ctxc, low(r2g[...])))):
        left = left[...].T
        pieces += [(1, index * COLS + c, left, right[:, cols(c)]) for c in range(COLS)]
    put_pieces(ring, rest, pieces)


def put_pieces(ring, rest, pieces):
    if not ring:
        for index, (_, _, left, right) in enumerate(pieces):
            rest[0][index] = mm(left, right)
        return
    refs, sender = rest[:-1], Sender(rest[-1])
    for part, piece, left, right in pieces:
        group = refs[: len(refs) // 2], refs[len(refs) // 2 :]
        out = part if len(refs) == 4 else 0
        sender.matrix(group[0][out], group[1][out], part, piece, mm(left, right))


def first_grads_kernel(ring, dq, dk, dv, n1, *rest):
    left = n1[...].T
    pieces = [(right, c) for right in (dq, dk, dv) for c in range(COLS)]
    put_pieces(
        ring,
        rest,
        [(int(i >= 5), i - 5 if i >= 5 else i, left, right[:, cols(c)]) for i, (right, c) in enumerate(pieces)],
    )


def first_back_kernel(dq, dk, dv, tok, r1g, gains, w, ig, gg):
    back = None
    for matrix, right in enumerate((dq, dk, dv)):
        for c in range(COLS):
            term = mm_nt(right[:, cols(c)], w[matrix, c])
            back = term if back is None else back + term
    moved, gain_grad = norm_back(tok[...].astype(F32), gains[0:1, :], back)
    gg[...] = gain_grad
    ig[...] = low(r1g[...] + moved)


ROW_GAINS, ROW_CONTRACT, ROW_EXPAND, ROW_BUCKETS, SUM_ROWS = 8, 11, 12, 18, 24
RUNS = ((0, D), (D, D), (2 * D, FF - 2 * D))


def squares_of(values):
    return values * values + TINY


def row_line(values):
    squares = squares_of(values)
    width = squares.shape[1]
    part = squares[:, :128]
    for start in range(128, width, 128):
        part = part + squares[:, start : start + 128]
    return jnp.sum(part.T, axis=0, keepdims=True) * (1.0 / width)


def share_kernel(counts, *refs):
    shares, start = [], 0
    for count in counts:
        parts = [ref[0].astype(F32) for ref in refs[start : start + count]]
        start += count
        shares.append((parts[0] + parts[1]) + (parts[2] + parts[3]) if count == 4 else parts[0] + parts[1] + parts[2])
    one, two, cross, own = shares
    gate = [one[b] if b < 4 else two[b - 4] for b in range(BLOCKS)]
    lift = [one[4 + b] if b < 4 else two[4 + b] for b in range(BLOCKS)]
    gain_one, gain_two, gain_three, diag, onehot, att, exp, con, sums = refs[start:]
    sums[...] = jnp.zeros_like(sums)

    def keep(out, matrix, row, column, piece):
        rows = piece.reshape(24, WIDE)
        out[matrix, :, cols(column)] = rows
        place = column * WIDE
        sums[row + place // D : row + place // D + 1, place % D : place % D + WIDE] = jnp.sum(
            squares_of(rows), axis=0, keepdims=True
        )

    for c in range(COLS):
        for matrix in range(3):
            keep(att, matrix, matrix, c, own[matrix * COLS + c])
        for index, matrix in enumerate((5, 6, 3, 4, 7)):
            keep(att, matrix, matrix, c, cross[index * COLS + c])
        total = jnp.zeros((1, WIDE), F32)
        for octet in range(8):
            rows = two[4 + octet if octet < 4 else 8 + octet, c]
            con[octet * 8 : octet * 8 + 8, cols(c)] = rows
            total = total + jnp.sum(squares_of(rows), axis=0, keepdims=True)
        sums[ROW_CONTRACT : ROW_CONTRACT + 1, cols(c)] = total
    for b in range(BLOCKS):
        keep(exp, 0, ROW_EXPAND, b, gate[b])
        keep(exp, 1, ROW_EXPAND + 3, b, lift[b])
    for row, gain in enumerate((gain_one, gain_two, gain_three)):
        sums[ROW_GAINS + row : ROW_GAINS + row + 1, :] = gain[...]
    for h in range(2):
        sums[ROW_BUCKETS:SUM_ROWS, h * BUCKETS : (h + 1) * BUCKETS] = jnp.dot(
            diag[:, h, :], onehot[...], precision=lax.Precision.HIGHEST, preferred_element_type=F32
        )


def rows_kernel(att, exp, con, att_rows, exp_rows, con_rows, pair_rows):
    for row, matrix in enumerate((0, 1, 2, 4, 5, 6)):
        att_rows[row : row + 1, :] = row_line(att[matrix])
    for row, matrix in enumerate((3, 7)):
        pair_rows[row : row + 1, :] = row_line(att[matrix])
    for matrix in range(2):
        exp_rows[matrix : matrix + 1, :] = row_line(exp[matrix])
    con_rows[...] = row_line(con[...])


def new_rows(weight, grad, column_stat):
    squares = squares_of(grad)
    row_stat = jnp.mean(squares, axis=-1, keepdims=True)
    scale = jnp.mean(column_stat, axis=-1, keepdims=True)
    second = (row_stat / scale) * column_stat
    return weight.astype(F32) - STEP_RATE * grad * lax.rsqrt(second)


def update_kernel(
    sums, pair_rows, att, exp, con, att_w, exp_w, con_w, att_new, exp_new, con_new, att_cols, exp_cols, con_cols, gains, pairs, buckets
):
    me = my_index()
    square = sums[0:8, :] * (1.0 / D)
    for matrix in range(8):
        att_new[matrix] = new_rows(att_w[matrix], att[matrix], square[matrix : matrix + 1, :])
    for row, matrix in enumerate((0, 1, 2, 4, 5, 6)):
        att_cols[row : row + 1, :] = square[matrix : matrix + 1, :]
    for matrix in range(2):
        first = ROW_EXPAND + 3 * matrix
        line = jnp.concatenate([sums[first + i : first + i + 1, :size] for i, (_, size) in enumerate(RUNS)], axis=1)
        line = line * (1.0 / D)
        exp_cols[matrix : matrix + 1, :] = line
        exp_new[matrix] = new_rows(exp_w[matrix], exp[matrix], line)
    line = sums[ROW_CONTRACT : ROW_CONTRACT + 1, :] * (1.0 / FF)
    con_cols[...] = line
    con_new[...] = new_rows(con_w[...], con[...], line)
    shift = lax.rem(D - me * 24, D)
    gains[...] = pltpu.roll(sums[8:16, :], shift, 1)[0:3, :24]
    turned = pltpu.roll(square, shift, 1)
    pairs[0] = pair_rows[...]
    pairs[1, 0:1, :] = turned[3:4, :24]
    pairs[1, 1:2, :] = turned[7:8, :24]
    lines = sums[16:24, :128].T
    row = lax.broadcasted_iota(jnp.int32, (8, HEADS), 0)
    column = lax.broadcasted_iota(jnp.int32, (8, HEADS), 1)
    total = jnp.zeros((BUCKETS, HEADS), F32)
    for h in range(2):
        pick = jnp.where(column == 2 * (row - (ROW_BUCKETS - 16)) + h, 1.0, 0.0)
        total = total + jnp.dot(
            lines[h * BUCKETS : (h + 1) * BUCKETS, :],
            pick,
            precision=lax.Precision.HIGHEST,
            preferred_element_type=F32,
        )
    buckets[...] = total


def hop(values, mask):
    return lax.ppermute(values, AXES, [(k, k ^ mask) for k in range(32)])


def after(values, *earlier):
    return lax.optimization_barrier((values,) + earlier)[0]


NEXT_Z = (1, 3, 0, 2)


def ring_hop(values):
    return lax.ppermute(values, AXES, [(k, NEXT_Z[k >> 3] * 8 + (k & 7)) for k in range(32)])


def ring_owner(me, steps, mask):
    z = lax.shift_right_logical(me, 3)
    inner = lax.bitwise_and(lax.bitwise_xor(z, lax.shift_right_logical(z, 1)), 1)
    distance = (0, 2 - inner, 3, 1 + inner)[steps]
    return lax.bitwise_xor(me, distance * 8 + mask)


def place_copies(plan, targets, ins, outs, sem):
    me = my_index()
    copies = []
    for ref, (slot, low_piece, high_piece) in zip(ins, plan):
        owner = ring_owner(me, *slot)
        for out, first, last, column in targets:
            begin, end = max(low_piece, first), min(high_piece, last)
            if begin >= end:
                continue
            pieces, into = pl.ds(begin - low_piece, end - begin), pl.ds(begin - first, end - begin)
            if column is None:
                pair = (ref.at[0, pieces], outs[out].at[into, owner])
            else:
                pair = (ref.at[0, pieces, column], outs[out].at[column, owner, into])
            copies.append(pltpu.make_async_copy(*pair, sem.at[len(copies)]))
    return copies


def place_kernel(plan, targets, count, *refs):
    copies = place_copies(plan, targets, refs[:count], refs[count:-1], refs[-1])
    for copy in copies:
        copy.start()
    for copy in copies:
        copy.wait()


def place(arrays, outs, targets):
    return call(
        functools.partial(place_kernel, [a[1:] for a in arrays], targets, len(arrays)),
        [(o, BF16) for o in outs],
        [pl.BlockSpec(memory_space=pl.ANY)] * len(arrays),
        [pltpu.with_memory_space_constraint(a[0], pltpu.HBM) for a in arrays],
        4.5,
        scratch=[pltpu.SemaphoreType.DMA((40 * len(targets),))],
        limit=24,
        spaces=[VMEM] * len(outs),
    )


def make_pieces(attention, expand, contract, gains):
    attention_pieces = attention.reshape(8, 24, COLS, WIDE).transpose(0, 2, 1, 3).reshape(24, 3, 8, WIDE)
    line = lax.dynamic_update_slice_in_dim(jnp.zeros((8, D), BF16), jnp.pad(gains, ((0, 5), (0, 0))), my_index() * 24, 1)
    gain_piece = line.reshape(1, 8, COLS, WIDE).transpose(0, 2, 1, 3)
    first = jnp.concatenate([attention_pieces, gain_piece])
    expand_pieces = expand.reshape(2, 24, BLOCKS, WIDE).transpose(0, 2, 1, 3).reshape(2, BLOCKS, 3, 8, WIDE)
    contract_pieces = contract.reshape(8, 8, COLS, WIDE).transpose(0, 2, 1, 3)
    second = jnp.concatenate([expand_pieces.reshape(2 * BLOCKS, 3, 8, WIDE), contract_pieces])
    return jnp.concatenate([first, second])


HALF = 24


def hop_xy(values):
    return hop(values, 1), hop(values, 4)


def corner_hops(by_x, by_y, *earlier):
    half_x, half_y = by_x[:, :HALF], by_y[:, HALF:]
    if earlier:
        half_x, half_y = lax.optimization_barrier((half_x, half_y) + earlier)[:2]
    return hop(half_x, 4), hop(half_y, 1)


def with_core(values, *earlier):
    return values, hop(after(values, *earlier) if earlier else values, 2)


def parts_of(steps, chunk, by_x, by_y, corner_x, corner_y):
    pieces = chunk[0].shape[1]
    plan = []
    for arrays, mask, first, last in (
        (chunk, 0, 0, pieces),
        (by_x, 1, 0, pieces),
        (by_y, 4, 0, pieces),
        (corner_x, 5, 0, HALF),
        (corner_y, 5, HALF, pieces),
    ):
        plan += [(arrays[core], (steps, mask + 2 * core), first, last) for core in range(2)]
    return plan


WIDE_SHAPES = [((16, 32, 3, 8, WIDE), BF16), ((COLS, 32, 8, 8, WIDE), BF16)]
WIDE_TARGETS = [(0, 25, 41, None)] + [(1, 41, 49, c) for c in range(COLS)]


def overlapping(arrays, first):
    return [a for a in arrays if a[3] > first]


def place_square(arrays):
    square, gains = place(
        [a for a in arrays if a[2] < 25],
        [(24, 32, 3, 8, WIDE), (1, 32, 3, 8, WIDE)],
        [(0, 0, 24, None), (1, 24, 25, None)],
    )
    return square.reshape(8, COLS, D, WIDE), gains


def gather_plain(attention, expand, contract, gains):
    attention, expand, contract, gains = (
        lax.all_gather(attention, AXES, axis=1, tiled=True),
        lax.all_gather(expand, AXES, axis=1, tiled=True),
        lax.all_gather(contract, AXES, axis=0, tiled=True),
        lax.all_gather(gains, AXES, axis=1, tiled=True),
    )
    return (
        attention.reshape(8, D, COLS, WIDE).transpose(0, 2, 1, 3),
        expand.reshape(2, D, BLOCKS, WIDE).transpose(0, 2, 1, 3),
        contract.reshape(FF, COLS, WIDE).transpose(1, 0, 2),
        gains,
    )


def total(*terms):
    result = terms[0].astype(F32)
    for term in terms[1:]:
        result = result + term.astype(F32)
    return result


class Scatter:
    def __init__(self, grads):
        self.own_a, self.own_b, self.sib_a, self.sib_b = grads

    def core(self, *earlier):
        if earlier:
            self.sib_a, self.sib_b = lax.optimization_barrier((self.sib_a, self.sib_b) + earlier)[:2]
        self.from_a, self.from_b = hop(self.sib_a, 2), hop(self.sib_b, 2)

    def pin(self, earlier):
        if earlier:
            self.own_a, self.own_b = lax.optimization_barrier((self.own_a, self.own_b) + earlier)[:2]

    def first(self, *earlier):
        self.pin(earlier)
        send_a = low(total(self.own_a[8:], self.from_a[8:]))
        send_b = low(total(self.own_b[8:], self.from_b[8:]))
        self.a1, self.b1 = hop(send_a, 4), hop(send_b, 1)
        return send_a, send_b

    def halves(self, part, slots):
        if part == 0:
            return total(self.own_a[slots], self.from_a[slots], self.a1[slots])
        return total(self.own_b[slots], self.from_b[slots], self.b1[slots])


class Finish:
    def __init__(self, groups):
        self.groups = groups

    def second(self, *earlier):
        for group in self.groups:
            group.pin(earlier)
        sends = [
            low(jnp.concatenate([group.halves(part, slice(4, 8)) for group in self.groups], axis=1))
            for part in range(2)
        ]
        self.a2, self.b2 = hop(sends[0], 1), hop(sends[1], 4)
        return tuple(sends)

    def sums(self, slots):
        arrays = []
        for part, last in enumerate((self.a2, self.b2)):
            mine = jnp.concatenate([group.halves(part, slots) for group in self.groups], axis=1)
            arrays.append(mine + last[slots].astype(F32))
        return jnp.concatenate(arrays, axis=1)

    def third(self, *earlier):
        for group in self.groups:
            group.pin(earlier)
        self.mine = self.sums(slice(0, 4))
        send = low(self.mine[1:3])
        self.near = hop(send, 8)
        return (send,)

    def fourth(self, *earlier):
        mine = after(self.mine, *earlier)
        send = low(mine[3:4] + self.near[1:2].astype(F32))
        self.parts = [self.mine, self.near, hop(send, 24)]
        return (send,)

    def third_direct(self, *earlier):
        for group in self.groups:
            group.pin(earlier)
        self.mine = self.sums(slice(0, 4))
        send = low(self.mine)
        self.parts = [self.mine] + [hop(send[d : d + 1], 8 * d) for d in (1, 3, 2)]
        return (send,)


def scatter_plain(pieces, shape, axis):
    count = pieces.shape[0]
    if axis == 0:
        whole = pieces.transpose(1, 0, 2).reshape(shape)
    else:
        per = shape[2] // WIDE
        whole = pieces.reshape(shape[0], per, shape[1], WIDE).transpose(0, 2, 1, 3).reshape(shape)
    return lax.psum_scatter(whole, AXES, scatter_dimension=axis, tiled=True)


def sum_ring(values):
    values = values + hop(values, 2)
    values = (values + hop(values, 1)) + (hop(values, 4) + hop(values, 5))
    return (values + hop(values, 8)) + (hop(values, 16) + hop(values, 24))


def factored_stats(grad_shard, total_rows):
    squares = grad_shard * grad_shard + TINY
    return (jnp.mean(squares, axis=-1), jnp.sum(squares, axis=-2) / total_rows)


def factored_update(weight_shard, grad_shard, row_stat, column_stat):
    scale = jnp.mean(column_stat, axis=-1, keepdims=True)[..., None]
    second = row_stat[..., :, None] * column_stat[..., None, :] / scale
    return weight_shard.astype(F32) - STEP_RATE * grad_shard * lax.rsqrt(second)


def without_outputs(stats):
    return jnp.concatenate([stats[0:3], stats[4:7]], axis=0)


def output_pair(stats):
    return jnp.stack([stats[3], stats[7]])


def on_device(
    ring,
    tokens,
    memory,
    target_segments,
    memory_segments,
    attention_weights,
    expand_weights,
    contract_weights,
    norm_gains,
    bucket_table,
    cotangent,
):
    rows = tokens.shape[0]
    spread_buckets = jnp.asarray(diagonal_onehot())
    lines = jnp.dot(
        bucket_table.T.astype(F32), jnp.asarray(tile_onehot()).T, precision=lax.Precision.HIGHEST
    ) + jnp.where(jnp.arange(3 * QROWS) // QROWS == 1, NEG_FILL, 0.0)
    far = jnp.pad(bucket_table[BUCKETS - 1].reshape(PAIRS, 1, 2), ((0, 0), (0, 0), (FAR_LANE, 126 - FAR_LANE)))
    act, act32 = ((rows, D), BF16), ((rows, D), F32)
    none = [None]
    query_mask, self_mask, cross_mask, near_bias = call(
        prepare_kernel,
        [((rows // QROWS, 2 * QROWS, 128), BF16), ((rows, 128), BF16), ((rows, 128), BF16)]
        + [((PAIRS, 2 * QROWS, 2 * QROWS), F32)],
        none * 3,
        (target_segments.reshape(1, rows), memory_segments.reshape(1, rows), lines),
        0.8,
    )
    head_acc = VMEM((rows, 128), F32)

    if ring:
        first = make_pieces(attention_weights, expand_weights, contract_weights, norm_gains)[None]
        r1 = ring_hop(first)
        x0, y0 = hop_xy(first)
        x1, y1 = hop_xy(r1)
        r2 = ring_hop(after(r1, near_bias, x0, y0))
        a0, b0 = corner_hops(x0, y0)
        r3 = ring_hop(r2)
        x2, y2 = hop_xy(after(r2, x1, y1))
        a1, b1 = corner_hops(x1, y1, a0, b0)
        x3, y3 = hop_xy(after(r3, x2, y2))
        a2, b2 = corner_hops(x2, y2, x3)
        a3, b3 = corner_hops(x3, y3)
        parts = []
        for steps, chunk, waits in (
            (0, (first, x0, y0, a0, b0), (x1, y1)),
            (1, (r1, x1, y1, a1, b1), (x2, y2)),
            (2, (r2, x2, y2, a2, b2), (x3, y3)),
            (3, (r3, x3, y3, a3, b3), ()),
        ):
            parts += parts_of(steps, *(with_core(values, *waits) for values in chunk))
        square, gains_in = place_square(parts)
        parts = overlapping(parts, 25)
    else:
        square, wide, narrow, gains_in = gather_plain(
            attention_weights, expand_weights, contract_weights, norm_gains
        )
    resident = ()
    if ring:
        square = in_vmem(square)

    n1, q, k, v, kc, vc, gains = call(
        functools.partial(pre_kernel, ring),
        [act] * 6 + [((8, D), F32)],
        none * 5,
        (tokens, memory, gains_in, square, square),
        3.4,
    )
    lse_shape = ((PAIRS, rows // QROWS, 2 * QROWS), F32)
    args = (q, k, v, near_bias, query_mask, self_mask, far)
    specs = [pair_spec(3)] * 3 + [near_spec(3), None, None, far_spec(3)]
    if ring:
        arrays = [pltpu.with_memory_space_constraint(a[0], pltpu.HBM) for a in parts]
        copies = functools.partial(place_copies, [a[1:] for a in parts], WIDE_TARGETS)
        ctxs, lse_self, wide, narrow = call(
            functools.partial(self_forward_kernel, copies, len(arrays)),
            [act, lse_shape] + WIDE_SHAPES,
            specs + [pl.BlockSpec(memory_space=pl.ANY)] * len(arrays),
            (*args, *arrays),
            5.0,
            grid=(PAIRS // 3,),
            scratch=[pltpu.SemaphoreType.DMA((len(arrays) * len(WIDE_TARGETS),))],
            out_specs=[pair_spec(3), lse_spec(3), None, None],
            spaces=[jax.ShapeDtypeStruct] * 2 + [VMEM] * 2,
        )
        wide = in_vmem(wide.reshape(2, BLOCKS, D, WIDE))
        narrow = in_vmem(narrow.reshape(COLS, FF, WIDE))
        resident = wide, narrow
    else:
        ctxs, lse_self = call(
            functools.partial(self_forward_kernel, None, 0),
            [act, lse_shape],
            specs,
            args,
            5.0,
            grid=(PAIRS // 3,),
            out_specs=[pair_spec(3), lse_spec(3)],
        )
    res1, n2, qc = call(
        mid_kernel, [act32, act, act], none * 4, (ctxs, tokens, gains, square), 1.9, resident=resident
    )
    ctxc, lse_cross = call(
        cross_forward_kernel,
        [act, lse_shape],
        [pair_spec(PAIRS)] * 3 + [None, None],
        (qc, kc, vc, query_mask, cross_mask),
        5.8,
        grid=(1,),
        out_specs=[pair_spec(PAIRS), lse_spec(PAIRS)],
        resident=resident,
    )
    res2, n3 = call(late_kernel, [act32, act], none * 4, (ctxc, res1, gains, square), 1.0, resident=resident)
    half = BLOCKS // 2
    hidden_shape = ((rows, FF // 2), BF16)
    if ring:
        grad_outs = grad_shapes(ring, False, half, half), grad_shapes(ring, False, half + 4, half + 4)
        more = [VMEM((2, FF, WIDE), F32)], 20
    else:
        grad_outs = [((half, D, WIDE), F32)] * 2
        grad_outs = [
            (outs, [jax.ShapeDtypeStruct] * len(outs), none * len(outs))
            for outs in (grad_outs, grad_outs + [((COLS, FF, WIDE), F32)])
        ]
        more = [VMEM((2, FF, WIDE), F32)], 40
    plain = [jax.ShapeDtypeStruct] * 3
    middle, dn3, hidden, *first_grads = call(
        functools.partial(ffn_kernel, ring, False),
        [act32, act32, hidden_shape] + grad_outs[0][0],
        none * 7,
        (n3, res2, res2, n3, cotangent, wide, narrow),
        8.0,
        scratch=send_scratch(ring, False),
        limit=more[1],
        spaces=plain + grad_outs[0][1],
        out_specs=none * 3 + grad_outs[0][2],
    )
    if ring:
        ffn_one = Scatter(first_grads)
        ffn_one.core()
        middle = after(middle, *ffn_one.first())
    output, dn3, _, *last_grads = call(
        functools.partial(ffn_kernel, ring, True),
        [act, act32, hidden_shape] + grad_outs[1][0],
        none * 7,
        (n3, middle, dn3, hidden, cotangent, wide, narrow),
        13.0,
        scratch=send_scratch(ring, False) + more[0],
        limit=more[1],
        spaces=plain + grad_outs[1][1],
        out_specs=none * 3 + grad_outs[1][2],
    )
    if ring:
        ffn_two = Scatter(last_grads)
        first_half, ffn = Finish([ffn_one]), Finish([ffn_two])
        sent = first_half.second(dn3)
        ffn_two.core(ffn_one.a1, ffn_one.b1)
        dn3 = after(dn3, *sent)
    r2g, ccg, gain_three = call(
        third_back_kernel,
        [act32, act, ((1, D), F32)],
        none * 5,
        (dn3, res2, cotangent, gains, square),
        1.3,
    )
    if ring:
        ccg = after(ccg, *ffn_two.first(r2g))
    dqc, dkc, dvc = call(
        cross_back_kernel,
        [act] * 3,
        [pair_spec(PAIRS)] * 5 + [lse_spec(PAIRS), None, None],
        (qc, kc, vc, ccg, ctxc, lse_cross, query_mask, cross_mask),
        8.8,
        grid=(1,),
        scratch=[head_acc, head_acc],
        out_specs=[pair_spec(PAIRS)] * 3,
    )
    if ring:
        dkc = after(dkc, *first_half.third(dqc))
    shapes = grad_shapes(ring, False, 6)
    memory_grad, *cross_a = call(
        functools.partial(memory_grads_kernel, ring),
        [act] + shapes[0],
        none * 4,
        (dkc, dvc, memory, square),
        3.9,
        scratch=send_scratch(ring, False),
        spaces=plain[:1] + shapes[1],
        out_specs=none + shapes[2],
    )
    dqc = after(dqc, memory_grad)
    r1g, csg, gain_two = call(
        second_back_kernel,
        [act32, act, ((1, D), F32)],
        none * 5,
        (dqc, res1, r2g, gains, square),
        3.0,
    )
    shapes = grad_shapes(ring, False, 9)
    cross_b = call(
        functools.partial(middle_grads_kernel, ring),
        shapes[0],
        none * 6,
        (dqc, n2, r1g, ctxs, r2g, ctxc),
        2.5,
        scratch=send_scratch(ring, False),
        spaces=shapes[1],
        out_specs=shapes[2],
    )
    if ring:
        cross = Scatter([cross_a[0], cross_b[0], cross_a[1], cross_b[1]])
        cross.core(ffn_two.a1, ffn_two.b1)
        rest = Finish([cross])
        csg = after(csg, *ffn.second(cross_b[0]), *first_half.fourth(cross_b[0]))
    dqs, dks, dvs, near_sum, far_sum = call(
        self_back_kernel,
        [act] * 3 + [((PAIRS, 2 * QROWS, 2 * QROWS), F32), ((PAIRS, 8, 2 * QROWS), F32)],
        [pair_spec(PAIRS)] * 5 + [lse_spec(PAIRS), near_spec(PAIRS), None, None, far_spec(PAIRS)],
        (q, k, v, csg, ctxs, lse_self, near_bias, query_mask, self_mask, far),
        8.1,
        grid=(1,),
        scratch=[head_acc, head_acc],
        out_specs=[pair_spec(PAIRS)] * 3 + [near_spec(PAIRS), step_spec(PAIRS, 8, 2 * QROWS)],
    )
    if ring:
        dqs = after(dqs, *cross.first(dqs))
    shapes = grad_shapes(ring, False, 5, 4)
    self_grads = call(
        functools.partial(first_grads_kernel, ring),
        shapes[0],
        none * 4,
        (dqs, dks, dvs, n1),
        2.5,
        scratch=send_scratch(ring, False),
        spaces=shapes[1],
        out_specs=shapes[2],
    )
    if ring:
        own = Scatter(self_grads)
        dks = after(dks, self_grads[0])
    input_grad, gain_one = call(
        first_back_kernel,
        [act, ((1, D), F32)],
        none * 7,
        (dqs, dks, dvs, tokens, r1g, gains, square),
        3.4,
    )
    if ring:
        last = Finish([own])
        own.core(ffn.a2, ffn.b2)
        sent = ffn.third(input_grad)
        sent = rest.second(*sent)
        sent = ffn.fourth(*sent)
        sent = own.first(*sent)
        sent = rest.third_direct(*sent)
        sent = last.second(*sent)
        last.third_direct(*sent)
    diag = call(
        diagonals_kernel,
        [((PAIRS, 2, 2 * QROWS), F32)],
        none * 2,
        (after(near_sum, input_grad), far_sum),
        3.0,
    )[0]
    gain_parts = (gain_one, gain_two, gain_three)
    if ring:
        parts = []
        for group in (first_half, ffn, rest, last):
            parts += group.parts
        attention_grad, expand_grad, contract_grad, sums = call(
            functools.partial(share_kernel, [len(group.parts) for group in (first_half, ffn, rest, last)]),
            [((8, 24, D), F32), ((2, 24, FF), F32), ((64, D), F32), ((SUM_ROWS, D), F32)],
            none * (len(parts) + 5),
            (*parts, *gain_parts, diag, spread_buckets),
            1.5,
        )
        sums = sum_ring(sums)
        attention_rows, expand_rows, contract_rows, pair_rows = call(
            rows_kernel,
            [((6, 24), F32), ((2, 24), F32), ((1, 64), F32), ((2, 24), F32)],
            none * 3,
            (attention_grad, expand_grad, contract_grad),
            0.8,
        )
        (
            attention_new,
            expand_new,
            contract_new,
            attention_columns,
            expand_columns,
            contract_columns,
            gains_grad,
            projection_statistics,
            bucket_grad,
        ) = call(
            update_kernel,
            [
                ((8, 24, D), F32),
                ((2, 24, FF), F32),
                ((64, D), F32),
                ((6, D), F32),
                ((2, FF), F32),
                ((1, D), F32),
                ((3, 24), F32),
                ((2, 2, 24), F32),
                ((BUCKETS, HEADS), F32),
            ],
            none * 8,
            (sums, pair_rows, attention_grad, expand_grad, contract_grad, attention_weights, expand_weights, contract_weights),
            1.4,
        )
        contract_rows, contract_columns = contract_rows.reshape(64), contract_columns.reshape(D)
    else:
        bucket_part = jnp.dot(
            spread_buckets.T,
            diag.reshape(HEADS, 2 * QROWS).T,
            precision=lax.Precision.HIGHEST,
            preferred_element_type=F32,
        )
        pieces = jnp.concatenate([self_grads[0], cross_b[0][:6], cross_a[0], cross_b[0][6:]])
        attention_grad = scatter_plain(pieces, (8, D, D), 1)
        expand_pieces = jnp.stack([jnp.concatenate([first_grads[i], last_grads[i]]) for i in range(2)])
        expand_grad = scatter_plain(expand_pieces, (2, D, FF), 1)
        contract_grad = scatter_plain(last_grads[2], (FF, D), 0)
        attention_rows, attention_part = factored_stats(attention_grad, D)
        expand_rows, expand_part = factored_stats(expand_grad, D)
        contract_rows, contract_part = factored_stats(contract_grad, FF)
        attention_columns, expand_columns, contract_columns, bucket_grad, gains_sum = lax.psum(
            (attention_part, expand_part, contract_part, bucket_part, jnp.concatenate(gain_parts)), AXES
        )
        attention_new = factored_update(attention_weights, attention_grad, attention_rows, attention_columns)
        expand_new = factored_update(expand_weights, expand_grad, expand_rows, expand_columns)
        contract_new = factored_update(contract_weights, contract_grad, contract_rows, contract_columns)
        share_width = attention_rows.shape[1]
        share_start = lax.axis_index(AXES) * share_width
        column_share = lax.dynamic_slice_in_dim(attention_columns, share_start, share_width, 1)
        gains_grad = lax.dynamic_slice_in_dim(gains_sum, share_start, share_width, 1)
        projection_statistics = jnp.stack([output_pair(attention_rows), output_pair(column_share)])
        attention_rows, attention_columns = without_outputs(attention_rows), without_outputs(attention_columns)
    return (
        output,
        input_grad,
        memory_grad,
        attention_grad,
        expand_grad,
        contract_grad,
        gains_grad,
        bucket_grad,
        attention_rows,
        attention_columns,
        expand_rows,
        expand_columns,
        contract_rows,
        contract_columns,
        attention_new,
        expand_new,
        contract_new,
        projection_statistics,
    )


def solution(mesh):
    ring = dict(mesh.shape) == {"wide": 16, "narrow": 2}
    rows, both = P(AXES, None), P(None, AXES, None)
    placed = (rows, rows, P(AXES), P(AXES), both, both, rows, P(None, AXES), P(), rows)
    return jax.shard_map(
        functools.partial(on_device, ring),
        mesh=mesh,
        in_specs=placed,
        out_specs=(
            rows,
            rows,
            rows,
            both,
            both,
            rows,
            P(None, AXES),
            P(),
            P(None, AXES),
            P(),
            P(None, AXES),
            P(),
            P(AXES),
            P(),
            both,
            both,
            rows,
            P(None, None, AXES),
        ),
        check_vma=False,
    )
```
